32 devices in a mesh: dp: 8 (over z, y), section: 4 (over x, core).
Axes of the slice: x: 2, y: 2, z: 4, core: 2. Of those that a mesh axis runs over, the one named last changes fastest.
Arguments:
- images: bfloat16 [64, 16, 16, 320], P('dp'), may hold values from -240 to 240
- image_counts: int32 [8], P('dp'), may hold values from 6 to 8, as said below
- conv_weight: bfloat16 [4, 5760, 640], P('section')
- bn_gain: float32 [4, 640], P('section'), may hold values from 0.25 to 1.75
- bn_bias: float32 [4, 640], P('section'), may hold values from -3 to 3
- out_grad: bfloat16 [64, 8, 8, 640], P('dp'), may hold values from -6 to 6
Outputs:
- section_outputs: bfloat16 [4, 64, 8, 8, 640], P('section', 'dp')
- input_grad: bfloat16 [64, 16, 16, 320], P('dp', 'section')
- weight_grad: float32 [4, 5760, 640], P('section')
- gain_grad: float32 [4, 640], P('section')
- bias_grad: float32 [4, 640], P('section')
The draws below stay inside these ranges and needn't reach their ends.
Inputs may be any that keep to these rules, and one draw needn't show every extreme that they name: `image_counts`: each index of dp has at least three quarters of 8 valid images; some index has exactly 8.
All inputs are finite; a program needn't handle non-finite values.
Results may differ from the reference program's by a relative error of at most 0.011.
Values may be sent and summed in bfloat16 or wider, within the bound.
No kernel may reach another device: no remote copies, remote signals or barrier semaphores. Data moves between devices by JAX's collectives and lax.ppermute only.
A program may use at most 128 MiB of HBM per device.

```python
import math
import jax
import jax.numpy as jnp
from jax import lax

C_IN = 320
C_OUT = 640
HEIGHT = 16
MICRO = 8
IMG_DEV = 8
MB = 1
IMAGES = 64
N_DP = 8
N_SECTION = 4


def draw_images(key, part):
    key = jax.random.fold_in(key, 3)
    key_base, key_image, key_chan = jax.random.split(key, 3)
    shape = (IMAGES, HEIGHT, HEIGHT, C_IN)
    base = jax.random.truncated_normal(key_base, -4.0, 4.0, shape, jnp.float32)
    image_scale = jnp.exp(jax.random.uniform(key_image, (IMAGES, 1, 1, 1), jnp.float32) * math.log(10.0))
    device_pos = (jnp.arange(IMAGES) // IMG_DEV).astype(jnp.float32) / max(N_DP - 1, 1)
    ramp = jnp.exp(device_pos * math.log(3.0))[:, None, None, None]
    chan_scale = jnp.exp(jax.random.uniform(key_chan, (C_IN,), jnp.float32, -math.log(2.0), math.log(2.0)))
    return (base * image_scale * ramp * chan_scale).astype(jnp.bfloat16)


def draw_image_counts(key, part):
    key = jax.random.fold_in(key, 5)
    key_counts, key_full = jax.random.split(key)
    low_count = IMG_DEV - IMG_DEV // 4
    counts = jax.random.randint(key_counts, (N_DP,), low_count, IMG_DEV + 1)
    full_index = jax.random.randint(key_full, (), 0, N_DP)
    return jnp.where(jnp.arange(N_DP) == full_index, IMG_DEV, counts).astype(jnp.int32)


def draw_conv_weight(key, part):
    key = jax.random.fold_in(key, 11)
    shape = (N_SECTION, 9 * C_OUT, C_OUT)
    base = jax.random.truncated_normal(key, -4.0, 4.0, shape, jnp.float32)
    row_index = jnp.arange(9 * C_OUT)[None, :, None]
    section_pos = jnp.arange(N_SECTION)[:, None, None]
    first_scale = jnp.where(row_index < 9 * C_IN, (9.0 * C_IN) ** (-0.5), jnp.where(row_index < 10 * C_IN, float(C_IN) ** (-0.5), (9.0 * C_OUT) ** (-0.5)))
    scale = jnp.where(section_pos == 0, first_scale, (9.0 * C_OUT) ** (-0.5))
    return (base * scale).astype(jnp.bfloat16)


def level_of(rng, shape, cuts, low, largest):
    def one(axis_at, blocks):
        draws = jax.random.uniform(jax.random.fold_in(jax.random.fold_in(rng, 6), axis_at), (blocks,), jnp.float32, low / len(cuts), largest / len(cuts))
        return jnp.repeat(jnp.exp(draws), shape[axis_at] // blocks).reshape((-1,) + (1,) * (len(shape) - axis_at - 1))

    factor_of = one(*cuts[0])
    for cut in cuts[1:]:
        factor_of = factor_of * one(*cut)
    return factor_of


def scatter_about(rng, dims, scale, reach, cuts=(), kind=jnp.bfloat16):
    level = level_of(rng, dims, cuts, -0.22, 0.18) if cuts else 1.0
    result = jax.random.normal(rng, dims, jnp.float32) * scale * level
    return jnp.minimum(jnp.maximum(result, -reach), reach).astype(kind)


def setup_inputs(seed: int = 0) -> dict:
    key_list = jax.random.split(jax.random.key(seed), 7)
    return {
        "images": draw_images(jax.random.fold_in(key_list[6], 71), 0),
        "image_counts": draw_image_counts(jax.random.fold_in(key_list[6], 71), 0),
        "conv_weight": draw_conv_weight(jax.random.fold_in(key_list[6], 71), 0),
        "bn_gain": jnp.clip(1.0 + 0.15 * jax.random.normal(key_list[3], (N_SECTION, C_OUT), jnp.float32), 0.25, 1.75),
        "bn_bias": scatter_about(key_list[4], (N_SECTION, C_OUT), 0.5, 3.0, ((0, 4),), jnp.float32),
        "out_grad": scatter_about(key_list[5], (IMAGES, HEIGHT // 2, HEIGHT // 2, C_OUT), 1.0, 6.0, ((0, 8),)),
    }


EPSILON = 1e-05

@jax.custom_vjp
def low(v):
    return lax.optimization_barrier(v.astype(jnp.bfloat16)).astype(jnp.float32)

@jax.custom_vjp
def low_back(v):
    return v

def low_keep(v):
    return (low(v), None)

def low_pass(kept, grad):
    return (grad,)

def back_keep(v):
    return (v, None)

def back_low(kept, grad):
    return (low(grad),)
low.defvjp(low_keep, low_pass)
low_back.defvjp(back_keep, back_low)

def batch_norm(field, gain, offset, mask_six):
    height, width, chans = (field.shape[1], field.shape[2], field.shape[3])
    reshaped = field.reshape(N_DP, MB, MICRO, height, width, chans)
    count_all = lax.optimization_barrier(jnp.sum(mask_six, axis=(0, 1), keepdims=True)) * (height * width)
    channel_mean = lax.optimization_barrier(jnp.sum(mask_six * reshaped, axis=(0, 1, 3, 4), keepdims=True)) / count_all
    centred = reshaped - channel_mean
    variance = lax.optimization_barrier(jnp.sum(mask_six * centred * centred, axis=(0, 1, 3, 4), keepdims=True)) / count_all
    pre_act = centred * lax.rsqrt(variance + EPSILON) * gain + offset
    return (jax.nn.silu(pre_act) * mask_six).reshape(field.shape)

def convolve(activation, kernel, stride):
    return lax.conv_general_dilated(activation, kernel, (stride, stride), ((1, 1), (1, 1)), dimension_numbers=('NHWC', 'HWIO', 'NHWC'), precision=lax.Precision.HIGHEST)

def reference(images, image_counts, conv_weight, bn_gain, bn_bias, out_grad):
    local_rows = jnp.arange(IMG_DEV, dtype=jnp.int32)
    valid_img = (local_rows[None, :] < image_counts[:, None]).astype(jnp.float32)
    mask_six = valid_img.reshape(N_DP, MB, MICRO)[:, :, :, None, None, None]
    images_f = images.astype(jnp.float32)
    kernels_f = conv_weight.astype(jnp.float32)
    side = HEIGHT // 2

    def forward(inputs, kernels, gains, offsets):
        act_one = low(batch_norm(inputs, gains[0, :C_IN], offsets[0, :C_IN], mask_six))
        kernel_first = kernels[0, :9 * C_IN].reshape(3, 3, C_IN, C_OUT)
        kernel_proj = kernels[0, 9 * C_IN:10 * C_IN]
        h_one = low_back(low(convolve(act_one, kernel_first, 2)))
        sub_grid = act_one[:, 0::2, 0::2, :].reshape(-1, C_IN)
        shortcut = low(jnp.dot(sub_grid, kernel_proj, precision=lax.Precision.HIGHEST).reshape(IMAGES, side, side, C_OUT))
        act_two = low(batch_norm(h_one, gains[1], offsets[1], mask_six))
        y_one = low_back(low(convolve(act_two, kernels[1].reshape(3, 3, C_OUT, C_OUT), 1) + shortcut))
        act_three = low(batch_norm(y_one, gains[2], offsets[2], mask_six))
        h_three = low_back(low(convolve(act_three, kernels[2].reshape(3, 3, C_OUT, C_OUT), 1)))
        act_four = low(batch_norm(h_three, gains[3], offsets[3], mask_six))
        y_two = convolve(act_four, kernels[3].reshape(3, 3, C_OUT, C_OUT), 1) + y_one
        return (y_two, (h_one, y_one, h_three))
    y_two, pullback, kept = jax.vjp(forward, images_f, kernels_f, bn_gain, bn_bias, has_aux=True)
    grad_in, grad_kernel, grad_gain, grad_bias = pullback(out_grad.astype(jnp.float32))
    section_outputs = jnp.stack([kept[0], kept[1], kept[2], y_two]).astype(jnp.bfloat16)
    return (section_outputs, grad_in.astype(jnp.bfloat16), grad_kernel, grad_gain, grad_bias)
```

```python
import jax
import jax.numpy as jnp
from jax import lax
from jax.experimental import pallas as pl
from jax.experimental.pallas import tpu as pltpu
from jax.sharding import PartitionSpec as P

MICRO = 8


EPSILON = 1e-05


def for_sending(value):

    def short(part):
        return part.astype(jnp.bfloat16) if part.dtype == jnp.float32 else part

    return jax.tree.map(short, value)


def shifted(value, axis, steps):
    count = lax.axis_size(axis)
    initial, last = (max(0, -steps), min(count, count - steps))
    return lax.ppermute(value, axis, [(source, source + steps) for source in range(initial, last)])


def conv_forward(activation, kernel, stride):
    return lax.conv_general_dilated(
        activation,
        kernel,
        (stride, stride),
        ((1, 1), (1, 1)),
        dimension_numbers=("NHWC", "HWIO", "NHWC"),
        preferred_element_type=jnp.float32,
    )


def conv_input_grad(gradient, kernel, stride):
    upper = 1 if stride == 1 else 2
    return lax.conv_general_dilated(
        gradient,
        kernel[::-1, ::-1],
        (1, 1),
        ((1, upper), (1, upper)),
        lhs_dilation=(stride, stride),
        dimension_numbers=("NHWC", "HWOI", "NHWC"),
        preferred_element_type=jnp.float32,
    )


def conv_kernel_grad(activation, gradient, stride):
    upper = 1 if stride == 1 else 0
    return lax.conv_general_dilated(
        activation,
        gradient,
        (1, 1),
        ((1, upper), (1, upper)),
        rhs_dilation=(stride, stride),
        dimension_numbers=("CHWN", "IHWO", "HWNC"),
        preferred_element_type=jnp.float32,
    )


def channel_sum(values, image_mask):
    return jnp.sum(image_mask[:, None, None, None] * values, axis=(0, 1, 2))


def normalize(values, channel_mean, inv_std, norm_gain, norm_bias):
    scaled = (values - channel_mean) * inv_std
    return (scaled, scaled * norm_gain + norm_bias)


def norm_terms(grad_act, values, image_mask, channel_mean, inv_std, norm_gain, norm_bias):
    scaled, pre_act = normalize(values, channel_mean, inv_std, norm_gain, norm_bias)
    sigmoid_val = jax.nn.sigmoid(pre_act)
    grad_pre = (
        grad_act
        * image_mask[:, None, None, None]
        * sigmoid_val
        * (1.0 + pre_act * (1.0 - sigmoid_val))
    )
    return (grad_pre, scaled)


def pipelined(images, image_counts, conv_weight, bn_gain, bn_bias, out_grad):
    section_count = lax.axis_size("section")
    section_index = lax.axis_index("section")
    img_dev = images.shape[0]
    per_micro = img_dev // MICRO
    height = images.shape[1]
    side = height // 2
    c_in = images.shape[3]
    c_out = conv_weight.shape[2]
    kernel_rows = conv_weight.shape[1]
    is_first = section_index == 0
    is_last = section_index == section_count - 1
    adds_residual = section_index % 2 == 1
    merges_back = (section_index % 2 == 0) & (section_index > 0)
    valid_img = (jnp.arange(img_dev, dtype=jnp.int32) < image_counts[0]).astype(jnp.float32)
    valid_img = valid_img.reshape(per_micro, MICRO)
    image_groups = images.reshape(per_micro, MICRO, height, height, c_in)
    grad_groups = out_grad.reshape(per_micro, MICRO, side, side, c_out)
    kernel_all = conv_weight[0]
    kernel_first = kernel_all[: 9 * c_in].reshape(3, 3, c_in, c_out)
    kernel_proj = kernel_all[9 * c_in : 10 * c_in]
    kernel_rest = kernel_all.reshape(3, 3, c_out, c_out)
    norm_gain = bn_gain[0]
    norm_bias = bn_bias[0]
    tick_count = MICRO + section_count - 1
    pad_width = (0, c_out - c_in)

    def forward_first(raw_input, section_input, residual, image_mask, channel_mean, inv_std):
        scaled, pre_act = normalize(
            raw_input, channel_mean[:c_in], inv_std[:c_in], norm_gain[:c_in], norm_bias[:c_in]
        )
        activation = (jax.nn.silu(pre_act) * image_mask[:, None, None, None]).astype(jnp.bfloat16)
        conv_out = conv_forward(activation, kernel_first, 2)
        sub_grid = activation[:, 0::2, 0::2, :].reshape(-1, c_in)
        projected = jnp.dot(sub_grid, kernel_proj, preferred_element_type=jnp.float32)
        projected = projected.reshape(per_micro, side, side, c_out)
        return (conv_out.astype(jnp.bfloat16), projected.astype(jnp.bfloat16))

    def forward_rest(raw_input, section_input, residual, image_mask, channel_mean, inv_std):
        scaled, pre_act = normalize(section_input, channel_mean, inv_std, norm_gain, norm_bias)
        activation = (jax.nn.silu(pre_act) * image_mask[:, None, None, None]).astype(jnp.bfloat16)
        conv_out = conv_forward(activation, kernel_rest, 1)
        summed = conv_out + jnp.where(adds_residual, 1.0, 0.0) * residual.astype(jnp.float32)
        sent_main = summed.astype(jnp.bfloat16)
        return (sent_main, jnp.where(adds_residual, sent_main, residual))

    def forward_tick(step_index, state_carry):
        recv_main, recv_side, out_buf, in_buf, moment_buf, count_buf = state_carry
        micro_index = step_index - section_index
        active = (micro_index >= 0) & (micro_index < MICRO)
        slot_index = jnp.clip(micro_index, 0, MICRO - 1)
        image_mask = lax.dynamic_index_in_dim(valid_img, slot_index, 1, keepdims=False)
        raw_input = lax.dynamic_index_in_dim(image_groups, slot_index, 1, keepdims=False).astype(
            jnp.float32
        )
        section_input = recv_main.astype(jnp.float32)
        positions = jnp.where(is_first, float(height * height), float(side * side))
        local_count = jnp.sum(image_mask) * positions
        local_total = jnp.where(
            is_first,
            jnp.pad(channel_sum(raw_input, image_mask), pad_width),
            channel_sum(section_input, image_mask),
        )
        total_sum, count_sum = lax.psum((local_total, local_count), "dp")
        channel_mean = total_sum / count_sum
        first_dev = raw_input - channel_mean[:c_in]
        rest_dev = section_input - channel_mean
        local_spread = jnp.where(
            is_first,
            jnp.pad(channel_sum(first_dev * first_dev, image_mask), pad_width),
            channel_sum(rest_dev * rest_dev, image_mask),
        )
        spread_sum = lax.psum(local_spread, "dp")
        variance = spread_sum / count_sum
        inv_std = lax.rsqrt(variance + EPSILON)
        sent_main, sent_side = lax.cond(
            is_first,
            forward_first,
            forward_rest,
            raw_input,
            section_input,
            recv_side,
            image_mask,
            channel_mean,
            inv_std,
        )
        old_out = lax.dynamic_index_in_dim(out_buf, slot_index, 0, keepdims=False)
        out_buf = lax.dynamic_update_index_in_dim(
            out_buf, jnp.where(active, sent_main, old_out), slot_index, 0
        )
        old_in = lax.dynamic_index_in_dim(in_buf, slot_index, 0, keepdims=False)
        in_buf = lax.dynamic_update_index_in_dim(
            in_buf, jnp.where(active, recv_main, old_in), slot_index, 0
        )
        moments = jnp.stack([channel_mean, inv_std])
        old_moment = lax.dynamic_index_in_dim(moment_buf, slot_index, 0, keepdims=False)
        moment_buf = lax.dynamic_update_index_in_dim(
            moment_buf, jnp.where(active, moments, old_moment), slot_index, 0
        )
        old_count = lax.dynamic_index_in_dim(count_buf, slot_index, 0, keepdims=False)
        count_buf = lax.dynamic_update_index_in_dim(
            count_buf, jnp.where(active, count_sum, old_count), slot_index, 0
        )
        recv_main, recv_side = (
            shifted(for_sending(sent_main), "section", 1).astype(sent_main.dtype),
            shifted(for_sending(sent_side), "section", 1).astype(sent_side.dtype),
        )
        return (recv_main, recv_side, out_buf, in_buf, moment_buf, count_buf)

    act_zeros = jnp.zeros((per_micro, side, side, c_out), jnp.bfloat16)
    forward_init = (
        act_zeros,
        act_zeros,
        jnp.zeros((MICRO, per_micro, side, side, c_out), jnp.bfloat16),
        jnp.zeros((MICRO, per_micro, side, side, c_out), jnp.bfloat16),
        jnp.zeros((MICRO, 2, c_out), jnp.float32),
        jnp.ones((MICRO,), jnp.float32),
    )
    forward_done = lax.fori_loop(0, tick_count, forward_tick, forward_init)
    out_buf, in_buf, moment_buf, count_buf = (
        forward_done[2],
        forward_done[3],
        forward_done[4],
        forward_done[5],
    )

    def backward_first(
        raw_input, section_input, grad_conv, grad_side, image_mask, channel_mean, inv_std
    ):
        scaled, pre_act = normalize(
            raw_input, channel_mean[:c_in], inv_std[:c_in], norm_gain[:c_in], norm_bias[:c_in]
        )
        activation = (jax.nn.silu(pre_act) * image_mask[:, None, None, None]).astype(jnp.bfloat16)
        kernel_part = conv_kernel_grad(activation, grad_conv, 2).reshape(9 * c_in, c_out)
        sub_grid = activation[:, 0::2, 0::2, :].reshape(-1, c_in)
        side_flat = grad_side.reshape(-1, c_out)
        proj_part = lax.dot_general(
            sub_grid, side_flat, (((0,), (0,)), ((), ())), preferred_element_type=jnp.float32
        )
        weight_part = jnp.concatenate(
            [kernel_part, proj_part, jnp.zeros((kernel_rows - 10 * c_in, c_out), jnp.float32)],
            axis=0,
        )
        sub_grad = lax.dot_general(
            side_flat, kernel_proj, (((1,), (1,)), ((), ())), preferred_element_type=jnp.float32
        )
        sub_grad = sub_grad.reshape(per_micro, side, side, c_in)
        spread_grad = lax.pad(
            sub_grad, jnp.float32(0.0), ((0, 0, 0), (0, 1, 1), (0, 1, 1), (0, 0, 0))
        )
        grad_first = conv_input_grad(grad_conv, kernel_first, 2) + spread_grad
        return (weight_part, grad_first, jnp.zeros((per_micro, side, side, c_out), jnp.float32))

    def backward_rest(
        raw_input, section_input, grad_conv, grad_side, image_mask, channel_mean, inv_std
    ):
        scaled, pre_act = normalize(section_input, channel_mean, inv_std, norm_gain, norm_bias)
        activation = (jax.nn.silu(pre_act) * image_mask[:, None, None, None]).astype(jnp.bfloat16)
        weight_part = conv_kernel_grad(activation, grad_conv, 1).reshape(kernel_rows, c_out)
        grad_rest = conv_input_grad(grad_conv, kernel_rest, 1)
        return (weight_part, jnp.zeros((per_micro, height, height, c_in), jnp.float32), grad_rest)

    def backward_tick(step_index, state_carry):
        recv_main, recv_side, weight_acc, gain_acc, bias_acc, input_buf = state_carry
        micro_index = step_index - (section_count - 1 - section_index)
        active = (micro_index >= 0) & (micro_index < MICRO)
        slot_index = jnp.clip(micro_index, 0, MICRO - 1)
        image_mask = lax.dynamic_index_in_dim(valid_img, slot_index, 1, keepdims=False)
        raw_input = lax.dynamic_index_in_dim(image_groups, slot_index, 1, keepdims=False).astype(
            jnp.float32
        )
        section_input = lax.dynamic_index_in_dim(in_buf, slot_index, 0, keepdims=False).astype(
            jnp.float32
        )
        moments = lax.dynamic_index_in_dim(moment_buf, slot_index, 0, keepdims=False)
        channel_mean, inv_std = (moments[0], moments[1])
        count_sum = lax.dynamic_index_in_dim(count_buf, slot_index, 0, keepdims=False)
        top_grad = jnp.where(
            is_last, lax.dynamic_index_in_dim(grad_groups, slot_index, 1, keepdims=False), recv_main
        )
        joined = (top_grad.astype(jnp.float32) + recv_side.astype(jnp.float32)).astype(jnp.bfloat16)
        grad_conv = jnp.where(adds_residual, joined, top_grad)
        grad_side = jnp.where(adds_residual, joined, recv_side)
        weight_part, grad_first, grad_rest = lax.cond(
            is_first,
            backward_first,
            backward_rest,
            raw_input,
            section_input,
            grad_conv,
            grad_side,
            image_mask,
            channel_mean,
            inv_std,
        )
        pre_first, scaled_first = norm_terms(
            grad_first,
            raw_input,
            image_mask,
            channel_mean[:c_in],
            inv_std[:c_in],
            norm_gain[:c_in],
            norm_bias[:c_in],
        )
        pre_rest, scaled_rest = norm_terms(
            grad_rest, section_input, image_mask, channel_mean, inv_std, norm_gain, norm_bias
        )
        local_pre = jnp.where(
            is_first,
            jnp.pad(jnp.sum(pre_first, axis=(0, 1, 2)), pad_width),
            jnp.sum(pre_rest, axis=(0, 1, 2)),
        )
        local_cross = jnp.where(
            is_first,
            jnp.pad(jnp.sum(pre_first * scaled_first, axis=(0, 1, 2)), pad_width),
            jnp.sum(pre_rest * scaled_rest, axis=(0, 1, 2)),
        )
        sum_pre, sum_cross = lax.psum((local_pre, local_cross), "dp")
        mean_pre = sum_pre / count_sum
        mean_cross = sum_cross / count_sum
        mask_four = image_mask[:, None, None, None]
        grad_in_rest = (
            mask_four * inv_std * norm_gain * (pre_rest - mean_pre - scaled_rest * mean_cross)
        )
        grad_in_first = (
            mask_four
            * inv_std[:c_in]
            * norm_gain[:c_in]
            * (pre_first - mean_pre[:c_in] - scaled_first * mean_cross[:c_in])
        )
        sent_main = jnp.where(
            merges_back, grad_in_rest + grad_side.astype(jnp.float32), grad_in_rest
        ).astype(jnp.bfloat16)
        sent_side = jnp.where(merges_back, jnp.zeros_like(grad_side), grad_side)
        weight_acc = weight_acc + jnp.where(active, weight_part, 0.0)
        gain_acc = gain_acc + jnp.where(active, sum_cross, 0.0)
        bias_acc = bias_acc + jnp.where(active, sum_pre, 0.0)
        old_input = lax.dynamic_index_in_dim(input_buf, slot_index, 0, keepdims=False)
        input_buf = lax.dynamic_update_index_in_dim(
            input_buf, jnp.where(active, grad_in_first, old_input), slot_index, 0
        )
        recv_main, recv_side = shifted((sent_main, sent_side), "section", -1)
        return (recv_main, recv_side, weight_acc, gain_acc, bias_acc, input_buf)

    backward_init = (
        act_zeros,
        act_zeros,
        jnp.zeros((kernel_rows, c_out), jnp.float32),
        jnp.zeros((c_out,), jnp.float32),
        jnp.zeros((c_out,), jnp.float32),
        jnp.zeros((MICRO, per_micro, height, height, c_in), jnp.float32),
    )
    backward_done = lax.fori_loop(0, tick_count, backward_tick, backward_init)
    weight_acc, gain_acc, bias_acc, input_buf = (
        backward_done[2],
        backward_done[3],
        backward_done[4],
        backward_done[5],
    )
    weight_total = lax.psum(weight_acc, "dp")
    input_full = jnp.transpose(input_buf, (1, 0, 2, 3, 4)).reshape(img_dev, height, height, c_in)
    input_full = jnp.where(is_first, input_full, 0.0)
    input_grad = lax.psum_scatter(
        input_full.astype(jnp.bfloat16), "section", scatter_dimension=1, tiled=True
    )
    section_outputs = jnp.transpose(out_buf, (1, 0, 2, 3, 4)).reshape(img_dev, side, side, c_out)[
        None
    ]
    return (section_outputs, input_grad, weight_total[None], gain_acc[None], bias_acc[None])


BF = jnp.bfloat16
F32 = jnp.float32
VMEM_BYTES = 56 * 1024 * 1024
ANY = pl.BlockSpec(memory_space=pl.ANY)
INSIDE = pl.BlockSpec(memory_space=pltpu.VMEM)
SCALARS = pl.BlockSpec(memory_space=pltpu.SMEM)


def lanes(width):
    return [(low, min(low + 128, width)) for low in range(0, width, 128)]


def by_image(values, mask):
    return (values.reshape(8, 64, values.shape[1]) * mask[None]).reshape(values.shape)


def column_iota(width):
    return lax.rem(lax.broadcasted_iota(jnp.int32, (512, width), 0), 8)


def from_left(values):
    moved = pltpu.roll(values, 1, 0)
    return jnp.where(column_iota(values.shape[1]) == 0, 0.0, moved)


def from_right(values):
    moved = pltpu.roll(values, 511, 0)
    return jnp.where(column_iota(values.shape[1]) == 7, 0.0, moved)


def matmul(a, b):
    return jnp.dot(a, b, preferred_element_type=F32)


def matmul_bt(a, b):
    return lax.dot_general(a, b, (((1,), (1,)), ((), ())), preferred_element_type=F32)


def matmul_at(a, b):
    return lax.dot_general(a, b, (((0,), (0,)), ((), ())), preferred_element_type=F32)


def start_all(copies):
    for one in copies:
        one.start()


def params():
    return pltpu.CompilerParams(vmem_limit_bytes=VMEM_BYTES, has_side_effects=False)


def forward_rest_kernel(
    flags, norm_n, h_ref, res_ref, w_ref, gain, bias, mask, keep_out, keep_act, keep_in, keep_stats,
    out_ref, act_ref, in_ref, stats_ref,
    w_vm, h_vm, res_vm, act_vm, x3, sems,
):
    @pl.when(flags[0] == 0)
    def _():
        stats_ref[...] = keep_stats[...]

    @pl.when(flags[0] == 1)
    def _():
        in_h = pltpu.make_async_copy(h_ref, h_vm, sems.at[0])
        in_res = pltpu.make_async_copy(res_ref, res_vm, sems.at[1])
        in_w = [
            pltpu.make_async_copy(w_ref.at[pl.ds(1920 * p, 1920)], w_vm.at[pl.ds(1920 * p, 1920)], sems.at[2 + p])
            for p in range(3)
        ]
        start_all([in_h, *in_w, in_res])
        in_h.wait()
        keep = pltpu.make_async_copy(h_vm, in_ref, sems.at[5])
        keep.start()
        x3[0:64, :] = jnp.zeros((64, 1920), BF)
        x3[576:640, :] = jnp.zeros((64, 1920), BF)
        count = norm_n[0]
        for low, high in lanes(640):
            valid = mask[:, 0 : high - low]
            x = h_vm[:, low:high].astype(F32)
            mean = jnp.sum(by_image(x, valid), axis=0, keepdims=True) / count
            cen = x - mean
            var = jnp.sum(by_image(cen * cen, valid), axis=0, keepdims=True) / count
            inv = lax.rsqrt(var + EPSILON)
            z = cen * inv * gain[:, low:high] + bias[:, low:high]
            act = by_image(z / (1.0 + jnp.exp(-z)), valid)
            stats_ref[0:1, low:high] = mean
            stats_ref[1:2, low:high] = inv
            x3[64:576, low:high] = from_left(act).astype(BF)
            x3[64:576, 640 + low : 640 + high] = act.astype(BF)
            x3[64:576, 1280 + low : 1280 + high] = from_right(act).astype(BF)
            act_vm[:, low:high] = act.astype(BF)
        keep_a = pltpu.make_async_copy(act_vm, act_ref, sems.at[6])
        keep_a.start()
        total = None
        for p in range(3):
            in_w[p].wait()
            part = matmul(x3[64 * p : 64 * p + 512, :], w_vm[1920 * p : 1920 * p + 1920, :])
            total = part if total is None else total + part
        in_res.wait()
        keep.wait()
        h_vm[...] = jnp.where(flags[1] == 1, total + res_vm[...].astype(F32), total).astype(BF)
        done = pltpu.make_async_copy(h_vm, out_ref, sems.at[0])
        done.start()
        done.wait()
        keep_a.wait()


def forward_rest(flags, norm_n, h, res, weight, gain, bias, mask, kept):
    field = jax.ShapeDtypeStruct((512, 640), BF)
    return pl.pallas_call(
        forward_rest_kernel,
        out_shape=(field, field, field, jax.ShapeDtypeStruct((2, 640), F32)),
        in_specs=[SCALARS, SCALARS, ANY, ANY, ANY, INSIDE, INSIDE, INSIDE, ANY, ANY, ANY, INSIDE],
        out_specs=(ANY, ANY, ANY, INSIDE),
        input_output_aliases={8: 0, 9: 1, 10: 2, 11: 3},
        scratch_shapes=[
            pltpu.VMEM((5760, 640), BF),
            pltpu.VMEM((512, 640), BF),
            pltpu.VMEM((512, 640), BF),
            pltpu.VMEM((512, 640), BF),
            pltpu.VMEM((640, 1920), BF),
            pltpu.SemaphoreType.DMA((7,)),
        ],
        compiler_params=params(),
    )(flags, norm_n, h, res, weight, gain, bias, mask, *kept)


def forward_first_kernel(
    flags, norm_n, x_ref, w_ref, gain, bias, mask,
    out_ref, side_ref, act_ref, stats_ref,
    w_vm, x_vm, act_vm, out_vm, side_vm, x_even, x_odd, sems,
):
    @pl.when(flags[0] == 1)
    def _():
        in_x = pltpu.make_async_copy(x_ref, x_vm, sems.at[0])
        in_w = pltpu.make_async_copy(w_ref.at[pl.ds(0, 3200)], w_vm, sems.at[1])
        start_all([in_x, in_w])
        in_x.wait()
        x_odd[0:64, :] = jnp.zeros((64, 960), BF)
        count = norm_n[1]
        for low, high in lanes(320):
            valid = mask[:, 0 : high - low]
            xs = [x_vm[k, :, low:high].astype(F32) for k in range(4)]
            mean = jnp.sum(by_image(xs[0] + xs[1] + xs[2] + xs[3], valid), axis=0, keepdims=True) / count
            cens = [x - mean for x in xs]
            var = jnp.sum(by_image(sum(c * c for c in cens), valid), axis=0, keepdims=True) / count
            inv = lax.rsqrt(var + EPSILON)
            stats_ref[0:1, low:high] = mean
            stats_ref[1:2, low:high] = inv
            for k in range(4):
                z = cens[k] * inv * gain[:, low:high] + bias[:, low:high]
                act = by_image(z / (1.0 + jnp.exp(-z)), valid)
                act_vm[k, :, low:high] = act.astype(BF)
                rows = x_even if k < 2 else x_odd
                first = 0 if k < 2 else 64
                if k % 2 == 0:
                    rows[first : first + 512, 320 + low : 320 + high] = act.astype(BF)
                else:
                    rows[first : first + 512, low:high] = from_left(act).astype(BF)
                    rows[first : first + 512, 640 + low : 640 + high] = act.astype(BF)
        keep_a = pltpu.make_async_copy(act_vm, act_ref, sems.at[2])
        keep_a.start()
        in_w.wait()
        total = matmul(x_odd[0:512, :], w_vm[0:960, :])
        total = total + matmul(x_even[...], w_vm[960:1920, :])
        total = total + matmul(x_odd[64:576, :], w_vm[1920:2880, :])
        out_vm[...] = total.astype(BF)
        out = pltpu.make_async_copy(out_vm, out_ref, sems.at[0])
        out.start()
        side_vm[...] = matmul(act_vm[0], w_vm[2880:3200, :]).astype(BF)
        side = pltpu.make_async_copy(side_vm, side_ref, sems.at[1])
        side.start()
        out.wait()
        side.wait()
        keep_a.wait()


def forward_first(flags, norm_n, x, weight, gain, bias, mask):
    field = jax.ShapeDtypeStruct((512, 640), BF)
    return pl.pallas_call(
        forward_first_kernel,
        out_shape=(field, field, jax.ShapeDtypeStruct((4, 512, 320), BF), jax.ShapeDtypeStruct((2, 640), F32)),
        in_specs=[SCALARS, SCALARS, ANY, ANY, INSIDE, INSIDE, INSIDE],
        out_specs=(ANY, ANY, ANY, INSIDE),
        scratch_shapes=[
            pltpu.VMEM((3200, 640), BF),
            pltpu.VMEM((4, 512, 320), BF),
            pltpu.VMEM((4, 512, 320), BF),
            pltpu.VMEM((512, 640), BF),
            pltpu.VMEM((512, 640), BF),
            pltpu.VMEM((512, 960), BF),
            pltpu.VMEM((576, 960), BF),
            pltpu.SemaphoreType.DMA((3,)),
        ],
        compiler_params=params(),
    )(flags, norm_n, x, weight, gain, bias, mask)


def norm_back(grad, x, valid, mean, inv, gain, bias):
    xhat = (x - mean) * inv
    z = xhat * gain + bias
    sig = 1.0 / (1.0 + jnp.exp(-z))
    return by_image(grad, valid) * sig * (1.0 + z * (1.0 - sig)), xhat


def backward_rest_kernel(
    flags, norm_n, g_ref, add_ref, h_ref, stats, w_ref, gain, bias, mask, keep_sums,
    out_ref, sums_ref,
    w_vm, g_vm, add_vm, h_vm, g3, total, sems,
):
    @pl.when(flags[0] == 0)
    def _():
        sums_ref[...] = keep_sums[...]

    @pl.when(flags[0] == 1)
    def _():
        in_g = pltpu.make_async_copy(g_ref, g_vm, sems.at[0])
        in_w = [
            pltpu.make_async_copy(w_ref.at[pl.ds(1920 * p, 1920)], w_vm.at[pl.ds(1920 * p, 1920)], sems.at[1 + p])
            for p in range(3)
        ]
        in_h = pltpu.make_async_copy(h_ref, h_vm, sems.at[4])
        in_add = pltpu.make_async_copy(add_ref, add_vm, sems.at[5])
        start_all([in_g, *in_w, in_h, in_add])
        in_g.wait()
        for q in range(3):
            g3[q, 0:64, :] = jnp.zeros((64, 640), BF)
            g3[q, 576:640, :] = jnp.zeros((64, 640), BF)
        for low, high in lanes(640):
            g = g_vm[:, low:high].astype(F32)
            g3[0, 64:576, low:high] = from_right(g).astype(BF)
            g3[1, 64:576, low:high] = g_vm[:, low:high]
            g3[2, 64:576, low:high] = from_left(g).astype(BF)
        for p in range(3):
            in_w[p].wait()
            part = None
            for q in range(3):
                tap = 640 * (3 * p + q)
                one = matmul_bt(g3[q, 64 * (2 - p) : 64 * (2 - p) + 512, :], w_vm[tap : tap + 640, :])
                part = one if part is None else part + one
            total[...] = part if p == 0 else total[...] + part
        in_h.wait()
        in_add.wait()
        count = norm_n[0]
        for low, high in lanes(640):
            valid = mask[:, 0 : high - low]
            scale, offset, inv = gain[:, low:high], bias[:, low:high], stats[1:2, low:high]
            x = h_vm[:, low:high].astype(F32)
            dz, xhat = norm_back(total[:, low:high], x, valid, stats[0:1, low:high], inv, scale, offset)
            s1 = jnp.sum(dz, axis=0, keepdims=True)
            s2 = jnp.sum(dz * xhat, axis=0, keepdims=True)
            sums_ref[0:1, low:high] = s1
            sums_ref[1:2, low:high] = s2
            back = by_image(scale * inv * (dz - s1 / count - xhat * (s2 / count)), valid)
            back = jnp.where(flags[1] == 1, back + add_vm[:, low:high].astype(F32), back)
            g_vm[:, low:high] = back.astype(BF)
        done = pltpu.make_async_copy(g_vm, out_ref, sems.at[0])
        done.start()
        done.wait()


def backward_rest(flags, norm_n, g, add, h, stats, weight, gain, bias, mask, sums):
    return pl.pallas_call(
        backward_rest_kernel,
        out_shape=(jax.ShapeDtypeStruct((512, 640), BF), jax.ShapeDtypeStruct((2, 640), F32)),
        in_specs=[SCALARS, SCALARS, ANY, ANY, ANY, INSIDE, ANY, INSIDE, INSIDE, INSIDE, INSIDE],
        out_specs=(ANY, INSIDE),
        input_output_aliases={10: 1},
        scratch_shapes=[
            pltpu.VMEM((5760, 640), BF),
            pltpu.VMEM((512, 640), BF),
            pltpu.VMEM((512, 640), BF),
            pltpu.VMEM((512, 640), BF),
            pltpu.VMEM((3, 640, 640), BF),
            pltpu.VMEM((512, 640), F32),
            pltpu.SemaphoreType.DMA((6,)),
        ],
        compiler_params=params(),
    )(flags, norm_n, g, add, h, stats, weight, gain, bias, mask, sums)


def backward_first_kernel(
    flags, norm_n, g_ref, side_ref, x_ref, stats, w_ref, gain, bias, mask, keep_sums,
    out_ref, sums_ref,
    w_vm, g_vm, side_vm, x_vm, out_vm, g2, total, sems,
):
    @pl.when(flags[0] == 0)
    def _():
        sums_ref[...] = keep_sums[...]

    @pl.when(flags[0] == 1)
    def _():
        in_g = pltpu.make_async_copy(g_ref, g_vm, sems.at[0])
        in_w = pltpu.make_async_copy(w_ref.at[pl.ds(0, 3200)], w_vm, sems.at[1])
        in_side = pltpu.make_async_copy(side_ref, side_vm, sems.at[2])
        in_x = pltpu.make_async_copy(x_ref, x_vm, sems.at[3])
        start_all([in_g, in_w, in_side, in_x])
        in_g.wait()
        for q in range(2):
            g2[q, 512:576, :] = jnp.zeros((64, 640), BF)
        for low, high in lanes(640):
            g2[0, 0:512, low:high] = g_vm[:, low:high]
            g2[1, 0:512, low:high] = from_right(g_vm[:, low:high].astype(F32)).astype(BF)
        in_w.wait()

        def tap(p, q):
            row = 320 * (3 * p + q)
            first = 64 if p == 0 else 0
            return matmul_bt(g2[1 if q == 0 else 0, first : first + 512, :], w_vm[row : row + 320, :])

        in_side.wait()
        total[0] = tap(1, 1) + matmul_bt(side_vm[...], w_vm[2880:3200, :])
        total[1] = tap(1, 2) + tap(1, 0)
        total[2] = tap(2, 1) + tap(0, 1)
        total[3] = tap(2, 2) + tap(2, 0) + tap(0, 2) + tap(0, 0)
        in_x.wait()
        count = norm_n[1]
        for low, high in lanes(320):
            valid = mask[:, 0 : high - low]
            scale, offset, inv = gain[:, low:high], bias[:, low:high], stats[1:2, low:high]
            s1 = s2 = 0.0
            for k in range(4):
                x = x_vm[k, :, low:high].astype(F32)
                dz, xhat = norm_back(total[k, :, low:high], x, valid, stats[0:1, low:high], inv, scale, offset)
                total[k, :, low:high] = dz
                s1 = s1 + jnp.sum(dz, axis=0, keepdims=True)
                s2 = s2 + jnp.sum(dz * xhat, axis=0, keepdims=True)
            sums_ref[0:1, low:high] = s1
            sums_ref[1:2, low:high] = s2
            for k in range(4):
                xhat = (x_vm[k, :, low:high].astype(F32) - stats[0:1, low:high]) * inv
                dz = total[k, :, low:high]
                back = by_image(scale * inv * (dz - s1 / count - xhat * (s2 / count)), valid)
                out_vm[k, :, low:high] = back.astype(BF)
        sums_ref[:, 320:640] = jnp.zeros((2, 320), F32)
        done = pltpu.make_async_copy(out_vm, out_ref, sems.at[0])
        done.start()
        done.wait()


def backward_first(flags, norm_n, g, side, x, stats, weight, gain, bias, mask, sums):
    return pl.pallas_call(
        backward_first_kernel,
        out_shape=(jax.ShapeDtypeStruct((4, 512, 320), BF), jax.ShapeDtypeStruct((2, 640), F32)),
        in_specs=[SCALARS, SCALARS, ANY, ANY, ANY, INSIDE, ANY, INSIDE, INSIDE, INSIDE, INSIDE],
        out_specs=(ANY, INSIDE),
        input_output_aliases={10: 1},
        scratch_shapes=[
            pltpu.VMEM((3200, 640), BF),
            pltpu.VMEM((512, 640), BF),
            pltpu.VMEM((512, 640), BF),
            pltpu.VMEM((4, 512, 320), BF),
            pltpu.VMEM((4, 512, 320), BF),
            pltpu.VMEM((2, 576, 640), BF),
            pltpu.VMEM((4, 512, 320), F32),
            pltpu.SemaphoreType.DMA((4,)),
        ],
        compiler_params=params(),
    )(flags, norm_n, g, side, x, stats, weight, gain, bias, mask, sums)


def kernel_grad_rest_kernel(flags, act_ref, g_ref, out_ref, act_vm, g_vm, g3, tile, sems):
    @pl.when(flags[0] == 1)
    def _():
        in_a = pltpu.make_async_copy(act_ref, act_vm, sems.at[0])
        in_g = pltpu.make_async_copy(g_ref, g_vm, sems.at[1])
        start_all([in_a, in_g])
        in_g.wait()
        for q in range(3):
            g3[0:64, 640 * q : 640 * q + 640] = jnp.zeros((64, 640), BF)
            g3[576:640, 640 * q : 640 * q + 640] = jnp.zeros((64, 640), BF)
        for low, high in lanes(640):
            g = g_vm[:, low:high].astype(F32)
            g3[64:576, low:high] = from_right(g).astype(BF)
            g3[64:576, 640 + low : 640 + high] = g_vm[:, low:high]
            g3[64:576, 1280 + low : 1280 + high] = from_left(g).astype(BF)
        in_a.wait()
        writes = []
        for p in range(3):
            for q in range(3):
                k = 3 * p + q
                first = 64 * (2 - p)
                if k >= 2:
                    writes[k - 2].wait()
                tile[k % 2] = matmul_at(act_vm[...], g3[first : first + 512, 640 * q : 640 * q + 640]).astype(BF)
                writes.append(
                    pltpu.make_async_copy(tile.at[k % 2], out_ref.at[pl.ds(640 * k, 640)], sems.at[2 + k % 2])
                )
                writes[-1].start()
        writes[-2].wait()
        writes[-1].wait()


def kernel_grad_rest(flags, act, g):
    return pl.pallas_call(
        kernel_grad_rest_kernel,
        out_shape=jax.ShapeDtypeStruct((5760, 640), BF),
        in_specs=[SCALARS, ANY, ANY],
        out_specs=ANY,
        scratch_shapes=[
            pltpu.VMEM((512, 640), BF),
            pltpu.VMEM((512, 640), BF),
            pltpu.VMEM((640, 1920), BF),
            pltpu.VMEM((2, 640, 640), BF),
            pltpu.SemaphoreType.DMA((4,)),
        ],
        compiler_params=params(),
    )(flags, act, g)


def kernel_grad_first_kernel(flags, act_ref, g_ref, side_ref, keep, out_ref, act_vm, g_vm, side_vm, g2, tile, sems):
    @pl.when(flags[0] == 1)
    def _():
        in_a = pltpu.make_async_copy(act_ref, act_vm, sems.at[0])
        in_g = pltpu.make_async_copy(g_ref, g_vm, sems.at[1])
        in_side = pltpu.make_async_copy(side_ref, side_vm, sems.at[2])
        start_all([in_a, in_g, in_side])
        in_g.wait()
        for q in range(2):
            g2[q, 512:576, :] = jnp.zeros((64, 640), BF)
        for low, high in lanes(640):
            g2[0, 0:512, low:high] = g_vm[:, low:high]
            g2[1, 0:512, low:high] = from_right(g_vm[:, low:high].astype(F32)).astype(BF)
        in_a.wait()
        in_side.wait()
        for k in range(9):
            p, q = divmod(k, 3)
            first = 64 if p == 0 else 0
            phase = 2 * (1 if p != 1 else 0) + (1 if q != 1 else 0)
            g = g2[1 if q == 0 else 0, first : first + 512, :]
            tile[320 * k : 320 * k + 320, :] = matmul_at(act_vm[phase], g).astype(BF)
        tile[2880:3200, :] = matmul_at(act_vm[0], side_vm[...]).astype(BF)
        tile[3200:5760, :] = jnp.zeros((2560, 640), BF)
        done = pltpu.make_async_copy(tile, out_ref, sems.at[0])
        done.start()
        done.wait()


def kernel_grad_first(flags, act, g, side, keep):
    return pl.pallas_call(
        kernel_grad_first_kernel,
        out_shape=jax.ShapeDtypeStruct((5760, 640), BF),
        in_specs=[SCALARS, ANY, ANY, ANY, ANY],
        out_specs=ANY,
        input_output_aliases={4: 0},
        scratch_shapes=[
            pltpu.VMEM((4, 512, 320), BF),
            pltpu.VMEM((512, 640), BF),
            pltpu.VMEM((512, 640), BF),
            pltpu.VMEM((2, 576, 640), BF),
            pltpu.VMEM((5760, 640), BF),
            pltpu.SemaphoreType.DMA((3,)),
        ],
        compiler_params=params(),
    )(flags, act, g, side, keep)


def hop(value, source, target):
    return lax.ppermute(value, "section", [(source, target)])


def by_micro_batch(images, image_counts, conv_weight, bn_gain, bn_bias, out_grad):
    section = lax.axis_index("section")
    row = lax.axis_index("dp")
    weight = conv_weight[0]
    counts = lax.all_gather(image_counts[0], "dp")
    valid = (row < counts).astype(F32)
    mask = jnp.broadcast_to(jnp.repeat(valid, 8)[:, None], (64, 128))
    norm_n = jnp.stack([64.0 * jnp.sum(valid), 256.0 * jnp.sum(valid)])

    def flags(index, extra=False):
        return jnp.stack([section == index, jnp.asarray(extra)]).astype(jnp.int32)

    mine = lax.all_to_all(images, "dp", 0, 0, tiled=True)
    phases = mine.reshape(8, 8, 2, 8, 2, 320).transpose(2, 4, 1, 0, 3, 5).reshape(4, 512, 320)
    top = lax.all_to_all(out_grad, "dp", 0, 0, tiled=True)
    top = top.transpose(1, 0, 2, 3).reshape(512, 640)

    h1, shortcut, act_first, stats_first = forward_first(
        flags(0), norm_n, phases, weight, bn_gain, bn_bias, mask
    )
    kept = [
        jnp.zeros((512, 640), BF), jnp.zeros((512, 640), BF), jnp.zeros((512, 640), BF), jnp.zeros((2, 640), F32)
    ]
    main, side = hop(h1, 0, 1), hop(shortcut, 0, 1)
    kept = forward_rest(flags(1, True), norm_n, main, side, weight, bn_gain, bn_bias, mask, kept)
    y1 = hop(kept[0], 1, 2)
    kept = forward_rest(flags(2, False), norm_n, y1, y1, weight, bn_gain, bn_bias, mask, kept)
    main, side = hop(kept[0], 2, 3), hop(y1, 2, 3)
    kept = forward_rest(flags(3, True), norm_n, main, side, weight, bn_gain, bn_bias, mask, kept)
    out, act, h_in, stats = kept

    sums = jnp.zeros((2, 640), F32)
    g_h3, sums = backward_rest(
        flags(3), norm_n, top, top, h_in, stats, weight, bn_gain, bn_bias, mask, sums
    )
    g_h3_here = hop(g_h3, 3, 2)
    g_y1, sums = backward_rest(
        flags(2, True), norm_n, g_h3_here, top, h_in, stats, weight, bn_gain, bn_bias, mask, sums
    )
    g_y1_here = hop(g_y1, 2, 1)
    g_h1, sums = backward_rest(
        flags(1), norm_n, g_y1_here, top, h_in, stats, weight, bn_gain, bn_bias, mask, sums
    )
    g_side = hop(g_y1_here, 1, 0)
    g_h1_here = hop(g_h1, 1, 0)
    grad_phases, sums = backward_first(
        flags(0), norm_n, g_h1_here, g_side, phases, stats_first, weight, bn_gain, bn_bias, mask, sums
    )
    g_conv = jnp.where(section == 3, top, jnp.where(section == 2, g_h3_here, g_y1_here))
    rest = jnp.stack([section > 0, section > 0]).astype(jnp.int32)
    grads = kernel_grad_rest(rest, act, g_conv)
    grads = kernel_grad_first(flags(0), act_first, g_h1_here, g_side, grads)
    weight_total = lax.psum(grads, "dp").astype(F32)
    sums = lax.psum(sums, "dp")

    grad = grad_phases.reshape(2, 2, 8, 8, 8, 320).transpose(3, 2, 0, 4, 1, 5).reshape(8, 16, 16, 320)
    parts = [grad[:, 4 * k : 4 * k + 4] for k in range(4)]
    mine = parts[0]
    for k in range(1, 4):
        mine = jnp.where(section == k, hop(parts[k], 0, k), mine)
    input_grad = lax.all_to_all(mine, "dp", 0, 0, tiled=True)
    out = jnp.where(section == 0, h1, out)
    out = out.reshape(8, 8, 8, 640).transpose(1, 0, 2, 3)
    section_outputs = lax.all_to_all(out, "dp", 0, 0, tiled=True)[None]
    return (section_outputs, input_grad, weight_total[None], sums[1][None], sums[0][None])


def solution(mesh):
    one_each = mesh.shape["dp"] == MICRO and mesh.shape["section"] == 4

    def on_device(images, *rest):
        if one_each and images.shape == (MICRO, 16, 16, 320):
            return by_micro_batch(images, *rest)
        return pipelined(images, *rest)

    return jax.shard_map(
        on_device,
        mesh=mesh,
        in_specs=(
            P("dp", None, None, None),
            P("dp"),
            P("section", None, None),
            P("section", None),
            P("section", None),
            P("dp", None, None, None),
        ),
        out_specs=(
            P("section", "dp", None, None, None),
            P("dp", "section", None, None),
            P("section", None, None),
            P("section", None),
            P("section", None),
        ),
        check_vma=False,
    )
```

```python
import jax
import jax.numpy as jnp
from jax import lax
from jax.experimental import pallas as pl
from jax.experimental.pallas import tpu as pltpu
from jax.sharding import PartitionSpec as P

MICRO = 8


EPSILON = 1e-05


def for_sending(value):

    def short(part):
        return part.astype(jnp.bfloat16) if part.dtype == jnp.float32 else part

    return jax.tree.map(short, value)


def shifted(value, axis, steps):
    count = lax.axis_size(axis)
    initial, last = (max(0, -steps), min(count, count - steps))
    return lax.ppermute(value, axis, [(source, source + steps) for source in range(initial, last)])


def conv_forward(activation, kernel, stride):
    return lax.conv_general_dilated(
        activation,
        kernel,
        (stride, stride),
        ((1, 1), (1, 1)),
        dimension_numbers=("NHWC", "HWIO", "NHWC"),
        preferred_element_type=jnp.float32,
    )


def conv_input_grad(gradient, kernel, stride):
    upper = 1 if stride == 1 else 2
    return lax.conv_general_dilated(
        gradient,
        kernel[::-1, ::-1],
        (1, 1),
        ((1, upper), (1, upper)),
        lhs_dilation=(stride, stride),
        dimension_numbers=("NHWC", "HWOI", "NHWC"),
        preferred_element_type=jnp.float32,
    )


def conv_kernel_grad(activation, gradient, stride):
    upper = 1 if stride == 1 else 0
    return lax.conv_general_dilated(
        activation,
        gradient,
        (1, 1),
        ((1, upper), (1, upper)),
        rhs_dilation=(stride, stride),
        dimension_numbers=("CHWN", "IHWO", "HWNC"),
        preferred_element_type=jnp.float32,
    )


def channel_sum(values, image_mask):
    return jnp.sum(image_mask[:, None, None, None] * values, axis=(0, 1, 2))


def normalize(values, channel_mean, inv_std, norm_gain, norm_bias):
    scaled = (values - channel_mean) * inv_std
    return (scaled, scaled * norm_gain + norm_bias)


def norm_terms(grad_act, values, image_mask, channel_mean, inv_std, norm_gain, norm_bias):
    scaled, pre_act = normalize(values, channel_mean, inv_std, norm_gain, norm_bias)
    sigmoid_val = jax.nn.sigmoid(pre_act)
    grad_pre = (
        grad_act
        * image_mask[:, None, None, None]
        * sigmoid_val
        * (1.0 + pre_act * (1.0 - sigmoid_val))
    )
    return (grad_pre, scaled)


def pipelined(images, image_counts, conv_weight, bn_gain, bn_bias, out_grad):
    section_count = lax.axis_size("section")
    section_index = lax.axis_index("section")
    img_dev = images.shape[0]
    per_micro = img_dev // MICRO
    height = images.shape[1]
    side = height // 2
    c_in = images.shape[3]
    c_out = conv_weight.shape[2]
    kernel_rows = conv_weight.shape[1]
    is_first = section_index == 0
    is_last = section_index == section_count - 1
    adds_residual = section_index % 2 == 1
    merges_back = (section_index % 2 == 0) & (section_index > 0)
    valid_img = (jnp.arange(img_dev, dtype=jnp.int32) < image_counts[0]).astype(jnp.float32)
    valid_img = valid_img.reshape(per_micro, MICRO)
    image_groups = images.reshape(per_micro, MICRO, height, height, c_in)
    grad_groups = out_grad.reshape(per_micro, MICRO, side, side, c_out)
    kernel_all = conv_weight[0]
    kernel_first = kernel_all[: 9 * c_in].reshape(3, 3, c_in, c_out)
    kernel_proj = kernel_all[9 * c_in : 10 * c_in]
    kernel_rest = kernel_all.reshape(3, 3, c_out, c_out)
    norm_gain = bn_gain[0]
    norm_bias = bn_bias[0]
    tick_count = MICRO + section_count - 1
    pad_width = (0, c_out - c_in)

    def forward_first(raw_input, section_input, residual, image_mask, channel_mean, inv_std):
        scaled, pre_act = normalize(
            raw_input, channel_mean[:c_in], inv_std[:c_in], norm_gain[:c_in], norm_bias[:c_in]
        )
        activation = (jax.nn.silu(pre_act) * image_mask[:, None, None, None]).astype(jnp.bfloat16)
        conv_out = conv_forward(activation, kernel_first, 2)
        sub_grid = activation[:, 0::2, 0::2, :].reshape(-1, c_in)
        projected = jnp.dot(sub_grid, kernel_proj, preferred_element_type=jnp.float32)
        projected = projected.reshape(per_micro, side, side, c_out)
        return (conv_out.astype(jnp.bfloat16), projected.astype(jnp.bfloat16))

    def forward_rest(raw_input, section_input, residual, image_mask, channel_mean, inv_std):
        scaled, pre_act = normalize(section_input, channel_mean, inv_std, norm_gain, norm_bias)
        activation = (jax.nn.silu(pre_act) * image_mask[:, None, None, None]).astype(jnp.bfloat16)
        conv_out = conv_forward(activation, kernel_rest, 1)
        summed = conv_out + jnp.where(adds_residual, 1.0, 0.0) * residual.astype(jnp.float32)
        sent_main = summed.astype(jnp.bfloat16)
        return (sent_main, jnp.where(adds_residual, sent_main, residual))

    def forward_tick(step_index, state_carry):
        recv_main, recv_side, out_buf, in_buf, moment_buf, count_buf = state_carry
        micro_index = step_index - section_index
        active = (micro_index >= 0) & (micro_index < MICRO)
        slot_index = jnp.clip(micro_index, 0, MICRO - 1)
        image_mask = lax.dynamic_index_in_dim(valid_img, slot_index, 1, keepdims=False)
        raw_input = lax.dynamic_index_in_dim(image_groups, slot_index, 1, keepdims=False).astype(
            jnp.float32
        )
        section_input = recv_main.astype(jnp.float32)
        positions = jnp.where(is_first, float(height * height), float(side * side))
        local_count = jnp.sum(image_mask) * positions
        local_total = jnp.where(
            is_first,
            jnp.pad(channel_sum(raw_input, image_mask), pad_width),
            channel_sum(section_input, image_mask),
        )
        total_sum, count_sum = lax.psum((local_total, local_count), "dp")
        channel_mean = total_sum / count_sum
        first_dev = raw_input - channel_mean[:c_in]
        rest_dev = section_input - channel_mean
        local_spread = jnp.where(
            is_first,
            jnp.pad(channel_sum(first_dev * first_dev, image_mask), pad_width),
            channel_sum(rest_dev * rest_dev, image_mask),
        )
        spread_sum = lax.psum(local_spread, "dp")
        variance = spread_sum / count_sum
        inv_std = lax.rsqrt(variance + EPSILON)
        sent_main, sent_side = lax.cond(
            is_first,
            forward_first,
            forward_rest,
            raw_input,
            section_input,
            recv_side,
            image_mask,
            channel_mean,
            inv_std,
        )
        old_out = lax.dynamic_index_in_dim(out_buf, slot_index, 0, keepdims=False)
        out_buf = lax.dynamic_update_index_in_dim(
            out_buf, jnp.where(active, sent_main, old_out), slot_index, 0
        )
        old_in = lax.dynamic_index_in_dim(in_buf, slot_index, 0, keepdims=False)
        in_buf = lax.dynamic_update_index_in_dim(
            in_buf, jnp.where(active, recv_main, old_in), slot_index, 0
        )
        moments = jnp.stack([channel_mean, inv_std])
        old_moment = lax.dynamic_index_in_dim(moment_buf, slot_index, 0, keepdims=False)
        moment_buf = lax.dynamic_update_index_in_dim(
            moment_buf, jnp.where(active, moments, old_moment), slot_index, 0
        )
        old_count = lax.dynamic_index_in_dim(count_buf, slot_index, 0, keepdims=False)
        count_buf = lax.dynamic_update_index_in_dim(
            count_buf, jnp.where(active, count_sum, old_count), slot_index, 0
        )
        recv_main, recv_side = (
            shifted(for_sending(sent_main), "section", 1).astype(sent_main.dtype),
            shifted(for_sending(sent_side), "section", 1).astype(sent_side.dtype),
        )
        return (recv_main, recv_side, out_buf, in_buf, moment_buf, count_buf)

    act_zeros = jnp.zeros((per_micro, side, side, c_out), jnp.bfloat16)
    forward_init = (
        act_zeros,
        act_zeros,
        jnp.zeros((MICRO, per_micro, side, side, c_out), jnp.bfloat16),
        jnp.zeros((MICRO, per_micro, side, side, c_out), jnp.bfloat16),
        jnp.zeros((MICRO, 2, c_out), jnp.float32),
        jnp.ones((MICRO,), jnp.float32),
    )
    forward_done = lax.fori_loop(0, tick_count, forward_tick, forward_init)
    out_buf, in_buf, moment_buf, count_buf = (
        forward_done[2],
        forward_done[3],
        forward_done[4],
        forward_done[5],
    )

    def backward_first(
        raw_input, section_input, grad_conv, grad_side, image_mask, channel_mean, inv_std
    ):
        scaled, pre_act = normalize(
            raw_input, channel_mean[:c_in], inv_std[:c_in], norm_gain[:c_in], norm_bias[:c_in]
        )
        activation = (jax.nn.silu(pre_act) * image_mask[:, None, None, None]).astype(jnp.bfloat16)
        kernel_part = conv_kernel_grad(activation, grad_conv, 2).reshape(9 * c_in, c_out)
        sub_grid = activation[:, 0::2, 0::2, :].reshape(-1, c_in)
        side_flat = grad_side.reshape(-1, c_out)
        proj_part = lax.dot_general(
            sub_grid, side_flat, (((0,), (0,)), ((), ())), preferred_element_type=jnp.float32
        )
        weight_part = jnp.concatenate(
            [kernel_part, proj_part, jnp.zeros((kernel_rows - 10 * c_in, c_out), jnp.float32)],
            axis=0,
        )
        sub_grad = lax.dot_general(
            side_flat, kernel_proj, (((1,), (1,)), ((), ())), preferred_element_type=jnp.float32
        )
        sub_grad = sub_grad.reshape(per_micro, side, side, c_in)
        spread_grad = lax.pad(
            sub_grad, jnp.float32(0.0), ((0, 0, 0), (0, 1, 1), (0, 1, 1), (0, 0, 0))
        )
        grad_first = conv_input_grad(grad_conv, kernel_first, 2) + spread_grad
        return (weight_part, grad_first, jnp.zeros((per_micro, side, side, c_out), jnp.float32))

    def backward_rest(
        raw_input, section_input, grad_conv, grad_side, image_mask, channel_mean, inv_std
    ):
        scaled, pre_act = normalize(section_input, channel_mean, inv_std, norm_gain, norm_bias)
        activation = (jax.nn.silu(pre_act) * image_mask[:, None, None, None]).astype(jnp.bfloat16)
        weight_part = conv_kernel_grad(activation, grad_conv, 1).reshape(kernel_rows, c_out)
        grad_rest = conv_input_grad(grad_conv, kernel_rest, 1)
        return (weight_part, jnp.zeros((per_micro, height, height, c_in), jnp.float32), grad_rest)

    def backward_tick(step_index, state_carry):
        recv_main, recv_side, weight_acc, gain_acc, bias_acc, input_buf = state_carry
        micro_index = step_index - (section_count - 1 - section_index)
        active = (micro_index >= 0) & (micro_index < MICRO)
        slot_index = jnp.clip(micro_index, 0, MICRO - 1)
        image_mask = lax.dynamic_index_in_dim(valid_img, slot_index, 1, keepdims=False)
        raw_input = lax.dynamic_index_in_dim(image_groups, slot_index, 1, keepdims=False).astype(
            jnp.float32
        )
        section_input = lax.dynamic_index_in_dim(in_buf, slot_index, 0, keepdims=False).astype(
            jnp.float32
        )
        moments = lax.dynamic_index_in_dim(moment_buf, slot_index, 0, keepdims=False)
        channel_mean, inv_std = (moments[0], moments[1])
        count_sum = lax.dynamic_index_in_dim(count_buf, slot_index, 0, keepdims=False)
        top_grad = jnp.where(
            is_last, lax.dynamic_index_in_dim(grad_groups, slot_index, 1, keepdims=False), recv_main
        )
        joined = (top_grad.astype(jnp.float32) + recv_side.astype(jnp.float32)).astype(jnp.bfloat16)
        grad_conv = jnp.where(adds_residual, joined, top_grad)
        grad_side = jnp.where(adds_residual, joined, recv_side)
        weight_part, grad_first, grad_rest = lax.cond(
            is_first,
            backward_first,
            backward_rest,
            raw_input,
            section_input,
            grad_conv,
            grad_side,
            image_mask,
            channel_mean,
            inv_std,
        )
        pre_first, scaled_first = norm_terms(
            grad_first,
            raw_input,
            image_mask,
            channel_mean[:c_in],
            inv_std[:c_in],
            norm_gain[:c_in],
            norm_bias[:c_in],
        )
        pre_rest, scaled_rest = norm_terms(
            grad_rest, section_input, image_mask, channel_mean, inv_std, norm_gain, norm_bias
        )
        local_pre = jnp.where(
            is_first,
            jnp.pad(jnp.sum(pre_first, axis=(0, 1, 2)), pad_width),
            jnp.sum(pre_rest, axis=(0, 1, 2)),
        )
        local_cross = jnp.where(
            is_first,
            jnp.pad(jnp.sum(pre_first * scaled_first, axis=(0, 1, 2)), pad_width),
            jnp.sum(pre_rest * scaled_rest, axis=(0, 1, 2)),
        )
        sum_pre, sum_cross = lax.psum((local_pre, local_cross), "dp")
        mean_pre = sum_pre / count_sum
        mean_cross = sum_cross / count_sum
        mask_four = image_mask[:, None, None, None]
        grad_in_rest = (
            mask_four * inv_std * norm_gain * (pre_rest - mean_pre - scaled_rest * mean_cross)
        )
        grad_in_first = (
            mask_four
            * inv_std[:c_in]
            * norm_gain[:c_in]
            * (pre_first - mean_pre[:c_in] - scaled_first * mean_cross[:c_in])
        )
        sent_main = jnp.where(
            merges_back, grad_in_rest + grad_side.astype(jnp.float32), grad_in_rest
        ).astype(jnp.bfloat16)
        sent_side = jnp.where(merges_back, jnp.zeros_like(grad_side), grad_side)
        weight_acc = weight_acc + jnp.where(active, weight_part, 0.0)
        gain_acc = gain_acc + jnp.where(active, sum_cross, 0.0)
        bias_acc = bias_acc + jnp.where(active, sum_pre, 0.0)
        old_input = lax.dynamic_index_in_dim(input_buf, slot_index, 0, keepdims=False)
        input_buf = lax.dynamic_update_index_in_dim(
            input_buf, jnp.where(active, grad_in_first, old_input), slot_index, 0
        )
        recv_main, recv_side = shifted((sent_main, sent_side), "section", -1)
        return (recv_main, recv_side, weight_acc, gain_acc, bias_acc, input_buf)

    backward_init = (
        act_zeros,
        act_zeros,
        jnp.zeros((kernel_rows, c_out), jnp.float32),
        jnp.zeros((c_out,), jnp.float32),
        jnp.zeros((c_out,), jnp.float32),
        jnp.zeros((MICRO, per_micro, height, height, c_in), jnp.float32),
    )
    backward_done = lax.fori_loop(0, tick_count, backward_tick, backward_init)
    weight_acc, gain_acc, bias_acc, input_buf = (
        backward_done[2],
        backward_done[3],
        backward_done[4],
        backward_done[5],
    )
    weight_total = lax.psum(weight_acc, "dp")
    input_full = jnp.transpose(input_buf, (1, 0, 2, 3, 4)).reshape(img_dev, height, height, c_in)
    input_full = jnp.where(is_first, input_full, 0.0)
    input_grad = lax.psum_scatter(
        input_full.astype(jnp.bfloat16), "section", scatter_dimension=1, tiled=True
    )
    section_outputs = jnp.transpose(out_buf, (1, 0, 2, 3, 4)).reshape(img_dev, side, side, c_out)[
        None
    ]
    return (section_outputs, input_grad, weight_total[None], gain_acc[None], bias_acc[None])


BF = jnp.bfloat16
F32 = jnp.float32
INF = float("inf")
VMEM_BYTES = 48 * 1024 * 1024
ANY = pl.BlockSpec(memory_space=pl.ANY)
INSIDE = pl.BlockSpec(memory_space=pltpu.VMEM)
SCALARS = pl.BlockSpec(memory_space=pltpu.SMEM)
FIELD = jax.ShapeDtypeStruct((512, 640), BF)
TWO = jax.ShapeDtypeStruct((2, 512, 640), BF)
PAIR = jax.ShapeDtypeStruct((2, 640), F32)


def lane(k, first=0):
    return pl.ds(pl.multiple_of(first + 128 * k, 128), 128)


def from_left(values):
    column = lax.broadcasted_iota(jnp.int32, values.shape, 0) & 7
    return jnp.where(column == 0, 0.0, pltpu.roll(values, 1, 0))


def from_right(values):
    column = lax.broadcasted_iota(jnp.int32, values.shape, 0) & 7
    return jnp.where(column == 7, 0.0, pltpu.roll(values, values.shape[0] - 1, 0))


def total_of(values):
    return jnp.sum(values, axis=0, keepdims=True)


def count_of(valid):
    return total_of(jnp.where(valid, 1.0, 0.0))


def sigmoid(z):
    return 0.5 * jnp.tanh(0.5 * z) + 0.5


def matmul(a, b):
    return jnp.dot(a, b, preferred_element_type=F32)


def matmul_bt(a, b):
    return lax.dot_general(a, b, (((1,), (1,)), ((), ())), preferred_element_type=F32)


def matmul_at(a, b):
    return lax.dot_general(a, b, (((0,), (0,)), ((), ())), preferred_element_type=F32)


def start_all(copies):
    for one in copies:
        one.start()


def wait_all(copies):
    for one in copies:
        one.wait()


def kernel_call(kernel, out_shape, in_specs, out_specs, scratch, aliases=None, flops=0):
    return pl.pallas_call(
        kernel,
        out_shape=out_shape,
        in_specs=in_specs,
        out_specs=out_specs,
        scratch_shapes=scratch,
        input_output_aliases=aliases or {},
        compiler_params=pltpu.CompilerParams(vmem_limit_bytes=VMEM_BYTES),
        cost_estimate=pl.CostEstimate(flops=flops, bytes_accessed=8_000_000, transcendentals=0),
    )


def half_turn(values):
    return jnp.concatenate([values[:, 320:640], values[:, 0:320]], axis=1)


def twice(values):
    return jnp.concatenate([values[:, 0:320], values[:, 0:320]], axis=1)


def weight_first(w_ref, w_vm, sems):
    copies = []
    for p in range(3):
        copies.append(
            pltpu.make_async_copy(
                w_ref.at[pl.ds(960 * p + 320, 640)], w_vm.at[pl.ds(1024 * p, 640)], sems.at[2 * p]
            )
        )
        copies.append(
            pltpu.make_async_copy(
                w_ref.at[pl.ds(960 * p, 320)], w_vm.at[pl.ds(1024 * p + 704, 320)], sems.at[2 * p + 1]
            )
        )
        w_vm[1024 * p + 640 : 1024 * p + 704, :] = jnp.zeros((64, 640), BF)
    copies.append(pltpu.make_async_copy(w_ref.at[pl.ds(2880, 320)], w_vm.at[pl.ds(3072, 320)], sems.at[6]))
    w_vm[3392:3456, :] = jnp.zeros((64, 640), BF)
    return copies


def forward_first_kernel(
    flags, x_ref, w_ref, gain, bias, out_ref, side_ref, ring_ref, stats_ref,
    w_vm, x_vm, cat, acc, out_vm, side_vm, part, sems,
):
    @pl.when(flags[0] == 1)
    def _():
        in_x = pltpu.make_async_copy(x_ref, x_vm, sems.at[7])
        in_x.start()
        in_w = weight_first(w_ref, w_vm, sems)
        start_all(in_w)
        cat[0:64, :] = jnp.zeros((64, 1024), BF)
        part[4:5, :] = twice(gain)
        part[5:6, :] = twice(bias)
        in_x.wait()

        @pl.loop(0, 5)
        def _(k):
            here = lane(k)
            x, y = x_vm[0, :, here].astype(F32), x_vm[1, :, here].astype(F32)
            valid = x < INF
            part[0:1, here] = total_of(jnp.where(valid, x + y, 0.0))
            part[2:3, here] = 4.0 * count_of(valid)

        part[0:1, :] = (part[0:1, :] + half_turn(part[0:1, :])) / part[2:3, :]

        @pl.loop(0, 5)
        def _(k):
            here = lane(k)
            x, y = x_vm[0, :, here].astype(F32), x_vm[1, :, here].astype(F32)
            valid = x < INF
            x = x - part[0:1, here]
            y = y - part[0:1, here]
            part[1:2, here] = total_of(jnp.where(valid, x * x + y * y, 0.0))

        part[1:2, :] = lax.rsqrt((part[1:2, :] + half_turn(part[1:2, :])) / part[2:3, :] + EPSILON)
        stats_ref[...] = part[0:2, :]

        @pl.loop(0, 5)
        def _(k):
            here = lane(k)
            for a in range(2):
                x = x_vm[a, :, here].astype(F32)
                z = (x - part[0:1, here]) * part[1:2, here] * part[4:5, here] + part[5:6, here]
                act = jnp.where(x < INF, z * sigmoid(z), 0.0)
                first = 576 if a == 0 else 64
                cat[first : first + 512, here] = act.astype(BF)

                @pl.when(k >= 2)
                def _():
                    cat[first : first + 512, lane(k, 384)] = from_left(act).astype(BF)

        keep = [
            pltpu.make_async_copy(cat.at[pl.ds(576, 512), pl.ds(0, 640)], ring_ref.at[0], sems.at[8]),
            pltpu.make_async_copy(cat.at[pl.ds(64, 512), pl.ds(0, 640)], ring_ref.at[1], sems.at[9]),
        ]
        start_all(keep)
        acc[...] = jnp.zeros((512, 640), F32)
        wait_all(in_w)

        @pl.loop(0, 3)
        def _(p):
            first = pl.multiple_of(jnp.where(p == 1, 576, 32 * p), 64)
            acc[...] += matmul(cat[pl.ds(first, 512), :], w_vm[pl.ds(pl.multiple_of(1024 * p, 1024), 1024), :])

        @pl.loop(0, 5)
        def _(k):
            row_valid = x_vm[0, :, 0:128].astype(F32) < INF
            out_vm[:, lane(k)] = jnp.where(row_valid, acc[:, lane(k)], INF).astype(BF)

        out = pltpu.make_async_copy(out_vm, out_ref, sems.at[0])
        out.start()
        side_vm[...] = matmul(cat[576:1088, 0:384], w_vm[3072:3456, :]).astype(BF)
        side = pltpu.make_async_copy(side_vm, side_ref, sems.at[1])
        side.start()
        wait_all([out, side, *keep])


def forward_first(flags, x, weight, gain, bias):
    return kernel_call(
        forward_first_kernel,
        (FIELD, FIELD, TWO, PAIR),
        [SCALARS, ANY, ANY, INSIDE, INSIDE],
        (ANY, ANY, ANY, INSIDE),
        [
            pltpu.VMEM((3456, 640), BF),
            pltpu.VMEM((2, 512, 640), BF),
            pltpu.VMEM((1088, 1024), BF),
            pltpu.VMEM((512, 640), F32),
            pltpu.VMEM((512, 640), BF),
            pltpu.VMEM((512, 640), BF),
            pltpu.VMEM((8, 640), F32),
            pltpu.SemaphoreType.DMA((10,)),
        ],
        flops=4_000_000_000,
    )(flags, x, weight, gain, bias)


def weight_part(w_ref, w_vm, sems, p):
    rows = pl.ds(pl.multiple_of(1920 * p, 1920), 1920)
    return pltpu.make_async_copy(w_ref.at[rows], w_vm.at[rows], sems.at[p])


def clear_edges(x3):
    x3[0:64, :] = jnp.zeros((64, x3.shape[1]), BF)
    x3[576:640, :] = jnp.zeros((64, x3.shape[1]), BF)


def place(x3, k, values, left, right):
    x3[64:576, lane(k, left)] = from_left(values).astype(BF)
    x3[64:576, lane(k, 640)] = values.astype(BF)
    x3[64:576, lane(k, right)] = from_right(values).astype(BF)


def forward_conv(x3, w_ref, w_vm, w_sems, acc):
    @pl.loop(0, 3)
    def _(p):
        weight_part(w_ref, w_vm, w_sems, p).wait()
        acc[...] += matmul(
            x3[pl.ds(pl.multiple_of(64 * p, 64), 512), :], w_vm[pl.ds(pl.multiple_of(1920 * p, 1920), 1920), :]
        )


def statistics(x):
    valid = x < INF
    count = count_of(valid)
    mean = total_of(jnp.where(valid, x, 0.0)) / count
    centred = jnp.where(valid, x - mean, 0.0)
    inv = lax.rsqrt(total_of(centred * centred) / count + EPSILON)
    return valid, count, mean, inv, centred


def forward_rest_kernel(
    flags, h_ref, res_ref, w_ref, gain, bias, keep_ring, out_ref, stats_ref, ring_ref,
    w_vm, h_vm, res_vm, x3, acc, sems, w_sems,
):
    @pl.when(flags[0] == 1)
    def _():
        in_h = pltpu.make_async_copy(h_ref, h_vm, sems.at[0])
        in_res = pltpu.make_async_copy(res_ref, res_vm, sems.at[1])
        in_h.start()
        for p in range(3):
            weight_part(w_ref, w_vm, w_sems, p).start()
        in_res.start()
        clear_edges(x3)
        in_h.wait()

        @pl.loop(0, 5)
        def _(k):
            here = lane(k)
            valid, _, mean, inv, centred = statistics(h_vm[:, here].astype(F32))
            stats_ref[0:1, here] = mean
            stats_ref[1:2, here] = inv
            z = centred * inv * gain[:, here] + bias[:, here]
            place(x3, k, jnp.where(valid, z * sigmoid(z), 0.0), 0, 1280)

        keep = pltpu.make_async_copy(x3.at[pl.ds(64, 512), pl.ds(640, 640)], ring_ref.at[0], sems.at[2])
        keep.start()
        in_res.wait()
        adds = flags[1] == 1

        @pl.loop(0, 5)
        def _(k):
            acc[:, lane(k)] = jnp.where(adds, res_vm[:, lane(k)].astype(F32), 0.0)

        forward_conv(x3, w_ref, w_vm, w_sems, acc)

        @pl.loop(0, 5)
        def _(k):
            row_valid = h_vm[:, 0:128].astype(F32) < INF
            res_vm[:, lane(k)] = jnp.where(row_valid, acc[:, lane(k)], INF).astype(BF)

        done = pltpu.make_async_copy(res_vm, out_ref, sems.at[0])
        done.start()
        wait_all([done, keep])


def forward_rest(flags, h, res, weight, gain, bias, keep_ring):
    return kernel_call(
        forward_rest_kernel,
        (FIELD, PAIR, TWO),
        [SCALARS, ANY, ANY, ANY, INSIDE, INSIDE, ANY],
        (ANY, INSIDE, ANY),
        [
            pltpu.VMEM((5760, 640), BF),
            pltpu.VMEM((512, 640), BF),
            pltpu.VMEM((512, 640), BF),
            pltpu.VMEM((640, 1920), BF),
            pltpu.VMEM((512, 640), F32),
            pltpu.SemaphoreType.DMA((3,)),
            pltpu.SemaphoreType.DMA((3,)),
        ],
        aliases={6: 2},
        flops=4_000_000_000,
    )(flags, h, res, weight, gain, bias, keep_ring)


def forward_last_kernel(
    flags, ring_ref, h_ref, res_ref, w_ref, out_ref, w_vm, a_vm, h_vm, res_vm, x3, acc, sems, w_sems
):
    @pl.when(flags[0] == 1)
    def _():
        ins = [
            pltpu.make_async_copy(ring_ref.at[0], a_vm, sems.at[0]),
            pltpu.make_async_copy(h_ref, h_vm, sems.at[1]),
            pltpu.make_async_copy(res_ref, res_vm, sems.at[2]),
        ]
        start_all(ins)
        for p in range(3):
            weight_part(w_ref, w_vm, w_sems, p).start()
        clear_edges(x3)
        wait_all(ins)

        @pl.loop(0, 5)
        def _(k):
            place(x3, k, a_vm[:, lane(k)].astype(F32), 0, 1280)
            acc[:, lane(k)] = res_vm[:, lane(k)].astype(F32)

        forward_conv(x3, w_ref, w_vm, w_sems, acc)

        @pl.loop(0, 5)
        def _(k):
            row_valid = h_vm[:, 0:128].astype(F32) < INF
            res_vm[:, lane(k)] = jnp.where(row_valid, acc[:, lane(k)], INF).astype(BF)

        done = pltpu.make_async_copy(res_vm, out_ref, sems.at[0])
        done.start()
        done.wait()


def forward_last(flags, ring, h, res, weight):
    return kernel_call(
        forward_last_kernel,
        FIELD,
        [SCALARS, ANY, ANY, ANY, ANY],
        ANY,
        [
            pltpu.VMEM((5760, 640), BF),
            pltpu.VMEM((512, 640), BF),
            pltpu.VMEM((512, 640), BF),
            pltpu.VMEM((512, 640), BF),
            pltpu.VMEM((640, 1920), BF),
            pltpu.VMEM((512, 640), F32),
            pltpu.SemaphoreType.DMA((3,)),
            pltpu.SemaphoreType.DMA((3,)),
        ],
        flops=4_000_000_000,
    )(flags, ring, h, res, weight)


def backward_conv(g_vm, g3, w_ref, w_vm, w_sems, acc):
    clear_edges(g3)

    @pl.loop(0, 5)
    def _(k):
        place(g3, k, g_vm[:, lane(k)].astype(F32), 1280, 0)
        acc[:, lane(k)] = jnp.zeros((512, 128), F32)

    @pl.loop(0, 3)
    def _(p):
        weight_part(w_ref, w_vm, w_sems, p).wait()

        @pl.loop(0, 3)
        def _(q):
            acc[...] += matmul_bt(
                g3[pl.ds(pl.multiple_of(64 * (2 - p), 64), 512), pl.ds(pl.multiple_of(640 * q, 640), 640)],
                w_vm[pl.ds(pl.multiple_of(640 * (3 * p + q), 640), 640), :],
            )


def backward_top_kernel(flags, g_ref, w_ref, keep_ring, total_ref, ring_ref, w_vm, g_vm, g3, acc, sems, w_sems):
    @pl.when(flags[0] == 1)
    def _():
        in_g = pltpu.make_async_copy(g_ref, g_vm, sems.at[0])
        in_g.start()
        for p in range(3):
            weight_part(w_ref, w_vm, w_sems, p).start()
        in_g.wait()
        keep = pltpu.make_async_copy(g_vm, ring_ref.at[1], sems.at[1])
        keep.start()
        backward_conv(g_vm, g3, w_ref, w_vm, w_sems, acc)
        done = pltpu.make_async_copy(acc, total_ref, sems.at[0])
        done.start()
        wait_all([done, keep])


def backward_top(flags, g, weight, keep_ring):
    return kernel_call(
        backward_top_kernel,
        (jax.ShapeDtypeStruct((512, 640), F32), TWO),
        [SCALARS, ANY, ANY, ANY],
        (ANY, ANY),
        [
            pltpu.VMEM((5760, 640), BF),
            pltpu.VMEM((512, 640), BF),
            pltpu.VMEM((640, 1920), BF),
            pltpu.VMEM((512, 640), F32),
            pltpu.SemaphoreType.DMA((2,)),
            pltpu.SemaphoreType.DMA((3,)),
        ],
        aliases={3: 1},
        flops=4_000_000_000,
    )(flags, g, weight, keep_ring)


def norm_back(grad, valid, count, centred, inv, scale, offset, sums_ref, here):
    xhat = centred * inv
    z = xhat * scale + offset
    sig = sigmoid(z)
    dz = jnp.where(valid, grad * sig * (1.0 + z * (1.0 - sig)), 0.0)
    s1 = total_of(dz)
    s2 = total_of(dz * xhat)
    sums_ref[0:1, here] = s1
    sums_ref[1:2, here] = s2
    back = scale * inv * (dz - s1 / count - xhat * (s2 / count))
    return jnp.where(valid, back, 0.0), jnp.where(valid, z * sig, 0.0)


def turn_kernel(
    flags, h_ref, grad_ref, gain, bias, keep_ring, out_ref, sums_ref, ring_ref, h_vm, grad, a_vm, g_vm, sems
):
    @pl.when(flags[0] == 1)
    def _():
        ins = [pltpu.make_async_copy(h_ref, h_vm, sems.at[0]), pltpu.make_async_copy(grad_ref, grad, sems.at[1])]
        start_all(ins)
        wait_all(ins)

        @pl.loop(0, 5)
        def _(k):
            here = lane(k)
            valid, count, _, inv, centred = statistics(h_vm[:, here].astype(F32))
            back, act = norm_back(
                grad[:, here], valid, count, centred, inv, gain[:, here], bias[:, here], sums_ref, here
            )
            a_vm[:, here] = act.astype(BF)
            g_vm[:, here] = back.astype(BF)

        outs = [
            pltpu.make_async_copy(g_vm, out_ref, sems.at[0]),
            pltpu.make_async_copy(a_vm, ring_ref.at[0], sems.at[1]),
        ]
        start_all(outs)
        wait_all(outs)


def turn(flags, h, grad, gain, bias, keep_ring):
    return kernel_call(
        turn_kernel,
        (FIELD, PAIR, TWO),
        [SCALARS, ANY, ANY, INSIDE, INSIDE, ANY],
        (ANY, INSIDE, ANY),
        [
            pltpu.VMEM((512, 640), BF),
            pltpu.VMEM((512, 640), F32),
            pltpu.VMEM((512, 640), BF),
            pltpu.VMEM((512, 640), BF),
            pltpu.SemaphoreType.DMA((2,)),
        ],
        aliases={5: 2},
        flops=1_000_000_000,
    )(flags, h, grad, gain, bias, keep_ring)


def backward_rest_kernel(
    flags, g_ref, add_ref, h_ref, stats, w_ref, gain, bias, keep_ring, out_ref, sums_ref, ring_ref,
    w_vm, g_vm, add_vm, h_vm, g3, acc, sems, w_sems,
):
    @pl.when(flags[0] == 1)
    def _():
        in_g = pltpu.make_async_copy(g_ref, g_vm, sems.at[0])
        ins = [pltpu.make_async_copy(h_ref, h_vm, sems.at[1]), pltpu.make_async_copy(add_ref, add_vm, sems.at[2])]
        in_g.start()
        for p in range(3):
            weight_part(w_ref, w_vm, w_sems, p).start()
        start_all(ins)
        in_g.wait()
        keep = pltpu.make_async_copy(g_vm, ring_ref.at[1], sems.at[3])
        keep.start()
        backward_conv(g_vm, g3, w_ref, w_vm, w_sems, acc)
        wait_all([*ins, keep])
        adds = flags[1] == 1

        @pl.loop(0, 5)
        def _(k):
            here = lane(k)
            x = h_vm[:, here].astype(F32)
            valid = x < INF
            centred = jnp.where(valid, x - stats[0:1, here], 0.0)
            back, _ = norm_back(
                acc[:, here], valid, count_of(valid), centred, stats[1:2, here], gain[:, here], bias[:, here],
                sums_ref, here,
            )
            g_vm[:, here] = jnp.where(adds, back + add_vm[:, here].astype(F32), back).astype(BF)

        done = pltpu.make_async_copy(g_vm, out_ref, sems.at[0])
        done.start()
        done.wait()


def backward_rest(flags, g, add, h, stats, weight, gain, bias, keep_ring):
    return kernel_call(
        backward_rest_kernel,
        (FIELD, PAIR, TWO),
        [SCALARS, ANY, ANY, ANY, INSIDE, ANY, INSIDE, INSIDE, ANY],
        (ANY, INSIDE, ANY),
        [
            pltpu.VMEM((5760, 640), BF),
            pltpu.VMEM((512, 640), BF),
            pltpu.VMEM((512, 640), BF),
            pltpu.VMEM((512, 640), BF),
            pltpu.VMEM((640, 1920), BF),
            pltpu.VMEM((512, 640), F32),
            pltpu.SemaphoreType.DMA((4,)),
            pltpu.SemaphoreType.DMA((3,)),
        ],
        aliases={8: 2},
        flops=4_000_000_000,
    )(flags, g, add, h, stats, weight, gain, bias, keep_ring)


def backward_first_kernel(
    flags, g_ref, side_ref, x_ref, stats, w_ref, gain, bias, out_ref, sums_ref,
    w_vm, g_vm, side_vm, x_vm, g2, acc, part, sems,
):
    @pl.when(flags[0] == 1)
    def _():
        in_g = pltpu.make_async_copy(g_ref, g_vm, sems.at[7])
        ins = [pltpu.make_async_copy(side_ref, side_vm, sems.at[8]), pltpu.make_async_copy(x_ref, x_vm, sems.at[9])]
        in_g.start()
        in_w = weight_first(w_ref, w_vm, sems)
        start_all(in_w)
        start_all(ins)
        g2[512:576, :] = jnp.zeros((64, 1280), BF)
        part[4:5, :] = twice(gain)
        part[5:6, :] = twice(bias)
        in_g.wait()

        @pl.loop(0, 5)
        def _(k):
            g = g_vm[:, lane(k)].astype(F32)
            g2[0:512, lane(k)] = g.astype(BF)
            g2[0:512, lane(k, 640)] = from_right(g).astype(BF)

        acc[...] = jnp.zeros((2, 512, 640), F32)
        wait_all(in_w)

        @pl.loop(0, 3)
        def _(p):
            rows = pl.ds(pl.multiple_of(jnp.where(p == 0, 64, 0), 64), 512)
            a = jnp.where(p == 1, 0, 1)
            first = pl.multiple_of(1024 * p, 1024)
            acc[a] += matmul_bt(g2[rows, 0:640], w_vm[pl.ds(first, 640), :])
            acc[a, :, 256:640] += matmul_bt(g2[rows, 640:1280], w_vm[pl.ds(first + 640, 384), :])

        wait_all(ins)
        acc[0, :, 0:384] += matmul_bt(side_vm[...], w_vm[3072:3456, :])

        @pl.loop(0, 5)
        def _(k):
            here = lane(k)
            s1 = s2 = 0.0
            for a in range(2):
                x = x_vm[a, :, here].astype(F32)
                valid = x < INF
                xhat = jnp.where(valid, x - stats[0:1, here], 0.0) * stats[1:2, here]
                z = xhat * part[4:5, here] + part[5:6, here]
                sig = sigmoid(z)
                dz = jnp.where(valid, acc[a, :, here] * sig * (1.0 + z * (1.0 - sig)), 0.0)
                acc[a, :, here] = dz
                s1 = s1 + total_of(dz)
                s2 = s2 + total_of(dz * xhat)
            part[0:1, here] = s1
            part[1:2, here] = s2
            part[2:3, here] = 4.0 * count_of(valid)

        part[0:1, :] = part[0:1, :] + half_turn(part[0:1, :])
        part[1:2, :] = part[1:2, :] + half_turn(part[1:2, :])
        sums_ref[...] = jnp.where(lax.broadcasted_iota(jnp.int32, (2, 640), 1) < 320, part[0:2, :], 0.0)

        @pl.loop(0, 5)
        def _(k):
            here = lane(k)
            count = part[2:3, here]
            scale = part[4:5, here] * stats[1:2, here]
            for a in range(2):
                x = x_vm[a, :, here].astype(F32)
                xhat = (x - stats[0:1, here]) * stats[1:2, here]
                back = scale * (acc[a, :, here] - part[0:1, here] / count - xhat * (part[1:2, here] / count))
                x_vm[a, :, here] = jnp.where(x < INF, back, 0.0).astype(BF)

        done = pltpu.make_async_copy(x_vm, out_ref, sems.at[0])
        done.start()
        done.wait()


def backward_first(flags, g, side, x, stats, weight, gain, bias):
    return kernel_call(
        backward_first_kernel,
        (TWO, PAIR),
        [SCALARS, ANY, ANY, ANY, INSIDE, ANY, INSIDE, INSIDE],
        (ANY, INSIDE),
        [
            pltpu.VMEM((3456, 640), BF),
            pltpu.VMEM((512, 640), BF),
            pltpu.VMEM((512, 640), BF),
            pltpu.VMEM((2, 512, 640), BF),
            pltpu.VMEM((576, 1280), BF),
            pltpu.VMEM((2, 512, 640), F32),
            pltpu.VMEM((8, 640), F32),
            pltpu.SemaphoreType.DMA((10,)),
        ],
        flops=5_000_000_000,
    )(flags, g, side, x, stats, weight, gain, bias)


def projection_grad_kernel(flags, ring_ref, g_ref, out_ref, a_vm, g_vm, out_vm, sems):
    @pl.when(flags[0] == 1)
    def _():
        ins = [pltpu.make_async_copy(ring_ref.at[0], a_vm, sems.at[0]), pltpu.make_async_copy(g_ref, g_vm, sems.at[1])]
        start_all(ins)
        wait_all(ins)
        out_vm[...] = matmul_at(a_vm[:, 0:384], g_vm[...])[0:320, :]
        done = pltpu.make_async_copy(out_vm, out_ref, sems.at[0])
        done.start()
        done.wait()


def projection_grad(flags, ring, g):
    return kernel_call(
        projection_grad_kernel,
        jax.ShapeDtypeStruct((320, 640), F32),
        [SCALARS, ANY, ANY],
        ANY,
        [
            pltpu.VMEM((512, 640), BF),
            pltpu.VMEM((512, 640), BF),
            pltpu.VMEM((320, 640), F32),
            pltpu.SemaphoreType.DMA((2,)),
        ],
        flops=200_000_000,
    )(flags, ring, g)


def kernel_grad_rest_kernel(blocks, fresh, flags, *refs):
    rings = refs[:blocks]
    out_ref, a_vm, g_vm, g3, tile, sems, read_sems, write_sems = refs[blocks + (0 if fresh else 1) :]

    def moves(p, out):
        slot = lax.rem(p, 2)
        copies = []
        for q in range(3):
            here = tile.at[slot, :, pl.ds(640 * q, 640)]
            there = out_ref.at[pl.ds(pl.multiple_of(640 * (3 * p + q), 640), 640)]
            if out:
                copies.append(pltpu.make_async_copy(here, there, write_sems.at[slot, q]))
            else:
                copies.append(pltpu.make_async_copy(there, here, read_sems.at[slot, q]))
        return copies

    @pl.when(flags[0] == 1)
    def _():
        ins = []
        for b in range(blocks):
            ins.append(pltpu.make_async_copy(rings[b].at[1], g_vm.at[b], sems.at[2 * b]))
            ins.append(pltpu.make_async_copy(rings[b].at[0], a_vm.at[b], sems.at[2 * b + 1]))
        start_all(ins)
        if not fresh:
            start_all(moves(0, False))
            start_all(moves(1, False))
        wait_all(ins)

        @pl.loop(0, blocks)
        def _(b):
            clear_edges(g3.at[b])

            @pl.loop(0, 5)
            def _(k):
                place(g3.at[b], k, g_vm[b, :, lane(k)].astype(F32), 1280, 0)

        @pl.loop(0, 3)
        def _(p):
            slot = lax.rem(p, 2)

            @pl.when(p == 2)
            def _():
                wait_all(moves(0, True))
                if not fresh:
                    start_all(moves(2, False))

            if fresh:
                tile[slot] = jnp.zeros((640, 1920), F32)
            else:
                wait_all(moves(p, False))

            @pl.loop(0, blocks)
            def _(b):
                tile[slot] += matmul_at(a_vm[b], g3[b, pl.ds(pl.multiple_of(64 * (2 - p), 64), 512), :])

            start_all(moves(p, True))

        wait_all(moves(1, True))
        wait_all(moves(2, True))


def kernel_grad_rest(flags, rings, kept=None):
    blocks = len(rings)
    fresh = kept is None
    return kernel_call(
        lambda *refs: kernel_grad_rest_kernel(blocks, fresh, *refs),
        jax.ShapeDtypeStruct((5760, 640), F32),
        [SCALARS] + [ANY] * (blocks + (0 if fresh else 1)),
        ANY,
        [
            pltpu.VMEM((blocks, 512, 640), BF),
            pltpu.VMEM((blocks, 512, 640), BF),
            pltpu.VMEM((blocks, 640, 1920), BF),
            pltpu.VMEM((2, 640, 1920), F32),
            pltpu.SemaphoreType.DMA((2 * blocks,)),
            pltpu.SemaphoreType.DMA((2, 3)),
            pltpu.SemaphoreType.DMA((2, 3)),
        ],
        aliases={} if fresh else {1 + blocks: 0},
        flops=4_000_000_000 * blocks,
    )(flags, *rings, *([] if fresh else [kept]))


def kernel_grad_first_kernel(blocks, fresh, last, flags, *refs):
    rings, gs = refs[:blocks], refs[blocks : 2 * blocks]
    refs = refs[2 * blocks :]
    if last:
        side_ref, refs = refs[0], refs[1:]
    _, out_ref, a_vm, g_vm, g2, tile, zeros, sems, tile_sems, extra_sems = refs

    @pl.when(flags[0] == 1)
    def _():
        ins = []
        for b in range(blocks):
            ins.append(pltpu.make_async_copy(gs[b], g_vm.at[b], sems.at[2 * b]))
            ins.append(pltpu.make_async_copy(rings[b], a_vm.at[b], sems.at[2 * b + 1]))
        start_all(ins)
        if not fresh:
            whole = pltpu.make_async_copy(out_ref.at[pl.ds(0, 2880)], tile, tile_sems.at[0])
            whole.start()
        extra = []
        if last:
            zeros[...] = jnp.zeros((320, 640), F32)
            extra.append(pltpu.make_async_copy(side_ref, out_ref.at[pl.ds(2880, 320)], extra_sems.at[0]))
            for k in range(8):
                extra.append(
                    pltpu.make_async_copy(zeros, out_ref.at[pl.ds(3200 + 320 * k, 320)], extra_sems.at[1 + k])
                )
            start_all(extra)
        wait_all(ins)

        @pl.loop(0, blocks)
        def _(b):
            g2[b, 512:576, :] = jnp.zeros((64, 1280), BF)

            @pl.loop(0, 5)
            def _(k):
                g = g_vm[b, :, lane(k)].astype(F32)
                g2[b, 0:512, lane(k)] = g.astype(BF)
                g2[b, 0:512, lane(k, 640)] = from_right(g).astype(BF)

        if fresh:
            tile[...] = jnp.zeros((2880, 640), F32)
        else:
            whole.wait()

        @pl.loop(0, 3)
        def _(p):
            rows = pl.ds(pl.multiple_of(jnp.where(p == 0, 64, 0), 64), 512)
            parity = jnp.where(p == 1, 0, 1)
            row = pl.multiple_of(960 * p, 960)

            @pl.loop(0, blocks)
            def _(b):
                tile[pl.ds(row + 320, 640), :] += matmul_at(a_vm[b, parity], g2[b, rows, 0:640])
                left = matmul_at(a_vm[b, parity, :, 256:640], g2[b, rows, 640:1280])
                tile[pl.ds(row, 320), :] += left[64:384, :]

        back = pltpu.make_async_copy(tile, out_ref.at[pl.ds(0, 2880)], tile_sems.at[1])
        back.start()
        wait_all([back, *extra])


def kernel_grad_first(flags, rings, gs, kept, fresh, side=None):
    blocks = len(rings)
    last = side is not None
    extra = [side] if last else []
    return kernel_call(
        lambda *refs: kernel_grad_first_kernel(blocks, fresh, last, *refs),
        jax.ShapeDtypeStruct((5760, 640), F32),
        [SCALARS] + [ANY] * (2 * blocks + 1 + len(extra)),
        ANY,
        [
            pltpu.VMEM((blocks, 2, 512, 640), BF),
            pltpu.VMEM((blocks, 512, 640), BF),
            pltpu.VMEM((blocks, 576, 1280), BF),
            pltpu.VMEM((2880, 640), F32),
            pltpu.VMEM((320, 640), F32),
            pltpu.SemaphoreType.DMA((2 * blocks,)),
            pltpu.SemaphoreType.DMA((2,)),
            pltpu.SemaphoreType.DMA((9,)),
        ],
        aliases={1 + 2 * blocks + len(extra): 0},
        flops=2_000_000_000 * blocks,
    )(flags, *rings, *gs, *extra, kept)


BOTH = ("dp", "section")
RING = (0, 2, 4, 6, 7, 5, 3, 1)


def move(value, triples):
    count = lax.axis_size("section")
    return lax.ppermute(value, BOTH, [(d * count + s, e * count + t) for (d, s), (e, t) in triples])


def hop(value, source, target):
    return move(value, [((d, source), (d, target)) for d in range(MICRO)])


def ring_pairs(sections):
    up = [((RING[k], s), (RING[(k + 1) % 8], s)) for k in range(8) for s in sections]
    return up, [(b, a) for a, b in up]


def dp_total(value, sections):
    for k in (1, 2, 4):
        value = value + move(value, [((d, s), (d ^ k, s)) for d in range(MICRO) for s in sections])
    return value


def after(value, *others):
    return lax.optimization_barrier((value, *others))[0]


FAR = (4, 5, 6, 7)
NEAR = (1, 2, 3, 0)


def exchange_images(images, row, section):
    far = 4 + section
    near = (section + 1) & 3
    got_far = move(
        lax.dynamic_index_in_dim(images, row ^ far, 0),
        [((d, s), (d ^ FAR[s], s)) for d in range(MICRO) for s in range(4)],
    )
    got_near = move(
        lax.dynamic_index_in_dim(images, row ^ near, 0),
        [((d, s), (d ^ NEAR[s], s)) for d in range(MICRO) for s in range(3)],
    )
    pair = jnp.concatenate([got_far, got_near], axis=0)
    one, two, three = hop(pair, 1, 0), hop(pair, 2, 0), hop(got_far, 3, 0)
    own = lax.dynamic_index_in_dim(images, row, 0)
    return jnp.concatenate([own, got_near, one[1:], two[1:], got_far, one[:1], two[:1], three], axis=0)


def by_micro_batch(images, image_counts, conv_weight, bn_gain, bn_bias, out_grad):
    section = lax.axis_index("section")
    row = lax.axis_index("dp")
    weight = conv_weight[0]
    slots = jnp.arange(MICRO, dtype=jnp.int32)

    def flags(on, extra=False):
        return jnp.stack([on, jnp.asarray(extra)]).astype(jnp.int32)

    valid = (slots < image_counts[0])[:, None, None, None]
    mine = exchange_images(jnp.where(valid, images, INF), row, section)
    fields = mine.reshape(8, 8, 2, 8, 640).transpose(2, 1, 0, 3, 4).reshape(2, 512, 640)
    h1, shortcut, ring, stats_0 = forward_first(flags(section == 0), fields, weight, bn_gain, bn_bias)
    h1_in, side_in = hop(h1, 0, 1), hop(shortcut, 0, 1)

    top = lax.all_to_all(after(out_grad, h1), "dp", 0, 0, tiled=True)[slots ^ row]
    top = top.transpose(1, 0, 2, 3).reshape(512, 640)
    top_grad, ring = backward_top(flags(section == 3), top, weight, ring)

    y1, stats_1, ring = forward_rest(
        flags(section == 1, True), h1_in, side_in, weight, bn_gain, bn_bias, ring
    )
    y1_in = hop(y1, 1, 2)
    h3, stats_2, ring = forward_rest(flags(section == 2), y1_in, y1_in, weight, bn_gain, bn_bias, ring)
    h3_in, y1_top = hop(h3, 2, 3), hop(y1_in, 2, 3)
    g_h3, sums_3, ring = turn(flags(section == 3), h3_in, top_grad, bn_gain, bn_bias, ring)
    g_h3_in = hop(g_h3, 3, 2)
    g_y1, sums_2, ring = backward_rest(
        flags(section == 2, True), g_h3_in, top, y1_in, stats_2, weight, bn_gain, bn_bias, ring
    )
    g_y1_in = hop(g_y1, 2, 1)
    g_h1, sums_1, ring = backward_rest(
        flags(section == 1), g_y1_in, top, h1_in, stats_1, weight, bn_gain, bn_bias, ring
    )
    g_h1_in, g_side = hop(g_h1, 1, 0), hop(g_y1_in, 1, 0)

    up, down = ring_pairs((0, 1, 2, 3))
    up_0, down_0 = ring_pairs((0,))
    blocks = [ring, move(ring, up), move(ring, down)]
    blocks += [move(blocks[1], up), move(blocks[2], down)]
    y2 = forward_last(flags(section == 3), ring, h3_in, y1_top, weight)
    rest = flags(section >= 1)
    grads = kernel_grad_rest(rest, blocks[:3])
    blocks += [move(blocks[3], up), move(blocks[4], down)]
    g_h1_in = after(g_h1_in, blocks[3], blocks[4])
    lasts = [g_h1_in, move(g_h1_in, up_0), move(g_h1_in, down_0)]
    blocks += [move(blocks[5], up)]
    input_fields, sums_0 = backward_first(
        flags(section == 0), g_h1_in, g_side, fields, stats_0, weight, bn_gain, bn_bias
    )
    grads = kernel_grad_rest(rest, blocks[3:5], grads)
    grads = kernel_grad_first(flags(section == 0), blocks[:3], lasts[:3], grads, True)
    lasts += [move(lasts[1], up_0), move(lasts[2], down_0)]
    grads = kernel_grad_rest(rest, blocks[5:8], grads)
    projected = dp_total(projection_grad(flags(section == 0), ring, g_side), (0,))
    sums = jnp.where(
        section == 0, sums_0, jnp.where(section == 1, sums_1, jnp.where(section == 2, sums_2, sums_3))
    )
    sums = dp_total(sums, (0, 1, 2, 3))
    grads = kernel_grad_first(flags(section == 0), blocks[3:5], lasts[3:5], grads, False)
    lasts += [move(lasts[3], up_0), move(lasts[4], down_0)]
    lasts += [move(lasts[5], up_0)]
    grads = kernel_grad_first(flags(section == 0), blocks[5:8], lasts[5:8], grads, False, projected)

    grad = input_fields.reshape(2, 4, 2, 8, 8, 640)
    quarter = grad[:, 0]
    for k in range(1, 4):
        quarter = jnp.where(section == k, hop(grad[:, k], 0, k), quarter)
    quarter = quarter.transpose(2, 1, 0, 3, 4)[slots ^ row]
    input_grad = lax.all_to_all(quarter, "dp", 0, 0, tiled=True).reshape(8, 4, 16, 320)
    out = jnp.where(section == 0, h1, jnp.where(section == 1, y1, jnp.where(section == 2, h3, y2)))
    out = jnp.where(out < INF, out, 0.0).reshape(8, 8, 8, 640).transpose(1, 0, 2, 3)
    section_outputs = lax.all_to_all(out[slots ^ row], "dp", 0, 0, tiled=True)[None]
    return (section_outputs, input_grad, grads[None], sums[None, 1], sums[None, 0])


def solution(mesh):
    one_each = mesh.shape["dp"] == MICRO and mesh.shape["section"] == 4

    def on_device(images, *rest):
        if one_each and images.shape == (MICRO, 16, 16, 320):
            return by_micro_batch(images, *rest)
        return pipelined(images, *rest)

    return jax.shard_map(
        on_device,
        mesh=mesh,
        in_specs=(
            P("dp", None, None, None),
            P("dp"),
            P("section", None, None),
            P("section", None),
            P("section", None),
            P("dp", None, None, None),
        ),
        out_specs=(
            P("section", "dp", None, None, None),
            P("dp", "section", None, None),
            P("section", None, None),
            P("section", None),
            P("section", None),
        ),
        check_vma=False,
    )
```

```python
import jax
import jax.numpy as jnp
from jax import lax
from jax.experimental import pallas as pl
from jax.experimental.pallas import tpu as pltpu
from jax.sharding import PartitionSpec as P

MICRO = 8


EPSILON = 1e-05


def for_sending(value):

    def short(part):
        return part.astype(jnp.bfloat16) if part.dtype == jnp.float32 else part

    return jax.tree.map(short, value)


def shifted(value, axis, steps):
    count = lax.axis_size(axis)
    initial, last = (max(0, -steps), min(count, count - steps))
    return lax.ppermute(value, axis, [(source, source + steps) for source in range(initial, last)])


def conv_forward(activation, kernel, stride):
    return lax.conv_general_dilated(
        activation,
        kernel,
        (stride, stride),
        ((1, 1), (1, 1)),
        dimension_numbers=("NHWC", "HWIO", "NHWC"),
        preferred_element_type=jnp.float32,
    )


def conv_input_grad(gradient, kernel, stride):
    upper = 1 if stride == 1 else 2
    return lax.conv_general_dilated(
        gradient,
        kernel[::-1, ::-1],
        (1, 1),
        ((1, upper), (1, upper)),
        lhs_dilation=(stride, stride),
        dimension_numbers=("NHWC", "HWOI", "NHWC"),
        preferred_element_type=jnp.float32,
    )


def conv_kernel_grad(activation, gradient, stride):
    upper = 1 if stride == 1 else 0
    return lax.conv_general_dilated(
        activation,
        gradient,
        (1, 1),
        ((1, upper), (1, upper)),
        rhs_dilation=(stride, stride),
        dimension_numbers=("CHWN", "IHWO", "HWNC"),
        preferred_element_type=jnp.float32,
    )


def channel_sum(values, image_mask):
    return jnp.sum(image_mask[:, None, None, None] * values, axis=(0, 1, 2))


def normalize(values, channel_mean, inv_std, norm_gain, norm_bias):
    scaled = (values - channel_mean) * inv_std
    return (scaled, scaled * norm_gain + norm_bias)


def norm_terms(grad_act, values, image_mask, channel_mean, inv_std, norm_gain, norm_bias):
    scaled, pre_act = normalize(values, channel_mean, inv_std, norm_gain, norm_bias)
    sigmoid_val = jax.nn.sigmoid(pre_act)
    grad_pre = (
        grad_act
        * image_mask[:, None, None, None]
        * sigmoid_val
        * (1.0 + pre_act * (1.0 - sigmoid_val))
    )
    return (grad_pre, scaled)


def pipelined(images, image_counts, conv_weight, bn_gain, bn_bias, out_grad):
    section_count = lax.axis_size("section")
    section_index = lax.axis_index("section")
    img_dev = images.shape[0]
    per_micro = img_dev // MICRO
    height = images.shape[1]
    side = height // 2
    c_in = images.shape[3]
    c_out = conv_weight.shape[2]
    kernel_rows = conv_weight.shape[1]
    is_first = section_index == 0
    is_last = section_index == section_count - 1
    adds_residual = section_index % 2 == 1
    merges_back = (section_index % 2 == 0) & (section_index > 0)
    valid_img = (jnp.arange(img_dev, dtype=jnp.int32) < image_counts[0]).astype(jnp.float32)
    valid_img = valid_img.reshape(per_micro, MICRO)
    image_groups = images.reshape(per_micro, MICRO, height, height, c_in)
    grad_groups = out_grad.reshape(per_micro, MICRO, side, side, c_out)
    kernel_all = conv_weight[0]
    kernel_first = kernel_all[: 9 * c_in].reshape(3, 3, c_in, c_out)
    kernel_proj = kernel_all[9 * c_in : 10 * c_in]
    kernel_rest = kernel_all.reshape(3, 3, c_out, c_out)
    norm_gain = bn_gain[0]
    norm_bias = bn_bias[0]
    tick_count = MICRO + section_count - 1
    pad_width = (0, c_out - c_in)

    def forward_first(raw_input, section_input, residual, image_mask, channel_mean, inv_std):
        scaled, pre_act = normalize(
            raw_input, channel_mean[:c_in], inv_std[:c_in], norm_gain[:c_in], norm_bias[:c_in]
        )
        activation = (jax.nn.silu(pre_act) * image_mask[:, None, None, None]).astype(jnp.bfloat16)
        conv_out = conv_forward(activation, kernel_first, 2)
        sub_grid = activation[:, 0::2, 0::2, :].reshape(-1, c_in)
        projected = jnp.dot(sub_grid, kernel_proj, preferred_element_type=jnp.float32)
        projected = projected.reshape(per_micro, side, side, c_out)
        return (conv_out.astype(jnp.bfloat16), projected.astype(jnp.bfloat16))

    def forward_rest(raw_input, section_input, residual, image_mask, channel_mean, inv_std):
        scaled, pre_act = normalize(section_input, channel_mean, inv_std, norm_gain, norm_bias)
        activation = (jax.nn.silu(pre_act) * image_mask[:, None, None, None]).astype(jnp.bfloat16)
        conv_out = conv_forward(activation, kernel_rest, 1)
        summed = conv_out + jnp.where(adds_residual, 1.0, 0.0) * residual.astype(jnp.float32)
        sent_main = summed.astype(jnp.bfloat16)
        return (sent_main, jnp.where(adds_residual, sent_main, residual))

    def forward_tick(step_index, state_carry):
        recv_main, recv_side, out_buf, in_buf, moment_buf, count_buf = state_carry
        micro_index = step_index - section_index
        active = (micro_index >= 0) & (micro_index < MICRO)
        slot_index = jnp.clip(micro_index, 0, MICRO - 1)
        image_mask = lax.dynamic_index_in_dim(valid_img, slot_index, 1, keepdims=False)
        raw_input = lax.dynamic_index_in_dim(image_groups, slot_index, 1, keepdims=False).astype(
            jnp.float32
        )
        section_input = recv_main.astype(jnp.float32)
        positions = jnp.where(is_first, float(height * height), float(side * side))
        local_count = jnp.sum(image_mask) * positions
        local_total = jnp.where(
            is_first,
            jnp.pad(channel_sum(raw_input, image_mask), pad_width),
            channel_sum(section_input, image_mask),
        )
        total_sum, count_sum = lax.psum((local_total, local_count), "dp")
        channel_mean = total_sum / count_sum
        first_dev = raw_input - channel_mean[:c_in]
        rest_dev = section_input - channel_mean
        local_spread = jnp.where(
            is_first,
            jnp.pad(channel_sum(first_dev * first_dev, image_mask), pad_width),
            channel_sum(rest_dev * rest_dev, image_mask),
        )
        spread_sum = lax.psum(local_spread, "dp")
        variance = spread_sum / count_sum
        inv_std = lax.rsqrt(variance + EPSILON)
        sent_main, sent_side = lax.cond(
            is_first,
            forward_first,
            forward_rest,
            raw_input,
            section_input,
            recv_side,
            image_mask,
            channel_mean,
            inv_std,
        )
        old_out = lax.dynamic_index_in_dim(out_buf, slot_index, 0, keepdims=False)
        out_buf = lax.dynamic_update_index_in_dim(
            out_buf, jnp.where(active, sent_main, old_out), slot_index, 0
        )
        old_in = lax.dynamic_index_in_dim(in_buf, slot_index, 0, keepdims=False)
        in_buf = lax.dynamic_update_index_in_dim(
            in_buf, jnp.where(active, recv_main, old_in), slot_index, 0
        )
        moments = jnp.stack([channel_mean, inv_std])
        old_moment = lax.dynamic_index_in_dim(moment_buf, slot_index, 0, keepdims=False)
        moment_buf = lax.dynamic_update_index_in_dim(
            moment_buf, jnp.where(active, moments, old_moment), slot_index, 0
        )
        old_count = lax.dynamic_index_in_dim(count_buf, slot_index, 0, keepdims=False)
        count_buf = lax.dynamic_update_index_in_dim(
            count_buf, jnp.where(active, count_sum, old_count), slot_index, 0
        )
        recv_main, recv_side = (
            shifted(for_sending(sent_main), "section", 1).astype(sent_main.dtype),
            shifted(for_sending(sent_side), "section", 1).astype(sent_side.dtype),
        )
        return (recv_main, recv_side, out_buf, in_buf, moment_buf, count_buf)

    act_zeros = jnp.zeros((per_micro, side, side, c_out), jnp.bfloat16)
    forward_init = (
        act_zeros,
        act_zeros,
        jnp.zeros((MICRO, per_micro, side, side, c_out), jnp.bfloat16),
        jnp.zeros((MICRO, per_micro, side, side, c_out), jnp.bfloat16),
        jnp.zeros((MICRO, 2, c_out), jnp.float32),
        jnp.ones((MICRO,), jnp.float32),
    )
    forward_done = lax.fori_loop(0, tick_count, forward_tick, forward_init)
    out_buf, in_buf, moment_buf, count_buf = (
        forward_done[2],
        forward_done[3],
        forward_done[4],
        forward_done[5],
    )

    def backward_first(
        raw_input, section_input, grad_conv, grad_side, image_mask, channel_mean, inv_std
    ):
        scaled, pre_act = normalize(
            raw_input, channel_mean[:c_in], inv_std[:c_in], norm_gain[:c_in], norm_bias[:c_in]
        )
        activation = (jax.nn.silu(pre_act) * image_mask[:, None, None, None]).astype(jnp.bfloat16)
        kernel_part = conv_kernel_grad(activation, grad_conv, 2).reshape(9 * c_in, c_out)
        sub_grid = activation[:, 0::2, 0::2, :].reshape(-1, c_in)
        side_flat = grad_side.reshape(-1, c_out)
        proj_part = lax.dot_general(
            sub_grid, side_flat, (((0,), (0,)), ((), ())), preferred_element_type=jnp.float32
        )
        weight_part = jnp.concatenate(
            [kernel_part, proj_part, jnp.zeros((kernel_rows - 10 * c_in, c_out), jnp.float32)],
            axis=0,
        )
        sub_grad = lax.dot_general(
            side_flat, kernel_proj, (((1,), (1,)), ((), ())), preferred_element_type=jnp.float32
        )
        sub_grad = sub_grad.reshape(per_micro, side, side, c_in)
        spread_grad = lax.pad(
            sub_grad, jnp.float32(0.0), ((0, 0, 0), (0, 1, 1), (0, 1, 1), (0, 0, 0))
        )
        grad_first = conv_input_grad(grad_conv, kernel_first, 2) + spread_grad
        return (weight_part, grad_first, jnp.zeros((per_micro, side, side, c_out), jnp.float32))

    def backward_rest(
        raw_input, section_input, grad_conv, grad_side, image_mask, channel_mean, inv_std
    ):
        scaled, pre_act = normalize(section_input, channel_mean, inv_std, norm_gain, norm_bias)
        activation = (jax.nn.silu(pre_act) * image_mask[:, None, None, None]).astype(jnp.bfloat16)
        weight_part = conv_kernel_grad(activation, grad_conv, 1).reshape(kernel_rows, c_out)
        grad_rest = conv_input_grad(grad_conv, kernel_rest, 1)
        return (weight_part, jnp.zeros((per_micro, height, height, c_in), jnp.float32), grad_rest)

    def backward_tick(step_index, state_carry):
        recv_main, recv_side, weight_acc, gain_acc, bias_acc, input_buf = state_carry
        micro_index = step_index - (section_count - 1 - section_index)
        active = (micro_index >= 0) & (micro_index < MICRO)
        slot_index = jnp.clip(micro_index, 0, MICRO - 1)
        image_mask = lax.dynamic_index_in_dim(valid_img, slot_index, 1, keepdims=False)
        raw_input = lax.dynamic_index_in_dim(image_groups, slot_index, 1, keepdims=False).astype(
            jnp.float32
        )
        section_input = lax.dynamic_index_in_dim(in_buf, slot_index, 0, keepdims=False).astype(
            jnp.float32
        )
        moments = lax.dynamic_index_in_dim(moment_buf, slot_index, 0, keepdims=False)
        channel_mean, inv_std = (moments[0], moments[1])
        count_sum = lax.dynamic_index_in_dim(count_buf, slot_index, 0, keepdims=False)
        top_grad = jnp.where(
            is_last, lax.dynamic_index_in_dim(grad_groups, slot_index, 1, keepdims=False), recv_main
        )
        joined = (top_grad.astype(jnp.float32) + recv_side.astype(jnp.float32)).astype(jnp.bfloat16)
        grad_conv = jnp.where(adds_residual, joined, top_grad)
        grad_side = jnp.where(adds_residual, joined, recv_side)
        weight_part, grad_first, grad_rest = lax.cond(
            is_first,
            backward_first,
            backward_rest,
            raw_input,
            section_input,
            grad_conv,
            grad_side,
            image_mask,
            channel_mean,
            inv_std,
        )
        pre_first, scaled_first = norm_terms(
            grad_first,
            raw_input,
            image_mask,
            channel_mean[:c_in],
            inv_std[:c_in],
            norm_gain[:c_in],
            norm_bias[:c_in],
        )
        pre_rest, scaled_rest = norm_terms(
            grad_rest, section_input, image_mask, channel_mean, inv_std, norm_gain, norm_bias
        )
        local_pre = jnp.where(
            is_first,
            jnp.pad(jnp.sum(pre_first, axis=(0, 1, 2)), pad_width),
            jnp.sum(pre_rest, axis=(0, 1, 2)),
        )
        local_cross = jnp.where(
            is_first,
            jnp.pad(jnp.sum(pre_first * scaled_first, axis=(0, 1, 2)), pad_width),
            jnp.sum(pre_rest * scaled_rest, axis=(0, 1, 2)),
        )
        sum_pre, sum_cross = lax.psum((local_pre, local_cross), "dp")
        mean_pre = sum_pre / count_sum
        mean_cross = sum_cross / count_sum
        mask_four = image_mask[:, None, None, None]
        grad_in_rest = (
            mask_four * inv_std * norm_gain * (pre_rest - mean_pre - scaled_rest * mean_cross)
        )
        grad_in_first = (
            mask_four
            * inv_std[:c_in]
            * norm_gain[:c_in]
            * (pre_first - mean_pre[:c_in] - scaled_first * mean_cross[:c_in])
        )
        sent_main = jnp.where(
            merges_back, grad_in_rest + grad_side.astype(jnp.float32), grad_in_rest
        ).astype(jnp.bfloat16)
        sent_side = jnp.where(merges_back, jnp.zeros_like(grad_side), grad_side)
        weight_acc = weight_acc + jnp.where(active, weight_part, 0.0)
        gain_acc = gain_acc + jnp.where(active, sum_cross, 0.0)
        bias_acc = bias_acc + jnp.where(active, sum_pre, 0.0)
        old_input = lax.dynamic_index_in_dim(input_buf, slot_index, 0, keepdims=False)
        input_buf = lax.dynamic_update_index_in_dim(
            input_buf, jnp.where(active, grad_in_first, old_input), slot_index, 0
        )
        recv_main, recv_side = shifted((sent_main, sent_side), "section", -1)
        return (recv_main, recv_side, weight_acc, gain_acc, bias_acc, input_buf)

    backward_init = (
        act_zeros,
        act_zeros,
        jnp.zeros((kernel_rows, c_out), jnp.float32),
        jnp.zeros((c_out,), jnp.float32),
        jnp.zeros((c_out,), jnp.float32),
        jnp.zeros((MICRO, per_micro, height, height, c_in), jnp.float32),
    )
    backward_done = lax.fori_loop(0, tick_count, backward_tick, backward_init)
    weight_acc, gain_acc, bias_acc, input_buf = (
        backward_done[2],
        backward_done[3],
        backward_done[4],
        backward_done[5],
    )
    weight_total = lax.psum(weight_acc, "dp")
    input_full = jnp.transpose(input_buf, (1, 0, 2, 3, 4)).reshape(img_dev, height, height, c_in)
    input_full = jnp.where(is_first, input_full, 0.0)
    input_grad = lax.psum_scatter(
        input_full.astype(jnp.bfloat16), "section", scatter_dimension=1, tiled=True
    )
    section_outputs = jnp.transpose(out_buf, (1, 0, 2, 3, 4)).reshape(img_dev, side, side, c_out)[
        None
    ]
    return (section_outputs, input_grad, weight_total[None], gain_acc[None], bias_acc[None])


BF = jnp.bfloat16
F32 = jnp.float32
INF = float("inf")
MIB = 1024 * 1024
ANY = pl.BlockSpec(memory_space=pltpu.HBM)
FREE = pl.BlockSpec(memory_space=pl.ANY)
INSIDE = pl.BlockSpec(memory_space=pltpu.VMEM)
KEPT = pl.BlockSpec(memory_space=pltpu.VMEM)
SCALARS = pl.BlockSpec(memory_space=pltpu.SMEM)
FIELD = jax.ShapeDtypeStruct((512, 640), BF)
TWO = jax.ShapeDtypeStruct((2, 512, 640), BF)
PAIR = jax.ShapeDtypeStruct((2, 640), F32)
SUMS = jax.ShapeDtypeStruct((1920, 1920), F32)


def lane(k, first=0):
    return pl.ds(pl.multiple_of(first + 128 * k, 128), 128)


def from_left(values):
    column = lax.broadcasted_iota(jnp.int32, values.shape, 0) & 7
    return jnp.where(column == 0, 0.0, pltpu.roll(values, 1, 0))


def from_right(values):
    column = lax.broadcasted_iota(jnp.int32, values.shape, 0) & 7
    return jnp.where(column == 7, 0.0, pltpu.roll(values, values.shape[0] - 1, 0))


def total_of(values):
    return jnp.sum(values, axis=0, keepdims=True)


def count_of(valid):
    return total_of(jnp.where(valid, 1.0, 0.0))


def sigmoid(z):
    return 0.5 * jnp.tanh(0.5 * z) + 0.5


def matmul(a, b):
    return jnp.dot(a, b, preferred_element_type=F32)


def matmul_bt(a, b):
    return lax.dot_general(a, b, (((1,), (1,)), ((), ())), preferred_element_type=F32)


def matmul_at(a, b):
    return lax.dot_general(a, b, (((0,), (0,)), ((), ())), preferred_element_type=F32)


def start_all(copies):
    for one in copies:
        one.start()


def wait_all(copies):
    for one in copies:
        one.wait()


PINNED = {id(ANY): pltpu.HBM, id(KEPT): pltpu.VMEM}


def kernel_call(kernel, out_shape, in_specs, out_specs, scratch, aliases=None, flops=0, mib=18):
    outs = out_shape if isinstance(out_shape, tuple) else (out_shape,)
    specs = out_specs if isinstance(out_specs, tuple) else (out_specs,)
    outs = tuple(
        PINNED[id(spec)](one.shape, one.dtype) if id(spec) in PINNED else one for spec, one in zip(specs, outs)
    )
    call = pl.pallas_call(
        kernel,
        out_shape=outs,
        in_specs=in_specs,
        out_specs=specs,
        scratch_shapes=scratch,
        input_output_aliases=aliases or {},
        compiler_params=pltpu.CompilerParams(vmem_limit_bytes=mib * MIB),
        cost_estimate=pl.CostEstimate(flops=int(flops * 1.0), bytes_accessed=0, transcendentals=0),
    )

    def run(*args):
        args = [
            pltpu.with_memory_space_constraint(one, PINNED[id(spec)]) if id(spec) in PINNED else one
            for spec, one in zip(in_specs, args)
        ]
        results = call(*args)
        return results if isinstance(out_shape, tuple) else results[0]

    return run


def half_turn(values):
    return jnp.concatenate([values[:, 320:640], values[:, 0:320]], axis=1)


def twice(values):
    return jnp.concatenate([values[:, 0:320], values[:, 0:320]], axis=1)


def weight_first(w_ref, w_vm, sems):
    copies = []
    for p in range(3):
        copies.append(
            pltpu.make_async_copy(
                w_ref.at[pl.ds(960 * p + 320, 640)], w_vm.at[pl.ds(1024 * p, 640)], sems.at[2 * p]
            )
        )
        copies.append(
            pltpu.make_async_copy(
                w_ref.at[pl.ds(960 * p, 320)], w_vm.at[pl.ds(1024 * p + 704, 320)], sems.at[2 * p + 1]
            )
        )
        w_vm[1024 * p + 640 : 1024 * p + 704, :] = jnp.zeros((64, 640), BF)
    copies.append(pltpu.make_async_copy(w_ref.at[pl.ds(2880, 320)], w_vm.at[pl.ds(3072, 320)], sems.at[6]))
    w_vm[3392:3456, :] = jnp.zeros((64, 640), BF)
    return copies


def forward_first_kernel(
    flags, own, one, two, three, four, others, w_ref, gain, bias, out_ref, side_ref, ring_ref, field_ref, stats_ref,
    w_vm, x_vm, cat, acc, part, sems, x_sems,
):
    @pl.when(flags[0] == 1)
    def _():
        pieces = [ref.at[0] for ref in (own, one, two, three, four)] + [others.at[k] for k in range(3)]
        in_x = []
        for k, piece in enumerate(pieces):
            slot = flags[1] ^ k
            for a in range(2):
                in_x.append(
                    pltpu.make_async_copy(piece.at[:, a], x_vm.at[a, :, slot], x_sems.at[2 * k + a])
                )
        start_all(in_x)
        in_w = weight_first(w_ref, w_vm, sems)
        start_all(in_w)
        cat[0:64, :] = jnp.zeros((64, 1024), BF)
        part[4:5, :] = twice(gain)
        part[5:6, :] = twice(bias)
        wait_all(in_x)

        @pl.loop(0, 5)
        def _(k):
            here = lane(k)
            x = x_vm[0, :, :, :, here].astype(F32).reshape(512, 128)
            y = x_vm[1, :, :, :, here].astype(F32).reshape(512, 128)
            field_ref[0, :, here] = x.astype(BF)
            field_ref[1, :, here] = y.astype(BF)
            valid = x < INF
            part[0:1, here] = total_of(jnp.where(valid, x + y, 0.0))
            part[2:3, here] = 4.0 * count_of(valid)

        part[0:1, :] = (part[0:1, :] + half_turn(part[0:1, :])) / part[2:3, :]

        @pl.loop(0, 5)
        def _(k):
            here = lane(k)
            x, y = field_ref[0, :, here].astype(F32), field_ref[1, :, here].astype(F32)
            valid = x < INF
            x = x - part[0:1, here]
            y = y - part[0:1, here]
            part[1:2, here] = total_of(jnp.where(valid, x * x + y * y, 0.0))

        part[1:2, :] = lax.rsqrt((part[1:2, :] + half_turn(part[1:2, :])) / part[2:3, :] + EPSILON)
        stats_ref[...] = part[0:2, :]

        @pl.loop(0, 5)
        def _(k):
            here = lane(k)
            for a in range(2):
                x = field_ref[a, :, here].astype(F32)
                z = (x - part[0:1, here]) * part[1:2, here] * part[4:5, here] + part[5:6, here]
                act = jnp.where(x < INF, z * sigmoid(z), 0.0)
                first = 576 if a == 0 else 64
                cat[first : first + 512, here] = act.astype(BF)

                @pl.when(k >= 2)
                def _():
                    cat[first : first + 512, lane(k, 384)] = from_left(act).astype(BF)

        keep = [
            pltpu.make_async_copy(cat.at[pl.ds(576, 512), pl.ds(0, 640)], ring_ref.at[0], x_sems.at[0]),
            pltpu.make_async_copy(cat.at[pl.ds(64, 512), pl.ds(0, 640)], ring_ref.at[1], x_sems.at[1]),
        ]
        start_all(keep)
        acc[...] = jnp.zeros((512, 640), F32)
        wait_all(in_w)

        @pl.loop(0, 3)
        def _(p):
            first = pl.multiple_of(jnp.where(p == 1, 576, 32 * p), 64)
            acc[...] += matmul(cat[pl.ds(first, 512), :], w_vm[pl.ds(pl.multiple_of(1024 * p, 1024), 1024), :])

        @pl.loop(0, 5)
        def _(k):
            row_valid = field_ref[0, :, 0:128].astype(F32) < INF
            out_ref[:, lane(k)] = jnp.where(row_valid, acc[:, lane(k)], INF).astype(BF)

        side_ref[...] = matmul(cat[576:1088, 0:384], w_vm[3072:3456, :]).astype(BF)
        wait_all(keep)


def forward_first(flags, pieces, weight, gain, bias):
    return kernel_call(
        forward_first_kernel,
        (FIELD, FIELD, TWO, TWO, PAIR),
        [SCALARS] + [FREE] * 6 + [ANY, INSIDE, INSIDE],
        (INSIDE, INSIDE, ANY, INSIDE, INSIDE),
        [
            pltpu.VMEM((3456, 640), BF),
            pltpu.VMEM((2, 8, 8, 8, 640), BF),
            pltpu.VMEM((1088, 1024), BF),
            pltpu.VMEM((512, 640), F32),
            pltpu.VMEM((8, 640), F32),
            pltpu.SemaphoreType.DMA((7,)),
            pltpu.SemaphoreType.DMA((16,)),
        ],
        flops=4_000_000_000,
    )(flags, *pieces, weight, gain, bias)


def weight_part(w_ref, w_vm, sems, p):
    rows = pl.ds(pl.multiple_of(1920 * p, 1920), 1920)
    return pltpu.make_async_copy(w_ref.at[rows], w_vm.at[rows], sems.at[p])


def clear_edges(x3):
    x3[0:64, :] = jnp.zeros((64, x3.shape[1]), BF)
    x3[576:640, :] = jnp.zeros((64, x3.shape[1]), BF)


def place(x3, k, values, left, right):
    x3[64:576, lane(k, left)] = from_left(values).astype(BF)
    x3[64:576, lane(k, 640)] = values.astype(BF)
    x3[64:576, lane(k, right)] = from_right(values).astype(BF)


def forward_conv(x3, w_ref, w_vm, w_sems, acc):
    @pl.loop(0, 3)
    def _(p):
        weight_part(w_ref, w_vm, w_sems, p).wait()
        acc[...] += matmul(
            x3[pl.ds(pl.multiple_of(64 * p, 64), 512), :], w_vm[pl.ds(pl.multiple_of(1920 * p, 1920), 1920), :]
        )


def statistics(x):
    valid = x < INF
    count = count_of(valid)
    mean = total_of(jnp.where(valid, x, 0.0)) / count
    centred = jnp.where(valid, x - mean, 0.0)
    inv = lax.rsqrt(total_of(centred * centred) / count + EPSILON)
    return valid, count, mean, inv, centred


def forward_rest_kernel(
    handed, flags, h, res, w_ref, gain, bias, out_ref, stats_ref, act_ref, w_vm, x3, acc, w_sems
):
    @pl.when(flags[0] == 1)
    def _():
        for p in range(3):
            weight_part(w_ref, w_vm, w_sems, p).start()
        clear_edges(x3)

        @pl.loop(0, 5)
        def _(k):
            here = lane(k)
            valid, _, mean, inv, centred = statistics(h[:, here].astype(F32))
            stats_ref[0:1, here] = mean
            stats_ref[1:2, here] = inv
            z = centred * inv * gain[:, here] + bias[:, here]
            act = jnp.where(valid, z * sigmoid(z), 0.0)
            act_ref[:, here] = act.astype(BF)
            place(x3, k, act, 0, 1280)
            acc[:, here] = jnp.zeros((512, 128), F32) if handed else res[:, here].astype(F32)

        forward_conv(x3, w_ref, w_vm, w_sems, acc)

        @pl.loop(0, 5)
        def _(k):
            here = lane(k)
            row_valid = h[:, 0:128].astype(F32) < INF
            out = jnp.where(row_valid, acc[:, here], INF).astype(BF)
            if handed:
                out_ref[0, :, here] = out
                out_ref[1, :, here] = h[:, here]
            else:
                out_ref[:, here] = out


def forward_rest(flags, h, res, weight, gain, bias, handed=False):
    return kernel_call(
        lambda *refs: forward_rest_kernel(handed, *refs),
        (TWO if handed else FIELD, PAIR, FIELD),
        [SCALARS, INSIDE, INSIDE, ANY, INSIDE, INSIDE],
        (INSIDE, INSIDE, INSIDE),
        [
            pltpu.VMEM((5760, 640), BF),
            pltpu.VMEM((640, 1920), BF),
            pltpu.VMEM((512, 640), F32),
            pltpu.SemaphoreType.DMA((3,)),
        ],
        flops=4_000_000_000,
    )(flags, h, res, weight, gain, bias)


def forward_last_kernel(flags, act, pair, w_ref, out_ref, w_vm, x3, acc, w_sems):
    @pl.when(flags[0] == 1)
    def _():
        for p in range(3):
            weight_part(w_ref, w_vm, w_sems, p).start()
        clear_edges(x3)

        @pl.loop(0, 5)
        def _(k):
            place(x3, k, act[:, lane(k)].astype(F32), 0, 1280)
            acc[:, lane(k)] = pair[1, :, lane(k)].astype(F32)

        forward_conv(x3, w_ref, w_vm, w_sems, acc)

        @pl.loop(0, 5)
        def _(k):
            row_valid = pair[0, :, 0:128].astype(F32) < INF
            out_ref[:, lane(k)] = jnp.where(row_valid, acc[:, lane(k)], INF).astype(BF)


def forward_last(flags, act, pair, weight):
    return kernel_call(
        forward_last_kernel,
        FIELD,
        [SCALARS, INSIDE, INSIDE, ANY],
        INSIDE,
        [
            pltpu.VMEM((5760, 640), BF),
            pltpu.VMEM((640, 1920), BF),
            pltpu.VMEM((512, 640), F32),
            pltpu.SemaphoreType.DMA((3,)),
        ],
        flops=4_000_000_000,
    )(flags, act, pair, weight)


def by_row(values):
    return values.transpose(1, 0, 2, 3).reshape(512, values.shape[3])


def backward_conv(g3, w_ref, w_vm, w_sems, acc):
    @pl.loop(0, 3)
    def _(p):
        weight_part(w_ref, w_vm, w_sems, p).wait()

        @pl.loop(0, 3)
        def _(q):
            acc[...] += matmul_bt(
                g3[pl.ds(pl.multiple_of(64 * (2 - p), 64), 512), pl.ds(pl.multiple_of(640 * q, 640), 640)],
                w_vm[pl.ds(pl.multiple_of(640 * (3 * p + q), 640), 640), :],
            )


def backward_conv_turned(g3, w_ref, w_vm, w_sems, acc):
    @pl.loop(0, 3)
    def _(p):
        weight_part(w_ref, w_vm, w_sems, p).wait()
        acc[...] += matmul(
            g3[pl.ds(pl.multiple_of(64 * (2 - p), 64), 512), :],
            w_vm[pl.ds(pl.multiple_of(1920 * p, 1920), 1920), :],
        )


def backward_top_kernel(flags, g_ref, w_ref, total_ref, own_ref, w_vm, g3, w_sems):
    for p in range(3):
        weight_part(w_ref, w_vm, w_sems, p).start()
    clear_edges(g3)

    @pl.loop(0, 5)
    def _(k):
        here = lane(k)
        g = by_row(g_ref[:, :, :, here].astype(F32))
        own_ref[:, here] = g.astype(BF)
        place(g3, k, g, 1280, 0)
        total_ref[:, here] = jnp.zeros((512, 128), F32)

    backward_conv(g3, w_ref, w_vm, w_sems, total_ref)


def backward_top(flags, g, weight):
    return kernel_call(
        backward_top_kernel,
        (jax.ShapeDtypeStruct((512, 640), F32), FIELD),
        [SCALARS, INSIDE, ANY],
        (INSIDE, INSIDE),
        [
            pltpu.VMEM((5760, 640), BF),
            pltpu.VMEM((640, 1920), BF),
            pltpu.SemaphoreType.DMA((3,)),
        ],
        flops=4_000_000_000,
    )(flags, g, weight)


def norm_back(grad, valid, count, centred, inv, scale, offset, sums_ref, here):
    xhat = centred * inv
    z = xhat * scale + offset
    sig = sigmoid(z)
    dz = jnp.where(valid, grad * sig * (1.0 + z * (1.0 - sig)), 0.0)
    s1 = total_of(dz)
    s2 = total_of(dz * xhat)
    sums_ref[0:1, here] = s1
    sums_ref[1:2, here] = s2
    back = scale * inv * (dz - s1 / count - xhat * (s2 / count))
    return jnp.where(valid, back, 0.0), jnp.where(valid, z * sig, 0.0)


def turn_kernel(flags, pair, grad, gain, bias, out_ref, sums_ref, act_ref):
    @pl.when(flags[0] == 1)
    def _():
        @pl.loop(0, 5)
        def _(k):
            here = lane(k)
            valid, count, _, inv, centred = statistics(pair[0, :, here].astype(F32))
            back, act = norm_back(
                grad[:, here], valid, count, centred, inv, gain[:, here], bias[:, here], sums_ref, here
            )
            act_ref[:, here] = act.astype(BF)
            out_ref[:, here] = back.astype(BF)


def turn(flags, h, grad, gain, bias):
    return kernel_call(
        turn_kernel,
        (FIELD, PAIR, FIELD),
        [SCALARS] + [INSIDE] * 4,
        (INSIDE, INSIDE, INSIDE),
        [],
        flops=1_000_000_000,
    )(flags, h, grad, gain, bias)


def backward_rest_kernel(
    handed, flags, g_ref, add, h, stats, w_ref, gain, bias, out_ref, sums_ref, w_vm, g3, acc, w_sems
):
    @pl.when(flags[0] == 1)
    def _():
        for p in range(3):
            weight_part(w_ref, w_vm, w_sems, p).start()
        clear_edges(g3)

        @pl.loop(0, 5)
        def _(k):
            place(g3, k, g_ref[:, lane(k)].astype(F32), 1280, 0)
            acc[:, lane(k)] = jnp.zeros((512, 128), F32)

        backward_conv_turned(g3, w_ref, w_vm, w_sems, acc)
        @pl.loop(0, 5)
        def _(k):
            here = lane(k)
            x = h[:, here].astype(F32)
            valid = x < INF
            centred = jnp.where(valid, x - stats[0:1, here], 0.0)
            back, _ = norm_back(
                acc[:, here], valid, count_of(valid), centred, stats[1:2, here], gain[:, here], bias[:, here],
                sums_ref, here,
            )
            if handed:
                out_ref[0, :, here] = back.astype(BF)
                out_ref[1, :, here] = g_ref[:, here]
            else:
                out_ref[:, here] = (back + by_row(add[:, :, :, here].astype(F32))).astype(BF)


def backward_rest(flags, g, add, h, stats, weight, gain, bias, handed=False):
    return kernel_call(
        lambda *refs: backward_rest_kernel(handed, *refs),
        (TWO if handed else FIELD, PAIR),
        [SCALARS, INSIDE, INSIDE, INSIDE, INSIDE, ANY, INSIDE, INSIDE],
        (INSIDE, INSIDE),
        [
            pltpu.VMEM((5760, 640), BF),
            pltpu.VMEM((640, 1920), BF),
            pltpu.VMEM((512, 640), F32),
            pltpu.SemaphoreType.DMA((3,)),
        ],
        flops=4_000_000_000,
    )(flags, g, add, h, stats, weight, gain, bias)


def backward_first_conv_kernel(flags, pair, w_ref, acc, w_vm, g2, sems):
    in_w = weight_first(w_ref, w_vm, sems)
    start_all(in_w)
    g2[512:576, :] = jnp.zeros((64, 1280), BF)

    @pl.loop(0, 5)
    def _(k):
        g = pair[0, :, lane(k)].astype(F32)
        g2[0:512, lane(k)] = g.astype(BF)
        g2[0:512, lane(k, 640)] = from_right(g).astype(BF)

    acc[...] = jnp.zeros((2, 512, 640), F32)
    wait_all(in_w)

    @pl.loop(0, 3)
    def _(p):
        rows = pl.ds(pl.multiple_of(jnp.where(p == 0, 64, 0), 64), 512)
        a = jnp.where(p == 1, 0, 1)
        first = pl.multiple_of(1024 * p, 1024)
        acc[a] += matmul_bt(g2[rows, 0:640], w_vm[pl.ds(first, 640), :])
        acc[a, :, 256:640] += matmul_bt(g2[rows, 640:1280], w_vm[pl.ds(first + 640, 384), :])

    acc[0, :, 0:384] += matmul_bt(pair[1], w_vm[3072:3456, :])


def backward_first_conv(flags, pair, weight):
    return kernel_call(
        backward_first_conv_kernel,
        jax.ShapeDtypeStruct((2, 512, 640), F32),
        [SCALARS, INSIDE, ANY],
        INSIDE,
        [
            pltpu.VMEM((3456, 640), BF),
            pltpu.VMEM((576, 1280), BF),
            pltpu.SemaphoreType.DMA((7,)),
        ],
        flops=5_000_000_000,
    )(flags, pair, weight)


def backward_first_norm_kernel(flags, acc, x_ref, stats, gain, bias, out_ref, sums_ref, dz_vm, part):
    part[4:5, :] = twice(gain)
    part[5:6, :] = twice(bias)

    @pl.loop(0, 5)
    def _(k):
        here = lane(k)
        s1 = s2 = 0.0
        for a in range(2):
            x = x_ref[a, :, here].astype(F32)
            valid = x < INF
            xhat = jnp.where(valid, x - stats[0:1, here], 0.0) * stats[1:2, here]
            z = xhat * part[4:5, here] + part[5:6, here]
            sig = sigmoid(z)
            dz = jnp.where(valid, acc[a, :, here] * sig * (1.0 + z * (1.0 - sig)), 0.0)
            dz_vm[a, :, here] = dz
            s1 = s1 + total_of(dz)
            s2 = s2 + total_of(dz * xhat)
        part[0:1, here] = s1
        part[1:2, here] = s2
        part[2:3, here] = 4.0 * count_of(valid)

    part[0:1, :] = part[0:1, :] + half_turn(part[0:1, :])
    part[1:2, :] = part[1:2, :] + half_turn(part[1:2, :])
    sums_ref[...] = jnp.where(lax.broadcasted_iota(jnp.int32, (2, 640), 1) < 320, part[0:2, :], 0.0)

    @pl.loop(0, 5)
    def _(k):
        here = lane(k)
        count = part[2:3, here]
        scale = part[4:5, here] * stats[1:2, here]
        for a in range(2):
            x = x_ref[a, :, here].astype(F32)
            xhat = (x - stats[0:1, here]) * stats[1:2, here]
            back = scale * (dz_vm[a, :, here] - part[0:1, here] / count - xhat * (part[1:2, here] / count))
            back = jnp.where(x < INF, back, 0.0).reshape(4, 2, 8, 8, 128).transpose(2, 0, 1, 3, 4)
            out_ref[:, :, :, a, :, here] = back.astype(BF)


def backward_first_norm(flags, field, x, stats, gain, bias):
    return kernel_call(
        backward_first_norm_kernel,
        (jax.ShapeDtypeStruct((8, 4, 2, 2, 8, 640), BF), PAIR),
        [SCALARS, INSIDE, INSIDE, INSIDE, INSIDE, INSIDE],
        (INSIDE, INSIDE),
        [pltpu.VMEM((2, 512, 640), F32), pltpu.VMEM((8, 640), F32)],
        flops=1_000_000_000,
    )(flags, field, x, stats, gain, bias)


def send_sides(side, rows, sent_ref):
    sent_ref[0:320, :] = side.astype(BF)
    for k in range(3):
        piece = rows.astype(BF)
        sent_ref[320 + 2 * k : 322 + 2 * k, :] = piece
        rows = rows - piece.astype(F32)
    sent_ref[326:336, :] = jnp.zeros((10, 640), BF)


def projection_grad_kernel(flags, ring_ref, pair_ref, rows, out_ref, rows_ref, sent_ref, a_vm, g_vm, sems):
    ins = [
        pltpu.make_async_copy(ring_ref.at[0], a_vm, sems.at[0]),
        pltpu.make_async_copy(pair_ref.at[1], g_vm, sems.at[1]),
    ]
    start_all(ins)
    wait_all(ins)
    side = matmul_at(a_vm[:, 0:384], g_vm[...])[0:320, :]
    out_ref[...] = side
    rows_ref[...] = rows[...]
    send_sides(side, rows[...], sent_ref)


SIDES = (jax.ShapeDtypeStruct((320, 640), F32), PAIR, jax.ShapeDtypeStruct((336, 640), BF))


def projection_grad(flags, ring, pair, rows):
    return kernel_call(
        projection_grad_kernel,
        SIDES,
        [SCALARS, FREE, FREE, INSIDE],
        (INSIDE, INSIDE, INSIDE),
        [pltpu.VMEM((512, 640), BF), pltpu.VMEM((512, 640), BF), pltpu.SemaphoreType.DMA((2,))],
        flops=200_000_000,
        mib=8,
    )(flags, ring, pair, rows)


def add_sides_kernel(side, rows, got, out_ref, rows_ref, sent_ref):
    side = side[...] + got[0:320, :].astype(F32)
    rows = rows[...]
    for k in range(3):
        rows = rows + got[320 + 2 * k : 322 + 2 * k, :].astype(F32)
    out_ref[...] = side
    rows_ref[...] = rows
    send_sides(side, rows, sent_ref)


def add_sides(side, rows, got):
    return kernel_call(
        add_sides_kernel, SIDES, [INSIDE, INSIDE, INSIDE], (INSIDE, INSIDE, INSIDE), [], mib=8
    )(side, rows, got)


def ring_value_kernel(g, sums, out_ref):
    out_ref[0:512, :] = g[...]
    rows = sums[...]
    pieces = []
    for _ in range(3):
        pieces.append(rows.astype(BF).astype(F32))
        rows = rows - pieces[-1]
    out_ref[512:528, :] = jnp.concatenate([*pieces, jnp.zeros((10, 640), F32)], axis=0).astype(BF)


def ring_value(g, sums):
    return kernel_call(
        ring_value_kernel, jax.ShapeDtypeStruct((528, 640), BF), [INSIDE, INSIDE], INSIDE, [], mib=8
    )(g, sums)


def add_rows_kernel(first, *refs):
    blocks, out_ref, rows, sems = refs[:8], refs[8], refs[9], refs[10]
    copies = [
        pltpu.make_async_copy(blocks[b].at[pl.ds(first, 16)], rows.at[b], sems.at[b]) for b in range(8)
    ]
    start_all(copies)
    wait_all(copies)
    total = rows[0].astype(F32)
    for b in range(1, 8):
        total = total + rows[b].astype(F32)
    out_ref[...] = total[0:2, :] + total[2:4, :] + total[4:6, :]


def add_rows(blocks, first):
    return kernel_call(
        lambda *refs: add_rows_kernel(first, *refs),
        PAIR,
        [FREE] * 8,
        INSIDE,
        [pltpu.VMEM((8, 16, 640), BF), pltpu.SemaphoreType.DMA((8,))],
        mib=8,
    )(*blocks)


def kernel_grads_kernel(blocks, fresh, last, *refs):
    acts, gs = refs[:blocks], refs[blocks : 2 * blocks]
    refs = refs[2 * blocks :]
    gs = [one.at[pl.ds(512 if one.shape[0] == 1040 else 0, 512)] for one in gs]
    acts = [one.at[pl.ds(0, 512)] for one in acts]
    if not fresh:
        kept, refs = refs[0], refs[1:]
    sums, a_vm, g_vm, g3, sems = refs[0], *refs[-4:]
    if last:
        out_ref, out_sems = refs[0], refs[1]
        sums = kept
    ins = []
    for b in range(blocks):
        ins.append(pltpu.make_async_copy(gs[b], g_vm.at[b], sems.at[b, 0]))
        ins.append(pltpu.make_async_copy(acts[b], a_vm.at[b], sems.at[b, 1]))
    start_all(ins)

    @pl.loop(0, blocks)
    def _(b):
        clear_edges(g3.at[b])

    wait_all(ins)

    @pl.loop(0, blocks)
    def _(b):
        @pl.loop(0, 5)
        def _(k):
            place(g3.at[b], k, g_vm[b, :, lane(k)].astype(F32), 1280, 0)

    def outs(p):
        rows = pl.ds(pl.multiple_of(640 * p, 640), 640)
        return [
            pltpu.make_async_copy(
                sums.at[rows, pl.ds(640 * q, 640)],
                out_ref.at[pl.ds(pl.multiple_of(640 * (3 * p + q), 640), 640)],
                out_sems.at[p, q],
            )
            for q in range(3)
        ]

    @pl.loop(0, 3)
    def _(p):
        rows = pl.ds(pl.multiple_of(640 * p, 640), 640)
        here = pl.ds(pl.multiple_of(64 * (2 - p), 64), 512)
        if fresh:
            sums[rows, :] = jnp.zeros((640, 1920), F32)
        elif not last:
            sums[rows, :] = kept[rows, :]

        @pl.loop(0, blocks)
        def _(b):
            sums[rows, :] += matmul_at(a_vm[b], g3[b, here, :])

        if last:
            start_all(outs(p))

    if last:
        for p in range(3):
            wait_all(outs(p))


def kernel_grads_first_kernel(blocks, fresh, last, *refs):
    acts, gs = refs[:blocks], refs[blocks : 2 * blocks]
    refs = refs[2 * blocks :]
    if last:
        side, refs = refs[0], refs[1:]
    if not fresh:
        kept, refs = refs[0], refs[1:]
    sums, a_vm, g_vm, g2, sems = refs[0], *refs[-4:]
    extra = []
    if last:
        out_ref, zeros, out_sems, extra_sems = refs[:4]
        sums = kept
    ins = []
    for b in range(blocks):
        ins.append(pltpu.make_async_copy(gs[b].at[pl.ds(0, 512)], g_vm.at[b], sems.at[b, 0]))
        ins.append(pltpu.make_async_copy(acts[b], a_vm.at[b], sems.at[b, 1]))
    start_all(ins)
    if last:
        zeros[...] = jnp.zeros((320, 640), F32)
        extra.append(pltpu.make_async_copy(side, out_ref.at[pl.ds(2880, 320)], extra_sems.at[0]))
        for k in range(8):
            extra.append(pltpu.make_async_copy(zeros, out_ref.at[pl.ds(3200 + 320 * k, 320)], extra_sems.at[1 + k]))
        start_all(extra)
    wait_all(ins)

    @pl.loop(0, blocks)
    def _(b):
        g2[b, 512:576, :] = jnp.zeros((64, 1280), BF)

        @pl.loop(0, 5)
        def _(k):
            g = g_vm[b, :, lane(k)].astype(F32)
            g2[b, 0:512, lane(k)] = g.astype(BF)
            g2[b, 0:512, lane(k, 640)] = from_right(g).astype(BF)

    def outs(p):
        low = pl.multiple_of(640 * p, 640)
        return [
            pltpu.make_async_copy(
                sums.at[pl.ds(low, 640), pl.ds(0, 640)],
                out_ref.at[pl.ds(pl.multiple_of(960 * p + 320, 320), 640)],
                out_sems.at[p, 0],
            ),
            pltpu.make_async_copy(
                sums.at[pl.ds(low, 320), pl.ds(640, 640)],
                out_ref.at[pl.ds(pl.multiple_of(960 * p, 320), 320)],
                out_sems.at[p, 1],
            ),
        ]

    @pl.loop(0, 3)
    def _(p):
        here = pl.ds(pl.multiple_of(jnp.where(p == 0, 64, 0), 64), 512)
        low = pl.multiple_of(640 * p, 640)
        odd = jnp.where(p == 1, 0, 1)
        if fresh:
            sums[pl.ds(low, 640), :] = jnp.zeros((640, 1280), F32)
        elif not last:
            sums[pl.ds(low, 640), :] = kept[pl.ds(low, 640), :]

        @pl.loop(0, blocks)
        def _(b):
            sums[pl.ds(low, 640), 0:640] += matmul_at(a_vm[b, odd], g2[b, here, 0:640])
            left = matmul_at(a_vm[b, odd, :, 256:640], g2[b, here, 640:1280])
            sums[pl.ds(low, 320), 640:1280] += left[64:384, :]

        if last:
            start_all(outs(p))

    if last:
        for p in range(3):
            wait_all(outs(p))
    wait_all(extra)


def kernel_grads(acts, gs, kept=None, last=False, first=False, side=None):
    blocks = len(acts)
    fresh = kept is None
    scratch = []
    if last and first:
        scratch += [pltpu.VMEM((320, 640), F32)]
    if last:
        scratch += [pltpu.SemaphoreType.DMA((3, 3))]
    if last and first:
        scratch += [pltpu.SemaphoreType.DMA((9,))]
    scratch += [
        pltpu.VMEM((blocks, 2, 512, 640) if first else (blocks, 512, 640), BF),
        pltpu.VMEM((blocks, 512, 640), BF),
        pltpu.VMEM((blocks, 576, 1280) if first else (blocks, 640, 1920), BF),
        pltpu.SemaphoreType.DMA((blocks, 2)),
    ]
    extra = [side] if last and first else []
    count = 2 * blocks + len(extra)
    kernel = kernel_grads_first_kernel if first else kernel_grads_kernel
    sums = jax.ShapeDtypeStruct((1920, 1280 if first else 1920), F32)
    return kernel_call(
        lambda *refs: kernel(blocks, fresh, last, *refs),
        jax.ShapeDtypeStruct((5760, 640), F32) if last else sums,
        [FREE] * count + ([] if fresh else [KEPT]),
        ANY if last else KEPT,
        scratch,
        aliases={} if fresh or last else {count: 0},
        flops=4_000_000_000 * blocks,
        mib=20,
    )(*acts, *gs, *extra, *([] if fresh else [kept]))


def empty(shapes):
    return pl.pallas_call(
        lambda *refs: None,
        out_shape=tuple(shapes),
        out_specs=tuple(ANY for _ in shapes),
    )()


BOTH = ("dp", "section")
RING = (0, 2, 4, 6, 7, 5, 3, 1)


def move(value, triples):
    count = lax.axis_size("section")
    return lax.ppermute(value, BOTH, [(d * count + s, e * count + t) for (d, s), (e, t) in triples])


def hop(value, source, target):
    return move(value, [((d, source), (d, target)) for d in range(MICRO)])


class Ring:
    def __init__(self, value, sections):
        self.up = [((RING[k], s), (RING[(k + 1) % 8], s)) for k in range(8) for s in sections]
        self.down = [(b, a) for a, b in self.up]
        self.blocks = [value]

    def step(self):
        count = len(self.blocks)
        high = self.blocks[max(0, count - 2)]
        low = self.blocks[count - 1]
        self.blocks.append(move(high, self.up))
        if count < 7:
            self.blocks.append(move(low, self.down))


def dp_total(value, sections):
    for k in (1, 2, 4):
        value = value + move(value, [((d, s), (d ^ k, s)) for d in range(MICRO) for s in sections])
    return value


def after(value, *others):
    return lax.optimization_barrier((value, *others))[0]


def pick(images, image_count, index):
    image = lax.dynamic_index_in_dim(images, index, 0)
    return jnp.where(index < image_count, image, INF).reshape(1, 8, 2, 8, 640)


def exchange_images(images, image_count, row, section, offsets):
    return [
        move(pick(images, image_count, row ^ k), [((d, section), (d ^ k, section)) for d in range(MICRO)])
        for k in offsets
    ]


SLOTS = jax.ShapeDtypeStruct((8, 8, 8, 640), BF)
PARTS = jax.ShapeDtypeStruct((4, 8, 2, 2, 8, 640), BF)


SLOTS = jax.ShapeDtypeStruct((8, 8, 8, 640), BF)
PARTS = jax.ShapeDtypeStruct((8, 4, 2, 2, 8, 640), BF)


def by_micro_batch(images, image_counts, conv_weight, bn_gain, bn_bias, out_grad):
    section = lax.axis_index("section")
    row = lax.axis_index("dp")
    weight = conv_weight[0]
    norm = (bn_gain, bn_bias)
    plain, adds = jnp.array([1, 0], jnp.int32), jnp.array([1, 1], jnp.int32)

    def segment(shapes, *branches):
        def whole(branch):
            def run():
                found = branch()
                missing = [name for name in shapes if name not in found]
                if missing:
                    found.update(zip(missing, empty([shapes[name] for name in missing])))
                return [found[name] for name in shapes]

            return run

        return dict(zip(shapes, lax.switch(section, [whole(branch) for branch in branches])))

    def on_section(first, second, third, fourth):
        return jnp.where(
            section == 0, first, jnp.where(section == 1, second, jnp.where(section == 2, third, fourth))
        )

    def nothing():
        return {}

    def named(prefix, blocks):
        return {f"{prefix}{k}": one for k, one in enumerate(blocks)}

    def listed(found, prefix, count):
        return [found[f"{prefix}{k}"] for k in range(count)]

    def many(prefix, count, shape):
        return {f"{prefix}{k}": shape for k in range(count)}

    def exchange(value):
        return lax.all_to_all(value, "dp", 0, 0, tiled=True)

    def resume(value, blocks, index):
        ring = Ring(value, (index,))
        ring.blocks += blocks
        return ring

    def shown(value):
        return jnp.where(value < INF, value, 0.0).reshape(8, 8, 8, 640).transpose(1, 0, 2, 3)

    count = image_counts[0]
    piece = jax.ShapeDtypeStruct((1, 8, 2, 8, 640), BF)
    grad_shape = jax.ShapeDtypeStruct((512, 640), F32)

    def zero_0():
        got = exchange_images(images, count, row, 0, (4, 3, 2, 1))
        return {"p1": got[3], "p2": got[2], "p3": got[1], "p4": got[0]}

    def zero_1():
        return {"others": jnp.concatenate(exchange_images(images, count, row, 1, (5, 6, 7)), axis=0)}

    def zero_2():
        return {"top": exchange(out_grad)}

    def zero_3():
        grad, own = backward_top(plain, exchange(out_grad), weight)
        return {"grad": grad, "own": own}

    zeroth = segment(
        {
            **{f"p{k}": piece for k in range(1, 5)}, "others": jax.ShapeDtypeStruct((3, 8, 2, 8, 640), BF),
            "top": SLOTS, "grad": grad_shape, "own": FIELD,
        },
        zero_0, zero_1, zero_2, zero_3,
    )
    others = hop(zeroth["others"], 1, 0)

    def one_0():
        pieces = (pick(images, count, row), *[zeroth[f"p{k}"] for k in range(1, 5)], others)
        h1, side, ring, fields, stats = forward_first(
            jnp.stack([jnp.int32(1), row.astype(jnp.int32)]), pieces, weight, *norm
        )
        return {"h1": h1, "side": side, "ring": ring, "fields": fields, "stats": stats}

    def turned():
        return {"weight": weight.reshape(9, 640, 640).transpose(0, 2, 1).reshape(5760, 640)}

    first = segment(
        {"weight": jax.ShapeDtypeStruct((5760, 640), BF), "h1": FIELD, "side": FIELD, "ring": TWO, "fields": TWO, "stats": PAIR},
        one_0, turned, turned, nothing,
    )
    h1_in, side_in = hop(first["h1"], 0, 1), hop(first["side"], 0, 1)

    def two_1():
        y1, stats, act = forward_rest(adds, h1_in, side_in, weight, *norm)
        return {"y1": y1, "stats": stats, "act": act}

    second = segment(
        {"y1": FIELD, "act": FIELD, "stats": PAIR}, nothing, two_1, nothing, nothing
    )
    y1_in = hop(second["y1"], 1, 2)

    def three_2():
        pair, stats, act = forward_rest(plain, y1_in, y1_in, weight, *norm, handed=True)
        return {"pair": pair, "stats": stats, "act": act}

    third = segment({"pair": TWO, "act": FIELD, "stats": PAIR}, nothing, nothing, three_2, nothing)
    h3_in = hop(third["pair"], 2, 3)

    def four_3():
        g_h3, sums, act = turn(plain, h3_in, zeroth["grad"], *norm)
        return {"g": g_h3, "sums": sums, "act": act}

    fourth = segment({"g": FIELD, "act": FIELD, "sums": PAIR}, nothing, nothing, nothing, four_3)
    g_h3_in = hop(fourth["g"], 3, 2)

    def five_2():
        g_y1, sums = backward_rest(adds, g_h3_in, zeroth["top"], y1_in, third["stats"], first["weight"], *norm)
        return {"g": g_y1, "sums": sums}

    fifth = segment({"g": FIELD, "sums": PAIR}, nothing, nothing, five_2, nothing)
    g_y1_in = hop(fifth["g"], 2, 1)

    def two_steps(value, index, shows):
        value = after(value, fifth["g"])
        out = exchange(shown(shows(value)))
        ring = Ring(value, (index,))
        ring.step()
        ring.step()
        return {"out": out, **named("u", ring.blocks)}

    wait_5 = segment(
        {"out": SLOTS, **many("u", 5, FIELD)},
        nothing,
        lambda: two_steps(second["act"], 1, lambda _: second["y1"]),
        lambda: two_steps(third["act"], 2, lambda _: third["pair"][0]),
        lambda: two_steps(fourth["act"], 3, lambda act: forward_last(plain, act, h3_in, weight)),
    )
    g_y1_in = after(g_y1_in, wait_5["u0"])

    def six_0():
        ring = Ring(first["ring"], (0,))
        ring.step()
        ring.step()
        return named("a", ring.blocks)

    def six_1():
        pair, sums = backward_rest(
            plain, g_y1_in, zeroth["top"], h1_in, second["stats"], first["weight"], *norm, handed=True
        )
        return {"pair": pair, "sums": sums}

    sixth = segment(
        {"pair": TWO, "sums": PAIR, **many("a", 5, TWO)}, six_0, six_1, nothing, nothing
    )
    pair_sent = hop(sixth["pair"], 1, 0)

    def seven_0():
        ring = Ring(after(sixth["a0"], sixth["pair"]), (0,))
        ring.blocks = listed(sixth, "a", 5)
        ring.blocks[3] = after(ring.blocks[3], sixth["pair"])
        ring.step()
        return {"out": shown(first["h1"]), **named("a", ring.blocks[5:])}

    def seven_1():
        return {"g": ring_value(after(g_y1_in, sixth["pair"]), sixth["sums"])}

    def seven_2():
        return {"g": ring_value(g_h3_in, fifth["sums"])}

    def seven_3():
        return {"g": ring_value(zeroth["own"], fourth["sums"])}

    tall = jax.ShapeDtypeStruct((528, 640), BF)
    seventh = segment({"g": tall, "out": SLOTS, **many("a", 2, TWO)}, seven_0, seven_1, seven_2, seven_3)

    pair_in = after(pair_sent, seventh["g"])

    def work(ring, late):
        gs, acts = ring.blocks, late.blocks
        total = None
        for low, high in ((0, 3), (3, 5), (5, 7)):
            ring.step()
            if low >= 3:
                late.step()
            total = kernel_grads(acts[low:high], gs[low:high], total)
            if low < 5:
                gs[high : high + 2], acts[high:], total = lax.optimization_barrier(
                    (gs[high : high + 2], acts[high:], total)
                )
        return kernel_grads(acts[7:8], gs[7:8], total, True)

    def eight_0():
        fence = lax.optimization_barrier
        ring = Ring(pair_in[0], (0,))
        ring.step()
        field = backward_first_conv(plain, pair_in, weight)
        parts, sums = backward_first_norm(plain, field, first["fields"], first["stats"], *norm)
        side, rows, sent = projection_grad(plain, first["ring"], pair_in, sums)

        def to(k):
            return move(sent, [((d, 0), (d ^ k, 0)) for d in range(MICRO)])

        got = to(1)
        parts, out = exchange(after(parts, sent)), exchange(after(seventh["out"], sent))
        gs = ring.blocks
        late = Ring(sixth["a0"], (0,))
        late.blocks = acts = listed(sixth, "a", 5) + listed(seventh, "a", 2)
        got, gs[1:3] = fence((got, gs[1:3]))
        ring.step()
        side, rows, sent = add_sides(side, rows, got)
        got = to(2)
        acts[0] = after(acts[0], side)
        total = kernel_grads(acts[0:3], gs[0:3], first=True)
        gs[3:5], acts[3:], got, total = fence((gs[3:5], acts[3:], got, total))
        ring.step()
        late.step()
        side, rows, sent = add_sides(side, rows, got)
        got = to(4)
        acts[3] = after(acts[3], side)
        total = kernel_grads(acts[3:5], gs[3:5], total, first=True)
        gs[5:7], total = fence((gs[5:7], total))
        ring.step()
        total = kernel_grads(acts[5:7], gs[5:7], total, first=True)
        got, total = fence((got, total))
        side, rows, _ = add_sides(side, rows, got)
        total = kernel_grads(acts[7:8], gs[7:8], total, True, True, side)
        parts, out, total = fence((parts, out, total))
        return [parts, total, rows, out]

    def eight_rest():
        gs = Ring(seventh["g"], (1, 2, 3))
        gs.step()
        acts = Ring(wait_5["u0"], (1, 2, 3))
        acts.blocks = listed(wait_5, "u", 5)
        total = work(gs, acts)
        return [*empty([PARTS]), total, add_rows(gs.blocks, 512), *empty([SLOTS])]

    parts, grads, sums, out = lax.cond(section > 0, eight_rest, eight_0)

    mine = parts[:, 0]
    for k in range(1, 4):
        mine = jnp.where(section == k, hop(parts[:, k], 0, k), mine)
    out = jnp.where(section == 0, out, wait_5["out"])
    return (out[None], mine.reshape(8, 4, 16, 320), grads[None], sums[1:2], sums[0:1])


def solution(mesh):
    one_each = mesh.shape["dp"] == MICRO and mesh.shape["section"] == 4

    def on_device(images, *rest):
        if one_each and images.shape == (MICRO, 16, 16, 320):
            return by_micro_batch(images, *rest)
        return pipelined(images, *rest)

    return jax.shard_map(
        on_device,
        mesh=mesh,
        in_specs=(
            P("dp", None, None, None),
            P("dp"),
            P("section", None, None),
            P("section", None),
            P("section", None),
            P("dp", None, None, None),
        ),
        out_specs=(
            P("section", "dp", None, None, None),
            P("dp", "section", None, None),
            P("section", None, None),
            P("section", None),
            P("section", None),
        ),
        check_vma=False,
    )
```

```python
import jax
import jax.numpy as jnp
from jax import lax
from jax.experimental import pallas as pl
from jax.experimental.pallas import tpu as pltpu
from jax.sharding import PartitionSpec as P

MICRO = 8


EPSILON = 1e-05


def for_sending(value):

    def short(part):
        return part.astype(jnp.bfloat16) if part.dtype == jnp.float32 else part

    return jax.tree.map(short, value)


def shifted(value, axis, steps):
    count = lax.axis_size(axis)
    initial, last = (max(0, -steps), min(count, count - steps))
    return lax.ppermute(value, axis, [(source, source + steps) for source in range(initial, last)])


def conv_forward(activation, kernel, stride):
    return lax.conv_general_dilated(
        activation,
        kernel,
        (stride, stride),
        ((1, 1), (1, 1)),
        dimension_numbers=("NHWC", "HWIO", "NHWC"),
        preferred_element_type=jnp.float32,
    )


def conv_input_grad(gradient, kernel, stride):
    upper = 1 if stride == 1 else 2
    return lax.conv_general_dilated(
        gradient,
        kernel[::-1, ::-1],
        (1, 1),
        ((1, upper), (1, upper)),
        lhs_dilation=(stride, stride),
        dimension_numbers=("NHWC", "HWOI", "NHWC"),
        preferred_element_type=jnp.float32,
    )


def conv_kernel_grad(activation, gradient, stride):
    upper = 1 if stride == 1 else 0
    return lax.conv_general_dilated(
        activation,
        gradient,
        (1, 1),
        ((1, upper), (1, upper)),
        rhs_dilation=(stride, stride),
        dimension_numbers=("CHWN", "IHWO", "HWNC"),
        preferred_element_type=jnp.float32,
    )


def channel_sum(values, image_mask):
    return jnp.sum(image_mask[:, None, None, None] * values, axis=(0, 1, 2))


def normalize(values, channel_mean, inv_std, norm_gain, norm_bias):
    scaled = (values - channel_mean) * inv_std
    return (scaled, scaled * norm_gain + norm_bias)


def norm_terms(grad_act, values, image_mask, channel_mean, inv_std, norm_gain, norm_bias):
    scaled, pre_act = normalize(values, channel_mean, inv_std, norm_gain, norm_bias)
    sigmoid_val = jax.nn.sigmoid(pre_act)
    grad_pre = (
        grad_act
        * image_mask[:, None, None, None]
        * sigmoid_val
        * (1.0 + pre_act * (1.0 - sigmoid_val))
    )
    return (grad_pre, scaled)


def pipelined(images, image_counts, conv_weight, bn_gain, bn_bias, out_grad):
    section_count = lax.axis_size("section")
    section_index = lax.axis_index("section")
    img_dev = images.shape[0]
    per_micro = img_dev // MICRO
    height = images.shape[1]
    side = height // 2
    c_in = images.shape[3]
    c_out = conv_weight.shape[2]
    kernel_rows = conv_weight.shape[1]
    is_first = section_index == 0
    is_last = section_index == section_count - 1
    adds_residual = section_index % 2 == 1
    merges_back = (section_index % 2 == 0) & (section_index > 0)
    valid_img = (jnp.arange(img_dev, dtype=jnp.int32) < image_counts[0]).astype(jnp.float32)
    valid_img = valid_img.reshape(per_micro, MICRO)
    image_groups = images.reshape(per_micro, MICRO, height, height, c_in)
    grad_groups = out_grad.reshape(per_micro, MICRO, side, side, c_out)
    kernel_all = conv_weight[0]
    kernel_first = kernel_all[: 9 * c_in].reshape(3, 3, c_in, c_out)
    kernel_proj = kernel_all[9 * c_in : 10 * c_in]
    kernel_rest = kernel_all.reshape(3, 3, c_out, c_out)
    norm_gain = bn_gain[0]
    norm_bias = bn_bias[0]
    tick_count = MICRO + section_count - 1
    pad_width = (0, c_out - c_in)

    def forward_first(raw_input, section_input, residual, image_mask, channel_mean, inv_std):
        scaled, pre_act = normalize(
            raw_input, channel_mean[:c_in], inv_std[:c_in], norm_gain[:c_in], norm_bias[:c_in]
        )
        activation = (jax.nn.silu(pre_act) * image_mask[:, None, None, None]).astype(jnp.bfloat16)
        conv_out = conv_forward(activation, kernel_first, 2)
        sub_grid = activation[:, 0::2, 0::2, :].reshape(-1, c_in)
        projected = jnp.dot(sub_grid, kernel_proj, preferred_element_type=jnp.float32)
        projected = projected.reshape(per_micro, side, side, c_out)
        return (conv_out.astype(jnp.bfloat16), projected.astype(jnp.bfloat16))

    def forward_rest(raw_input, section_input, residual, image_mask, channel_mean, inv_std):
        scaled, pre_act = normalize(section_input, channel_mean, inv_std, norm_gain, norm_bias)
        activation = (jax.nn.silu(pre_act) * image_mask[:, None, None, None]).astype(jnp.bfloat16)
        conv_out = conv_forward(activation, kernel_rest, 1)
        summed = conv_out + jnp.where(adds_residual, 1.0, 0.0) * residual.astype(jnp.float32)
        sent_main = summed.astype(jnp.bfloat16)
        return (sent_main, jnp.where(adds_residual, sent_main, residual))

    def forward_tick(step_index, state_carry):
        recv_main, recv_side, out_buf, in_buf, moment_buf, count_buf = state_carry
        micro_index = step_index - section_index
        active = (micro_index >= 0) & (micro_index < MICRO)
        slot_index = jnp.clip(micro_index, 0, MICRO - 1)
        image_mask = lax.dynamic_index_in_dim(valid_img, slot_index, 1, keepdims=False)
        raw_input = lax.dynamic_index_in_dim(image_groups, slot_index, 1, keepdims=False).astype(
            jnp.float32
        )
        section_input = recv_main.astype(jnp.float32)
        positions = jnp.where(is_first, float(height * height), float(side * side))
        local_count = jnp.sum(image_mask) * positions
        local_total = jnp.where(
            is_first,
            jnp.pad(channel_sum(raw_input, image_mask), pad_width),
            channel_sum(section_input, image_mask),
        )
        total_sum, count_sum = lax.psum((local_total, local_count), "dp")
        channel_mean = total_sum / count_sum
        first_dev = raw_input - channel_mean[:c_in]
        rest_dev = section_input - channel_mean
        local_spread = jnp.where(
            is_first,
            jnp.pad(channel_sum(first_dev * first_dev, image_mask), pad_width),
            channel_sum(rest_dev * rest_dev, image_mask),
        )
        spread_sum = lax.psum(local_spread, "dp")
        variance = spread_sum / count_sum
        inv_std = lax.rsqrt(variance + EPSILON)
        sent_main, sent_side = lax.cond(
            is_first,
            forward_first,
            forward_rest,
            raw_input,
            section_input,
            recv_side,
            image_mask,
            channel_mean,
            inv_std,
        )
        old_out = lax.dynamic_index_in_dim(out_buf, slot_index, 0, keepdims=False)
        out_buf = lax.dynamic_update_index_in_dim(
            out_buf, jnp.where(active, sent_main, old_out), slot_index, 0
        )
        old_in = lax.dynamic_index_in_dim(in_buf, slot_index, 0, keepdims=False)
        in_buf = lax.dynamic_update_index_in_dim(
            in_buf, jnp.where(active, recv_main, old_in), slot_index, 0
        )
        moments = jnp.stack([channel_mean, inv_std])
        old_moment = lax.dynamic_index_in_dim(moment_buf, slot_index, 0, keepdims=False)
        moment_buf = lax.dynamic_update_index_in_dim(
            moment_buf, jnp.where(active, moments, old_moment), slot_index, 0
        )
        old_count = lax.dynamic_index_in_dim(count_buf, slot_index, 0, keepdims=False)
        count_buf = lax.dynamic_update_index_in_dim(
            count_buf, jnp.where(active, count_sum, old_count), slot_index, 0
        )
        recv_main, recv_side = (
            shifted(for_sending(sent_main), "section", 1).astype(sent_main.dtype),
            shifted(for_sending(sent_side), "section", 1).astype(sent_side.dtype),
        )
        return (recv_main, recv_side, out_buf, in_buf, moment_buf, count_buf)

    act_zeros = jnp.zeros((per_micro, side, side, c_out), jnp.bfloat16)
    forward_init = (
        act_zeros,
        act_zeros,
        jnp.zeros((MICRO, per_micro, side, side, c_out), jnp.bfloat16),
        jnp.zeros((MICRO, per_micro, side, side, c_out), jnp.bfloat16),
        jnp.zeros((MICRO, 2, c_out), jnp.float32),
        jnp.ones((MICRO,), jnp.float32),
    )
    forward_done = lax.fori_loop(0, tick_count, forward_tick, forward_init)
    out_buf, in_buf, moment_buf, count_buf = (
        forward_done[2],
        forward_done[3],
        forward_done[4],
        forward_done[5],
    )

    def backward_first(
        raw_input, section_input, grad_conv, grad_side, image_mask, channel_mean, inv_std
    ):
        scaled, pre_act = normalize(
            raw_input, channel_mean[:c_in], inv_std[:c_in], norm_gain[:c_in], norm_bias[:c_in]
        )
        activation = (jax.nn.silu(pre_act) * image_mask[:, None, None, None]).astype(jnp.bfloat16)
        kernel_part = conv_kernel_grad(activation, grad_conv, 2).reshape(9 * c_in, c_out)
        sub_grid = activation[:, 0::2, 0::2, :].reshape(-1, c_in)
        side_flat = grad_side.reshape(-1, c_out)
        proj_part = lax.dot_general(
            sub_grid, side_flat, (((0,), (0,)), ((), ())), preferred_element_type=jnp.float32
        )
        weight_part = jnp.concatenate(
            [kernel_part, proj_part, jnp.zeros((kernel_rows - 10 * c_in, c_out), jnp.float32)],
            axis=0,
        )
        sub_grad = lax.dot_general(
            side_flat, kernel_proj, (((1,), (1,)), ((), ())), preferred_element_type=jnp.float32
        )
        sub_grad = sub_grad.reshape(per_micro, side, side, c_in)
        spread_grad = lax.pad(
            sub_grad, jnp.float32(0.0), ((0, 0, 0), (0, 1, 1), (0, 1, 1), (0, 0, 0))
        )
        grad_first = conv_input_grad(grad_conv, kernel_first, 2) + spread_grad
        return (weight_part, grad_first, jnp.zeros((per_micro, side, side, c_out), jnp.float32))

    def backward_rest(
        raw_input, section_input, grad_conv, grad_side, image_mask, channel_mean, inv_std
    ):
        scaled, pre_act = normalize(section_input, channel_mean, inv_std, norm_gain, norm_bias)
        activation = (jax.nn.silu(pre_act) * image_mask[:, None, None, None]).astype(jnp.bfloat16)
        weight_part = conv_kernel_grad(activation, grad_conv, 1).reshape(kernel_rows, c_out)
        grad_rest = conv_input_grad(grad_conv, kernel_rest, 1)
        return (weight_part, jnp.zeros((per_micro, height, height, c_in), jnp.float32), grad_rest)

    def backward_tick(step_index, state_carry):
        recv_main, recv_side, weight_acc, gain_acc, bias_acc, input_buf = state_carry
        micro_index = step_index - (section_count - 1 - section_index)
        active = (micro_index >= 0) & (micro_index < MICRO)
        slot_index = jnp.clip(micro_index, 0, MICRO - 1)
        image_mask = lax.dynamic_index_in_dim(valid_img, slot_index, 1, keepdims=False)
        raw_input = lax.dynamic_index_in_dim(image_groups, slot_index, 1, keepdims=False).astype(
            jnp.float32
        )
        section_input = lax.dynamic_index_in_dim(in_buf, slot_index, 0, keepdims=False).astype(
            jnp.float32
        )
        moments = lax.dynamic_index_in_dim(moment_buf, slot_index, 0, keepdims=False)
        channel_mean, inv_std = (moments[0], moments[1])
        count_sum = lax.dynamic_index_in_dim(count_buf, slot_index, 0, keepdims=False)
        top_grad = jnp.where(
            is_last, lax.dynamic_index_in_dim(grad_groups, slot_index, 1, keepdims=False), recv_main
        )
        joined = (top_grad.astype(jnp.float32) + recv_side.astype(jnp.float32)).astype(jnp.bfloat16)
        grad_conv = jnp.where(adds_residual, joined, top_grad)
        grad_side = jnp.where(adds_residual, joined, recv_side)
        weight_part, grad_first, grad_rest = lax.cond(
            is_first,
            backward_first,
            backward_rest,
            raw_input,
            section_input,
            grad_conv,
            grad_side,
            image_mask,
            channel_mean,
            inv_std,
        )
        pre_first, scaled_first = norm_terms(
            grad_first,
            raw_input,
            image_mask,
            channel_mean[:c_in],
            inv_std[:c_in],
            norm_gain[:c_in],
            norm_bias[:c_in],
        )
        pre_rest, scaled_rest = norm_terms(
            grad_rest, section_input, image_mask, channel_mean, inv_std, norm_gain, norm_bias
        )
        local_pre = jnp.where(
            is_first,
            jnp.pad(jnp.sum(pre_first, axis=(0, 1, 2)), pad_width),
            jnp.sum(pre_rest, axis=(0, 1, 2)),
        )
        local_cross = jnp.where(
            is_first,
            jnp.pad(jnp.sum(pre_first * scaled_first, axis=(0, 1, 2)), pad_width),
            jnp.sum(pre_rest * scaled_rest, axis=(0, 1, 2)),
        )
        sum_pre, sum_cross = lax.psum((local_pre, local_cross), "dp")
        mean_pre = sum_pre / count_sum
        mean_cross = sum_cross / count_sum
        mask_four = image_mask[:, None, None, None]
        grad_in_rest = (
            mask_four * inv_std * norm_gain * (pre_rest - mean_pre - scaled_rest * mean_cross)
        )
        grad_in_first = (
            mask_four
            * inv_std[:c_in]
            * norm_gain[:c_in]
            * (pre_first - mean_pre[:c_in] - scaled_first * mean_cross[:c_in])
        )
        sent_main = jnp.where(
            merges_back, grad_in_rest + grad_side.astype(jnp.float32), grad_in_rest
        ).astype(jnp.bfloat16)
        sent_side = jnp.where(merges_back, jnp.zeros_like(grad_side), grad_side)
        weight_acc = weight_acc + jnp.where(active, weight_part, 0.0)
        gain_acc = gain_acc + jnp.where(active, sum_cross, 0.0)
        bias_acc = bias_acc + jnp.where(active, sum_pre, 0.0)
        old_input = lax.dynamic_index_in_dim(input_buf, slot_index, 0, keepdims=False)
        input_buf = lax.dynamic_update_index_in_dim(
            input_buf, jnp.where(active, grad_in_first, old_input), slot_index, 0
        )
        recv_main, recv_side = shifted((sent_main, sent_side), "section", -1)
        return (recv_main, recv_side, weight_acc, gain_acc, bias_acc, input_buf)

    backward_init = (
        act_zeros,
        act_zeros,
        jnp.zeros((kernel_rows, c_out), jnp.float32),
        jnp.zeros((c_out,), jnp.float32),
        jnp.zeros((c_out,), jnp.float32),
        jnp.zeros((MICRO, per_micro, height, height, c_in), jnp.float32),
    )
    backward_done = lax.fori_loop(0, tick_count, backward_tick, backward_init)
    weight_acc, gain_acc, bias_acc, input_buf = (
        backward_done[2],
        backward_done[3],
        backward_done[4],
        backward_done[5],
    )
    weight_total = lax.psum(weight_acc, "dp")
    input_full = jnp.transpose(input_buf, (1, 0, 2, 3, 4)).reshape(img_dev, height, height, c_in)
    input_full = jnp.where(is_first, input_full, 0.0)
    input_grad = lax.psum_scatter(
        input_full.astype(jnp.bfloat16), "section", scatter_dimension=1, tiled=True
    )
    section_outputs = jnp.transpose(out_buf, (1, 0, 2, 3, 4)).reshape(img_dev, side, side, c_out)[
        None
    ]
    return (section_outputs, input_grad, weight_total[None], gain_acc[None], bias_acc[None])


BF = jnp.bfloat16
F32 = jnp.float32
INF = float("inf")
MIB = 1024 * 1024
ANY = pl.BlockSpec(memory_space=pltpu.HBM)
FREE = pl.BlockSpec(memory_space=pl.ANY)
INSIDE = pl.BlockSpec(memory_space=pltpu.VMEM)
KEPT = pl.BlockSpec(memory_space=pltpu.VMEM)
SCALARS = pl.BlockSpec(memory_space=pltpu.SMEM)
FIELD = jax.ShapeDtypeStruct((512, 640), BF)
TWO = jax.ShapeDtypeStruct((2, 512, 640), BF)
PAIR = jax.ShapeDtypeStruct((2, 640), F32)
SUMS = jax.ShapeDtypeStruct((1920, 1920), F32)


def lane(k, first=0):
    return pl.ds(pl.multiple_of(first + 128 * k, 128), 128)


def from_left(values):
    column = lax.broadcasted_iota(jnp.int32, values.shape, 0) & 7
    return jnp.where(column == 0, 0.0, pltpu.roll(values, 1, 0))


def from_right(values):
    column = lax.broadcasted_iota(jnp.int32, values.shape, 0) & 7
    return jnp.where(column == 7, 0.0, pltpu.roll(values, values.shape[0] - 1, 0))


def total_of(values):
    return jnp.sum(values, axis=0, keepdims=True)


def count_of(valid):
    return total_of(jnp.where(valid, 1.0, 0.0))


def sigmoid(z):
    return 0.5 * jnp.tanh(0.5 * z) + 0.5


def matmul(a, b):
    return jnp.dot(a, b, preferred_element_type=F32)


def matmul_bt(a, b):
    return lax.dot_general(a, b, (((1,), (1,)), ((), ())), preferred_element_type=F32)


def matmul_at(a, b):
    return lax.dot_general(a, b, (((0,), (0,)), ((), ())), preferred_element_type=F32)


def start_all(copies):
    for one in copies:
        one.start()


def wait_all(copies):
    for one in copies:
        one.wait()


PINNED = {id(ANY): pltpu.HBM, id(KEPT): pltpu.VMEM}


def kernel_call(kernel, out_shape, in_specs, out_specs, scratch, aliases=None, flops=0, mib=18):
    outs = out_shape if isinstance(out_shape, tuple) else (out_shape,)
    specs = out_specs if isinstance(out_specs, tuple) else (out_specs,)
    outs = tuple(
        PINNED[id(spec)](one.shape, one.dtype) if id(spec) in PINNED else one for spec, one in zip(specs, outs)
    )
    call = pl.pallas_call(
        kernel,
        out_shape=outs,
        in_specs=in_specs,
        out_specs=specs,
        scratch_shapes=scratch,
        input_output_aliases=aliases or {},
        compiler_params=pltpu.CompilerParams(vmem_limit_bytes=mib * MIB),
        cost_estimate=pl.CostEstimate(flops=int(flops * 1.0), bytes_accessed=0, transcendentals=0),
    )

    def run(*args):
        args = [
            pltpu.with_memory_space_constraint(one, PINNED[id(spec)]) if id(spec) in PINNED else one
            for spec, one in zip(in_specs, args)
        ]
        results = call(*args)
        return results if isinstance(out_shape, tuple) else results[0]

    return run


def half_turn(values):
    return jnp.concatenate([values[:, 320:640], values[:, 0:320]], axis=1)


def twice(values):
    return jnp.concatenate([values[:, 0:320], values[:, 0:320]], axis=1)


def weight_first(w_ref, w_vm, sems):
    copies = []
    for p in range(3):
        copies.append(
            pltpu.make_async_copy(
                w_ref.at[pl.ds(960 * p + 320, 640)], w_vm.at[pl.ds(1024 * p, 640)], sems.at[2 * p]
            )
        )
        copies.append(
            pltpu.make_async_copy(
                w_ref.at[pl.ds(960 * p, 320)], w_vm.at[pl.ds(1024 * p + 704, 320)], sems.at[2 * p + 1]
            )
        )
        w_vm[1024 * p + 640 : 1024 * p + 704, :] = jnp.zeros((64, 640), BF)
    copies.append(pltpu.make_async_copy(w_ref.at[pl.ds(2880, 320)], w_vm.at[pl.ds(3072, 320)], sems.at[6]))
    w_vm[3392:3456, :] = jnp.zeros((64, 640), BF)
    return copies


def forward_first_kernel(
    flags, own, one, two, three, four, others, w_ref, gain, bias, out_ref, side_ref, ring_ref, field_ref, stats_ref,
    w_vm, x_vm, cat, acc, part, sems, x_sems,
):
    @pl.when(flags[0] == 1)
    def _():
        pieces = [ref.at[0] for ref in (own, one, two, three, four)] + [others.at[k] for k in range(3)]
        in_x = []
        for k, piece in enumerate(pieces):
            slot = flags[1] ^ k
            for a in range(2):
                in_x.append(
                    pltpu.make_async_copy(piece.at[:, a], x_vm.at[a, :, slot], x_sems.at[2 * k + a])
                )
        start_all(in_x)
        in_w = weight_first(w_ref, w_vm, sems)
        start_all(in_w)
        cat[0:64, :] = jnp.zeros((64, 1024), BF)
        part[4:5, :] = twice(gain)
        part[5:6, :] = twice(bias)
        wait_all(in_x)

        @pl.loop(0, 5)
        def _(k):
            here = lane(k)
            x = x_vm[0, :, :, :, here].astype(F32).reshape(512, 128)
            y = x_vm[1, :, :, :, here].astype(F32).reshape(512, 128)
            field_ref[0, :, here] = x.astype(BF)
            field_ref[1, :, here] = y.astype(BF)
            valid = x < INF
            part[0:1, here] = total_of(jnp.where(valid, x + y, 0.0))
            part[2:3, here] = 4.0 * count_of(valid)

        part[0:1, :] = (part[0:1, :] + half_turn(part[0:1, :])) / part[2:3, :]

        @pl.loop(0, 5)
        def _(k):
            here = lane(k)
            x, y = field_ref[0, :, here].astype(F32), field_ref[1, :, here].astype(F32)
            valid = x < INF
            x = x - part[0:1, here]
            y = y - part[0:1, here]
            part[1:2, here] = total_of(jnp.where(valid, x * x + y * y, 0.0))

        part[1:2, :] = lax.rsqrt((part[1:2, :] + half_turn(part[1:2, :])) / part[2:3, :] + EPSILON)
        stats_ref[...] = part[0:2, :]

        @pl.loop(0, 5)
        def _(k):
            here = lane(k)
            for a in range(2):
                x = field_ref[a, :, here].astype(F32)
                z = (x - part[0:1, here]) * part[1:2, here] * part[4:5, here] + part[5:6, here]
                act = jnp.where(x < INF, z * sigmoid(z), 0.0)
                first = 576 if a == 0 else 64
                cat[first : first + 512, here] = act.astype(BF)

                @pl.when(k >= 2)
                def _():
                    cat[first : first + 512, lane(k, 384)] = from_left(act).astype(BF)

        keep = [
            pltpu.make_async_copy(cat.at[pl.ds(576, 512), pl.ds(0, 640)], ring_ref.at[0], x_sems.at[0]),
            pltpu.make_async_copy(cat.at[pl.ds(64, 512), pl.ds(0, 640)], ring_ref.at[1], x_sems.at[1]),
        ]
        start_all(keep)
        acc[...] = jnp.zeros((512, 640), F32)
        wait_all(in_w)

        @pl.loop(0, 3)
        def _(p):
            first = pl.multiple_of(jnp.where(p == 1, 576, 32 * p), 64)
            acc[...] += matmul(cat[pl.ds(first, 512), :], w_vm[pl.ds(pl.multiple_of(1024 * p, 1024), 1024), :])

        @pl.loop(0, 5)
        def _(k):
            row_valid = field_ref[0, :, 0:128].astype(F32) < INF
            out_ref[:, lane(k)] = jnp.where(row_valid, acc[:, lane(k)], INF).astype(BF)

        side_ref[...] = matmul(cat[576:1088, 0:384], w_vm[3072:3456, :]).astype(BF)
        wait_all(keep)


def forward_first(flags, pieces, weight, gain, bias):
    return kernel_call(
        forward_first_kernel,
        (FIELD, FIELD, TWO, TWO, PAIR),
        [SCALARS] + [FREE] * 6 + [ANY, INSIDE, INSIDE],
        (INSIDE, INSIDE, ANY, INSIDE, INSIDE),
        [
            pltpu.VMEM((3456, 640), BF),
            pltpu.VMEM((2, 8, 8, 8, 640), BF),
            pltpu.VMEM((1088, 1024), BF),
            pltpu.VMEM((512, 640), F32),
            pltpu.VMEM((8, 640), F32),
            pltpu.SemaphoreType.DMA((7,)),
            pltpu.SemaphoreType.DMA((16,)),
        ],
        flops=4_000_000_000,
    )(flags, *pieces, weight, gain, bias)


def weight_part(w_ref, w_vm, sems, p):
    rows = pl.ds(pl.multiple_of(1920 * p, 1920), 1920)
    return pltpu.make_async_copy(w_ref.at[rows], w_vm.at[rows], sems.at[p])


def clear_edges(x3):
    x3[0:64, :] = jnp.zeros((64, x3.shape[1]), BF)
    x3[576:640, :] = jnp.zeros((64, x3.shape[1]), BF)


def place(x3, k, values, left, right):
    x3[64:576, lane(k, left)] = from_left(values).astype(BF)
    x3[64:576, lane(k, 640)] = values.astype(BF)
    x3[64:576, lane(k, right)] = from_right(values).astype(BF)


def forward_conv(x3, w_ref, w_vm, w_sems, acc):
    @pl.loop(0, 3)
    def _(p):
        weight_part(w_ref, w_vm, w_sems, p).wait()
        acc[...] += matmul(
            x3[pl.ds(pl.multiple_of(64 * p, 64), 512), :], w_vm[pl.ds(pl.multiple_of(1920 * p, 1920), 1920), :]
        )


def statistics(x):
    valid = x < INF
    count = count_of(valid)
    mean = total_of(jnp.where(valid, x, 0.0)) / count
    centred = jnp.where(valid, x - mean, 0.0)
    inv = lax.rsqrt(total_of(centred * centred) / count + EPSILON)
    return valid, count, mean, inv, centred


def forward_rest_kernel(
    handed, flags, h, res, w_ref, gain, bias, out_ref, stats_ref, act_ref, w_vm, x3, acc, w_sems
):
    @pl.when(flags[0] == 1)
    def _():
        for p in range(3):
            weight_part(w_ref, w_vm, w_sems, p).start()
        clear_edges(x3)

        @pl.loop(0, 5)
        def _(k):
            here = lane(k)
            valid, _, mean, inv, centred = statistics(h[:, here].astype(F32))
            stats_ref[0:1, here] = mean
            stats_ref[1:2, here] = inv
            z = centred * inv * gain[:, here] + bias[:, here]
            act = jnp.where(valid, z * sigmoid(z), 0.0)
            act_ref[:, here] = act.astype(BF)
            place(x3, k, act, 0, 1280)
            acc[:, here] = jnp.zeros((512, 128), F32) if handed else res[:, here].astype(F32)

        forward_conv(x3, w_ref, w_vm, w_sems, acc)

        @pl.loop(0, 5)
        def _(k):
            here = lane(k)
            row_valid = h[:, 0:128].astype(F32) < INF
            out = jnp.where(row_valid, acc[:, here], INF).astype(BF)
            if handed:
                out_ref[0, :, here] = out
                out_ref[1, :, here] = h[:, here]
            else:
                out_ref[:, here] = out


def forward_rest(flags, h, res, weight, gain, bias, handed=False):
    return kernel_call(
        lambda *refs: forward_rest_kernel(handed, *refs),
        (TWO if handed else FIELD, PAIR, FIELD),
        [SCALARS, INSIDE, INSIDE, ANY, INSIDE, INSIDE],
        (INSIDE, INSIDE, INSIDE),
        [
            pltpu.VMEM((5760, 640), BF),
            pltpu.VMEM((640, 1920), BF),
            pltpu.VMEM((512, 640), F32),
            pltpu.SemaphoreType.DMA((3,)),
        ],
        flops=4_000_000_000,
    )(flags, h, res, weight, gain, bias)


def forward_last_kernel(flags, act, pair, w_ref, out_ref, w_vm, x3, acc, w_sems):
    @pl.when(flags[0] == 1)
    def _():
        for p in range(3):
            weight_part(w_ref, w_vm, w_sems, p).start()
        clear_edges(x3)

        @pl.loop(0, 5)
        def _(k):
            place(x3, k, act[:, lane(k)].astype(F32), 0, 1280)
            acc[:, lane(k)] = pair[1, :, lane(k)].astype(F32)

        forward_conv(x3, w_ref, w_vm, w_sems, acc)

        @pl.loop(0, 5)
        def _(k):
            row_valid = pair[0, :, 0:128].astype(F32) < INF
            out_ref[:, lane(k)] = jnp.where(row_valid, acc[:, lane(k)], INF).astype(BF)


def forward_last(flags, act, pair, weight):
    return kernel_call(
        forward_last_kernel,
        FIELD,
        [SCALARS, INSIDE, INSIDE, ANY],
        INSIDE,
        [
            pltpu.VMEM((5760, 640), BF),
            pltpu.VMEM((640, 1920), BF),
            pltpu.VMEM((512, 640), F32),
            pltpu.SemaphoreType.DMA((3,)),
        ],
        flops=4_000_000_000,
    )(flags, act, pair, weight)


def by_row(values):
    return values.transpose(1, 0, 2, 3).reshape(512, values.shape[3])


def backward_conv(g3, w_ref, w_vm, w_sems, acc):
    @pl.loop(0, 3)
    def _(p):
        weight_part(w_ref, w_vm, w_sems, p).wait()

        @pl.loop(0, 3)
        def _(q):
            acc[...] += matmul_bt(
                g3[pl.ds(pl.multiple_of(64 * (2 - p), 64), 512), pl.ds(pl.multiple_of(640 * q, 640), 640)],
                w_vm[pl.ds(pl.multiple_of(640 * (3 * p + q), 640), 640), :],
            )


def backward_conv_turned(g3, w_ref, w_vm, w_sems, acc):
    @pl.loop(0, 3)
    def _(p):
        weight_part(w_ref, w_vm, w_sems, p).wait()
        acc[...] += matmul(
            g3[pl.ds(pl.multiple_of(64 * (2 - p), 64), 512), :],
            w_vm[pl.ds(pl.multiple_of(1920 * p, 1920), 1920), :],
        )


def backward_top_kernel(flags, g_ref, w_ref, total_ref, own_ref, w_vm, g3, w_sems):
    for p in range(3):
        weight_part(w_ref, w_vm, w_sems, p).start()
    clear_edges(g3)

    @pl.loop(0, 5)
    def _(k):
        here = lane(k)
        g = by_row(g_ref[:, :, :, here].astype(F32))
        own_ref[:, here] = g.astype(BF)
        place(g3, k, g, 1280, 0)
        total_ref[:, here] = jnp.zeros((512, 128), F32)

    backward_conv(g3, w_ref, w_vm, w_sems, total_ref)


def backward_top(flags, g, weight):
    return kernel_call(
        backward_top_kernel,
        (jax.ShapeDtypeStruct((512, 640), F32), FIELD),
        [SCALARS, INSIDE, ANY],
        (INSIDE, INSIDE),
        [
            pltpu.VMEM((5760, 640), BF),
            pltpu.VMEM((640, 1920), BF),
            pltpu.SemaphoreType.DMA((3,)),
        ],
        flops=4_000_000_000,
    )(flags, g, weight)


def norm_back(grad, valid, count, centred, inv, scale, offset, sums_ref, here):
    xhat = centred * inv
    z = xhat * scale + offset
    sig = sigmoid(z)
    dz = jnp.where(valid, grad * sig * (1.0 + z * (1.0 - sig)), 0.0)
    s1 = total_of(dz)
    s2 = total_of(dz * xhat)
    sums_ref[0:1, here] = s1
    sums_ref[1:2, here] = s2
    back = scale * inv * (dz - s1 / count - xhat * (s2 / count))
    return jnp.where(valid, back, 0.0), jnp.where(valid, z * sig, 0.0)


def turn_kernel(flags, pair, grad, gain, bias, out_ref, sums_ref, act_ref):
    @pl.when(flags[0] == 1)
    def _():
        @pl.loop(0, 5)
        def _(k):
            here = lane(k)
            valid, count, _, inv, centred = statistics(pair[0, :, here].astype(F32))
            back, act = norm_back(
                grad[:, here], valid, count, centred, inv, gain[:, here], bias[:, here], sums_ref, here
            )
            act_ref[:, here] = act.astype(BF)
            out_ref[:, here] = back.astype(BF)


def turn(flags, h, grad, gain, bias):
    return kernel_call(
        turn_kernel,
        (FIELD, PAIR, FIELD),
        [SCALARS] + [INSIDE] * 4,
        (INSIDE, INSIDE, INSIDE),
        [],
        flops=1_000_000_000,
    )(flags, h, grad, gain, bias)


def backward_rest_kernel(
    handed, flags, g_ref, add, h, stats, w_ref, gain, bias, out_ref, sums_ref, w_vm, g3, acc, w_sems
):
    @pl.when(flags[0] == 1)
    def _():
        for p in range(3):
            weight_part(w_ref, w_vm, w_sems, p).start()
        clear_edges(g3)

        @pl.loop(0, 5)
        def _(k):
            place(g3, k, g_ref[:, lane(k)].astype(F32), 1280, 0)
            acc[:, lane(k)] = jnp.zeros((512, 128), F32)

        backward_conv_turned(g3, w_ref, w_vm, w_sems, acc)
        @pl.loop(0, 5)
        def _(k):
            here = lane(k)
            x = h[:, here].astype(F32)
            valid = x < INF
            centred = jnp.where(valid, x - stats[0:1, here], 0.0)
            back, _ = norm_back(
                acc[:, here], valid, count_of(valid), centred, stats[1:2, here], gain[:, here], bias[:, here],
                sums_ref, here,
            )
            if handed:
                out_ref[0, :, here] = back.astype(BF)
                out_ref[1, :, here] = g_ref[:, here]
            else:
                out_ref[:, here] = (back + by_row(add[:, :, :, here].astype(F32))).astype(BF)


def backward_rest(flags, g, add, h, stats, weight, gain, bias, handed=False):
    return kernel_call(
        lambda *refs: backward_rest_kernel(handed, *refs),
        (TWO if handed else FIELD, PAIR),
        [SCALARS, INSIDE, INSIDE, INSIDE, INSIDE, ANY, INSIDE, INSIDE],
        (INSIDE, INSIDE),
        [
            pltpu.VMEM((5760, 640), BF),
            pltpu.VMEM((640, 1920), BF),
            pltpu.VMEM((512, 640), F32),
            pltpu.SemaphoreType.DMA((3,)),
        ],
        flops=4_000_000_000,
    )(flags, g, add, h, stats, weight, gain, bias)


def backward_first_conv_kernel(flags, pair, w_ref, acc, w_vm, g2, sems):
    in_w = weight_first(w_ref, w_vm, sems)
    start_all(in_w)
    g2[512:576, :] = jnp.zeros((64, 1280), BF)

    @pl.loop(0, 5)
    def _(k):
        g = pair[0, :, lane(k)].astype(F32)
        g2[0:512, lane(k)] = g.astype(BF)
        g2[0:512, lane(k, 640)] = from_right(g).astype(BF)

    acc[...] = jnp.zeros((2, 512, 640), F32)
    wait_all(in_w)

    @pl.loop(0, 3)
    def _(p):
        rows = pl.ds(pl.multiple_of(jnp.where(p == 0, 64, 0), 64), 512)
        a = jnp.where(p == 1, 0, 1)
        first = pl.multiple_of(1024 * p, 1024)
        acc[a] += matmul_bt(g2[rows, 0:640], w_vm[pl.ds(first, 640), :])
        acc[a, :, 256:640] += matmul_bt(g2[rows, 640:1280], w_vm[pl.ds(first + 640, 384), :])

    acc[0, :, 0:384] += matmul_bt(pair[1], w_vm[3072:3456, :])


def backward_first_conv(flags, pair, weight):
    return kernel_call(
        backward_first_conv_kernel,
        jax.ShapeDtypeStruct((2, 512, 640), F32),
        [SCALARS, INSIDE, ANY],
        INSIDE,
        [
            pltpu.VMEM((3456, 640), BF),
            pltpu.VMEM((576, 1280), BF),
            pltpu.SemaphoreType.DMA((7,)),
        ],
        flops=5_000_000_000,
    )(flags, pair, weight)


def backward_first_norm_kernel(flags, acc, x_ref, stats, gain, bias, out_ref, sums_ref, dz_vm, part):
    part[4:5, :] = twice(gain)
    part[5:6, :] = twice(bias)

    @pl.loop(0, 5)
    def _(k):
        here = lane(k)
        s1 = s2 = 0.0
        for a in range(2):
            x = x_ref[a, :, here].astype(F32)
            valid = x < INF
            xhat = jnp.where(valid, x - stats[0:1, here], 0.0) * stats[1:2, here]
            z = xhat * part[4:5, here] + part[5:6, here]
            sig = sigmoid(z)
            dz = jnp.where(valid, acc[a, :, here] * sig * (1.0 + z * (1.0 - sig)), 0.0)
            dz_vm[a, :, here] = dz
            s1 = s1 + total_of(dz)
            s2 = s2 + total_of(dz * xhat)
        part[0:1, here] = s1
        part[1:2, here] = s2
        part[2:3, here] = 4.0 * count_of(valid)

    part[0:1, :] = part[0:1, :] + half_turn(part[0:1, :])
    part[1:2, :] = part[1:2, :] + half_turn(part[1:2, :])
    sums_ref[...] = jnp.where(lax.broadcasted_iota(jnp.int32, (2, 640), 1) < 320, part[0:2, :], 0.0)

    @pl.loop(0, 5)
    def _(k):
        here = lane(k)
        count = part[2:3, here]
        scale = part[4:5, here] * stats[1:2, here]
        for a in range(2):
            x = x_ref[a, :, here].astype(F32)
            xhat = (x - stats[0:1, here]) * stats[1:2, here]
            back = scale * (dz_vm[a, :, here] - part[0:1, here] / count - xhat * (part[1:2, here] / count))
            back = jnp.where(x < INF, back, 0.0).reshape(4, 2, 8, 8, 128).transpose(2, 0, 1, 3, 4)
            out_ref[:, :, :, a, :, here] = back.astype(BF)


def backward_first_norm(flags, field, x, stats, gain, bias):
    return kernel_call(
        backward_first_norm_kernel,
        (jax.ShapeDtypeStruct((8, 4, 2, 2, 8, 640), BF), PAIR),
        [SCALARS, INSIDE, INSIDE, INSIDE, INSIDE, INSIDE],
        (INSIDE, INSIDE),
        [pltpu.VMEM((2, 512, 640), F32), pltpu.VMEM((8, 640), F32)],
        flops=1_000_000_000,
    )(flags, field, x, stats, gain, bias)


def send_sides(side, rows, sent_ref):
    sent_ref[0:320, :] = side.astype(BF)
    for k in range(3):
        piece = rows.astype(BF)
        sent_ref[320 + 2 * k : 322 + 2 * k, :] = piece
        rows = rows - piece.astype(F32)
    sent_ref[326:336, :] = jnp.zeros((10, 640), BF)


def projection_grad_kernel(flags, ring_ref, pair_ref, rows, out_ref, rows_ref, sent_ref, a_vm, g_vm, sems):
    ins = [
        pltpu.make_async_copy(ring_ref.at[0], a_vm, sems.at[0]),
        pltpu.make_async_copy(pair_ref.at[1], g_vm, sems.at[1]),
    ]
    start_all(ins)
    wait_all(ins)
    side = matmul_at(a_vm[:, 0:384], g_vm[...])[0:320, :]
    out_ref[...] = side
    rows_ref[...] = rows[...]
    send_sides(side, rows[...], sent_ref)


SIDES = (jax.ShapeDtypeStruct((320, 640), F32), PAIR, jax.ShapeDtypeStruct((336, 640), BF))


def projection_grad(flags, ring, pair, rows):
    return kernel_call(
        projection_grad_kernel,
        SIDES,
        [SCALARS, FREE, FREE, INSIDE],
        (INSIDE, INSIDE, INSIDE),
        [pltpu.VMEM((512, 640), BF), pltpu.VMEM((512, 640), BF), pltpu.SemaphoreType.DMA((2,))],
        flops=200_000_000,
        mib=8,
    )(flags, ring, pair, rows)


def add_sides_kernel(side, rows, got, out_ref, rows_ref, sent_ref):
    side = side[...] + got[0:320, :].astype(F32)
    rows = rows[...]
    for k in range(3):
        rows = rows + got[320 + 2 * k : 322 + 2 * k, :].astype(F32)
    out_ref[...] = side
    rows_ref[...] = rows
    send_sides(side, rows, sent_ref)


def add_sides(side, rows, got):
    return kernel_call(
        add_sides_kernel, SIDES, [INSIDE, INSIDE, INSIDE], (INSIDE, INSIDE, INSIDE), [], mib=8
    )(side, rows, got)


def ring_value_kernel(g, sums, out_ref):
    out_ref[0:512, :] = g[...]
    rows = sums[...]
    pieces = []
    for _ in range(3):
        pieces.append(rows.astype(BF).astype(F32))
        rows = rows - pieces[-1]
    out_ref[512:528, :] = jnp.concatenate([*pieces, jnp.zeros((10, 640), F32)], axis=0).astype(BF)


def ring_value(g, sums):
    return kernel_call(
        ring_value_kernel, jax.ShapeDtypeStruct((528, 640), BF), [INSIDE, INSIDE], INSIDE, [], mib=8
    )(g, sums)


def add_rows_kernel(first, *refs):
    blocks, out_ref, rows, sems = refs[:8], refs[8], refs[9], refs[10]
    copies = [
        pltpu.make_async_copy(blocks[b].at[pl.ds(first, 16)], rows.at[b], sems.at[b]) for b in range(8)
    ]
    start_all(copies)
    wait_all(copies)
    total = rows[0].astype(F32)
    for b in range(1, 8):
        total = total + rows[b].astype(F32)
    out_ref[...] = total[0:2, :] + total[2:4, :] + total[4:6, :]


def add_rows(blocks, first):
    return kernel_call(
        lambda *refs: add_rows_kernel(first, *refs),
        PAIR,
        [FREE] * 8,
        INSIDE,
        [pltpu.VMEM((8, 16, 640), BF), pltpu.SemaphoreType.DMA((8,))],
        mib=8,
    )(*blocks)


def kernel_grads_kernel(blocks, fresh, last, *refs):
    acts, gs = refs[:blocks], refs[blocks : 2 * blocks]
    refs = refs[2 * blocks :]
    gs = [one.at[pl.ds(512 if one.shape[0] == 1040 else 0, 512)] for one in gs]
    acts = [one.at[pl.ds(0, 512)] for one in acts]
    if not fresh:
        kept, refs = refs[0], refs[1:]
    sums, a_vm, g_vm, g3, sems = refs[0], *refs[-4:]
    if last:
        out_ref, out_sems = refs[0], refs[1]
        sums = kept
    ins = []
    for b in range(blocks):
        ins.append(pltpu.make_async_copy(gs[b], g_vm.at[b], sems.at[b, 0]))
        ins.append(pltpu.make_async_copy(acts[b], a_vm.at[b], sems.at[b, 1]))
    start_all(ins)

    @pl.loop(0, blocks)
    def _(b):
        clear_edges(g3.at[b])

    @pl.loop(0, blocks)
    def _(b):
        pltpu.make_async_copy(gs[0], g_vm.at[b], sems.at[b, 0]).wait()

        @pl.loop(0, 5)
        def _(k):
            place(g3.at[b], k, g_vm[b, :, lane(k)].astype(F32), 1280, 0)

    wait_all(ins[1::2])

    def outs(p):
        rows = pl.ds(pl.multiple_of(640 * p, 640), 640)
        return [
            pltpu.make_async_copy(
                sums.at[rows, pl.ds(640 * q, 640)],
                out_ref.at[pl.ds(pl.multiple_of(640 * (3 * p + q), 640), 640)],
                out_sems.at[p, q],
            )
            for q in range(3)
        ]

    @pl.loop(0, 3)
    def _(p):
        rows = pl.ds(pl.multiple_of(640 * p, 640), 640)
        here = pl.ds(pl.multiple_of(64 * (2 - p), 64), 512)
        if fresh:
            sums[rows, :] = jnp.zeros((640, 1920), F32)
        elif not last:
            sums[rows, :] = kept[rows, :]

        @pl.loop(0, blocks)
        def _(b):
            sums[rows, :] += matmul_at(a_vm[b], g3[b, here, :])

        if last:
            start_all(outs(p))

    if last:
        for p in range(3):
            wait_all(outs(p))


def kernel_grads_first_kernel(blocks, fresh, last, *refs):
    acts, gs = refs[:blocks], refs[blocks : 2 * blocks]
    refs = refs[2 * blocks :]
    if last:
        side, refs = refs[0], refs[1:]
    if not fresh:
        kept, refs = refs[0], refs[1:]
    sums, a_vm, g_vm, g2, sems = refs[0], *refs[-4:]
    extra = []
    if last:
        out_ref, zeros, out_sems, extra_sems = refs[:4]
        sums = kept
    ins = []
    for b in range(blocks):
        ins.append(pltpu.make_async_copy(gs[b].at[pl.ds(0, 512)], g_vm.at[b], sems.at[b, 0]))
        ins.append(pltpu.make_async_copy(acts[b], a_vm.at[b], sems.at[b, 1]))
    start_all(ins)
    if last:
        zeros[...] = jnp.zeros((320, 640), F32)
        extra.append(pltpu.make_async_copy(side, out_ref.at[pl.ds(2880, 320)], extra_sems.at[0]))
        for k in range(8):
            extra.append(pltpu.make_async_copy(zeros, out_ref.at[pl.ds(3200 + 320 * k, 320)], extra_sems.at[1 + k]))
        start_all(extra)
    @pl.loop(0, blocks)
    def _(b):
        g2[b, 512:576, :] = jnp.zeros((64, 1280), BF)
        pltpu.make_async_copy(gs[0].at[pl.ds(0, 512)], g_vm.at[b], sems.at[b, 0]).wait()

        @pl.loop(0, 5)
        def _(k):
            g = g_vm[b, :, lane(k)].astype(F32)
            g2[b, 0:512, lane(k)] = g.astype(BF)
            g2[b, 0:512, lane(k, 640)] = from_right(g).astype(BF)

    wait_all(ins[1::2])

    def outs(p):
        low = pl.multiple_of(640 * p, 640)
        return [
            pltpu.make_async_copy(
                sums.at[pl.ds(low, 640), pl.ds(0, 640)],
                out_ref.at[pl.ds(pl.multiple_of(960 * p + 320, 320), 640)],
                out_sems.at[p, 0],
            ),
            pltpu.make_async_copy(
                sums.at[pl.ds(low, 320), pl.ds(640, 640)],
                out_ref.at[pl.ds(pl.multiple_of(960 * p, 320), 320)],
                out_sems.at[p, 1],
            ),
        ]

    @pl.loop(0, 3)
    def _(p):
        here = pl.ds(pl.multiple_of(jnp.where(p == 0, 64, 0), 64), 512)
        low = pl.multiple_of(640 * p, 640)
        odd = jnp.where(p == 1, 0, 1)
        if fresh:
            sums[pl.ds(low, 640), :] = jnp.zeros((640, 1280), F32)
        elif not last:
            sums[pl.ds(low, 640), :] = kept[pl.ds(low, 640), :]

        @pl.loop(0, blocks)
        def _(b):
            sums[pl.ds(low, 640), 0:640] += matmul_at(a_vm[b, odd], g2[b, here, 0:640])
            left = matmul_at(a_vm[b, odd, :, 256:640], g2[b, here, 640:1280])
            sums[pl.ds(low, 320), 640:1280] += left[64:384, :]

        if last:
            start_all(outs(p))

    if last:
        for p in range(3):
            wait_all(outs(p))
    wait_all(extra)


def kernel_grads(acts, gs, kept=None, last=False, first=False, side=None):
    blocks = len(acts)
    fresh = kept is None
    scratch = []
    if last and first:
        scratch += [pltpu.VMEM((320, 640), F32)]
    if last:
        scratch += [pltpu.SemaphoreType.DMA((3, 3))]
    if last and first:
        scratch += [pltpu.SemaphoreType.DMA((9,))]
    scratch += [
        pltpu.VMEM((blocks, 2, 512, 640) if first else (blocks, 512, 640), BF),
        pltpu.VMEM((blocks, 512, 640), BF),
        pltpu.VMEM((blocks, 576, 1280) if first else (blocks, 640, 1920), BF),
        pltpu.SemaphoreType.DMA((blocks, 2)),
    ]
    extra = [side] if last and first else []
    count = 2 * blocks + len(extra)
    kernel = kernel_grads_first_kernel if first else kernel_grads_kernel
    sums = jax.ShapeDtypeStruct((1920, 1280 if first else 1920), F32)
    return kernel_call(
        lambda *refs: kernel(blocks, fresh, last, *refs),
        jax.ShapeDtypeStruct((5760, 640), F32) if last else sums,
        [FREE] * count + ([] if fresh else [KEPT]),
        ANY if last else KEPT,
        scratch,
        aliases={} if fresh or last else {count: 0},
        flops=4_000_000_000 * blocks,
        mib=20,
    )(*acts, *gs, *extra, *([] if fresh else [kept]))


def empty(shapes):
    return pl.pallas_call(
        lambda *refs: None,
        out_shape=tuple(shapes),
        out_specs=tuple(ANY for _ in shapes),
    )()


BOTH = ("dp", "section")
RING = (0, 2, 4, 6, 7, 5, 3, 1)


def move(value, triples):
    count = lax.axis_size("section")
    return lax.ppermute(value, BOTH, [(d * count + s, e * count + t) for (d, s), (e, t) in triples])


def hop(value, source, target):
    return move(value, [((d, source), (d, target)) for d in range(MICRO)])


class Ring:
    def __init__(self, value, sections):
        self.up = [((RING[k], s), (RING[(k + 1) % 8], s)) for k in range(8) for s in sections]
        self.down = [(b, a) for a, b in self.up]
        self.blocks = [value]

    def step(self, last_down=False):
        count = len(self.blocks)
        high = self.blocks[max(0, count - 2)]
        low = self.blocks[count - 1]
        if count < 7 or not last_down:
            self.blocks.append(move(high, self.up))
        if count < 7 or last_down:
            self.blocks.append(move(low, self.down))


def dp_total(value, sections):
    for k in (1, 2, 4):
        value = value + move(value, [((d, s), (d ^ k, s)) for d in range(MICRO) for s in sections])
    return value


def after(value, *others):
    return lax.optimization_barrier((value, *others))[0]


def pick(images, image_count, index):
    image = lax.dynamic_index_in_dim(images, index, 0)
    return jnp.where(index < image_count, image, INF).reshape(1, 8, 2, 8, 640)


def exchange_images(images, image_count, row, section, offsets):
    return [
        move(pick(images, image_count, row ^ k), [((d, section), (d ^ k, section)) for d in range(MICRO)])
        for k in offsets
    ]


SLOTS = jax.ShapeDtypeStruct((8, 8, 8, 640), BF)
PARTS = jax.ShapeDtypeStruct((4, 8, 2, 2, 8, 640), BF)


SLOTS = jax.ShapeDtypeStruct((8, 8, 8, 640), BF)
PARTS = jax.ShapeDtypeStruct((8, 4, 2, 2, 8, 640), BF)


def by_micro_batch(images, image_counts, conv_weight, bn_gain, bn_bias, out_grad):
    section = lax.axis_index("section")
    row = lax.axis_index("dp")
    weight = conv_weight[0]
    norm = (bn_gain, bn_bias)
    plain, adds = jnp.array([1, 0], jnp.int32), jnp.array([1, 1], jnp.int32)

    def segment(shapes, *branches):
        def whole(branch):
            def run():
                found = branch()
                missing = [name for name in shapes if name not in found]
                if missing:
                    found.update(zip(missing, empty([shapes[name] for name in missing])))
                return [found[name] for name in shapes]

            return run

        return dict(zip(shapes, lax.switch(section, [whole(branch) for branch in branches])))

    def on_section(first, second, third, fourth):
        return jnp.where(
            section == 0, first, jnp.where(section == 1, second, jnp.where(section == 2, third, fourth))
        )

    def nothing():
        return {}

    def named(prefix, blocks):
        return {f"{prefix}{k}": one for k, one in enumerate(blocks)}

    def listed(found, prefix, count):
        return [found[f"{prefix}{k}"] for k in range(count)]

    def many(prefix, count, shape):
        return {f"{prefix}{k}": shape for k in range(count)}

    def exchange(value):
        return lax.all_to_all(value, "dp", 0, 0, tiled=True)

    def resume(value, blocks, index):
        ring = Ring(value, (index,))
        ring.blocks += blocks
        return ring

    def shown(value):
        return jnp.where(value < INF, value, 0.0).reshape(8, 8, 8, 640).transpose(1, 0, 2, 3)

    count = image_counts[0]
    piece = jax.ShapeDtypeStruct((1, 8, 2, 8, 640), BF)
    grad_shape = jax.ShapeDtypeStruct((512, 640), F32)

    def zero_0():
        got = exchange_images(images, count, row, 0, (4, 3, 2, 1))
        return {"p1": got[3], "p2": got[2], "p3": got[1], "p4": got[0]}

    def zero_1():
        return {"others": jnp.concatenate(exchange_images(images, count, row, 1, (5, 6, 7)), axis=0)}

    def zero_2():
        return {"top": exchange(out_grad)}

    def zero_3():
        grad, own = backward_top(plain, exchange(out_grad), weight)
        return {"grad": grad, "own": own}

    zeroth = segment(
        {
            **{f"p{k}": piece for k in range(1, 5)}, "others": jax.ShapeDtypeStruct((3, 8, 2, 8, 640), BF),
            "top": SLOTS, "grad": grad_shape, "own": FIELD,
        },
        zero_0, zero_1, zero_2, zero_3,
    )
    others = hop(zeroth["others"], 1, 0)

    def one_0():
        pieces = (pick(images, count, row), *[zeroth[f"p{k}"] for k in range(1, 5)], others)
        h1, side, ring, fields, stats = forward_first(
            jnp.stack([jnp.int32(1), row.astype(jnp.int32)]), pieces, weight, *norm
        )
        return {"h1": h1, "side": side, "ring": ring, "fields": fields, "stats": stats}

    def turn_weight(weight):
        return weight.reshape(9, 640, 640).transpose(0, 2, 1).reshape(5760, 640)

    def turned():
        return {"weight": turn_weight(weight)}

    first = segment(
        {"weight": jax.ShapeDtypeStruct((5760, 640), BF), "h1": FIELD, "side": FIELD, "ring": TWO, "fields": TWO, "stats": PAIR},
        one_0, nothing, turned, nothing,
    )
    h1_in, side_in = hop(first["h1"], 0, 1), hop(first["side"], 0, 1)

    def two_1():
        y1, stats, act = forward_rest(adds, h1_in, side_in, weight, *norm)
        return {"y1": y1, "stats": stats, "act": act}

    second = segment(
        {"y1": FIELD, "act": FIELD, "stats": PAIR}, nothing, two_1, nothing, nothing
    )
    y1_in = hop(second["y1"], 1, 2)

    def turned_1():
        return {"weight": turn_weight(after(weight, second["y1"]))}

    wait_2 = segment({"weight": jax.ShapeDtypeStruct((5760, 640), BF)}, nothing, turned_1, nothing, nothing)
    y1_in = after(y1_in, wait_2["weight"])

    def three_2():
        pair, stats, act = forward_rest(plain, y1_in, y1_in, weight, *norm, handed=True)
        return {"pair": pair, "stats": stats, "act": act}

    third = segment({"pair": TWO, "act": FIELD, "stats": PAIR}, nothing, nothing, three_2, nothing)
    h3_in = hop(third["pair"], 2, 3)

    def four_3():
        g_h3, sums, act = turn(plain, h3_in, zeroth["grad"], *norm)
        return {"g": g_h3, "sums": sums, "act": act}

    fourth = segment({"g": FIELD, "act": FIELD, "sums": PAIR}, nothing, nothing, nothing, four_3)
    g_h3_in = hop(fourth["g"], 3, 2)

    def five_2():
        g_y1, sums = backward_rest(adds, g_h3_in, zeroth["top"], y1_in, third["stats"], first["weight"], *norm)
        return {"g": g_y1, "sums": sums}

    fifth = segment({"g": FIELD, "sums": PAIR}, nothing, nothing, five_2, nothing)
    g_y1_in = hop(fifth["g"], 2, 1)

    def one_step(value, index, beside):
        value = after(value, fifth["g"])
        ring = Ring(value, (index,))
        ring.step()
        ring.step()
        return {"out": beside(value), **named("u", ring.blocks)}

    wait_5 = segment(
        {"out": SLOTS, **many("u", 5, FIELD)},
        lambda: {"out": shown(after(first["h1"], fifth["g"]))},
        lambda: one_step(second["act"], 1, lambda _: shown(second["y1"])),
        lambda: one_step(third["act"], 2, lambda _: shown(third["pair"][0])),
        lambda: one_step(fourth["act"], 3, lambda act: shown(forward_last(plain, act, h3_in, weight))),
    )
    g_y1_in = after(g_y1_in, wait_5["u0"])

    def six_0():
        ring = Ring(first["ring"], (0,))
        ring.step()
        ring.step()
        return named("a", ring.blocks)

    def six_1():
        pair, sums = backward_rest(
            plain, g_y1_in, zeroth["top"], h1_in, second["stats"], wait_2["weight"], *norm, handed=True
        )
        return {"pair": pair, "sums": sums}

    sixth = segment(
        {"pair": TWO, "sums": PAIR, **many("a", 5, TWO)}, six_0, six_1, nothing, nothing
    )
    pair_sent = hop(sixth["pair"], 1, 0)

    def seven_0():
        ring = Ring(after(sixth["a0"], sixth["pair"]), (0,))
        ring.blocks = listed(sixth, "a", 5)
        ring.blocks[3] = after(ring.blocks[3], sixth["pair"])
        ring.step()
        return named("a", ring.blocks[5:])

    def seven_1():
        return {"g": ring_value(after(g_y1_in, sixth["pair"]), sixth["sums"])}

    def seven_2():
        return {"g": ring_value(g_h3_in, fifth["sums"])}

    def seven_3():
        return {"g": ring_value(zeroth["own"], fourth["sums"])}

    tall = jax.ShapeDtypeStruct((528, 640), BF)
    seventh = segment({"g": tall, **many("a", 2, TWO)}, seven_0, seven_1, seven_2, seven_3)

    pair_in = after(pair_sent, seventh["g"])

    def work(ring, late):
        gs, acts = ring.blocks, late.blocks
        total = None
        for low, high in ((0, 3), (3, 5), (5, 7)):
            ring.step()
            if low > 0:
                late.step(True)
            total = kernel_grads(acts[low:high], gs[low:high], total)
            if low < 5:
                gs[high : high + 2], acts[high:], total = lax.optimization_barrier(
                    (gs[high : high + 2], acts[high:], total)
                )
        return kernel_grads(acts[7:8], gs[7:8], total, True)

    def eight_0():
        fence = lax.optimization_barrier
        ring = Ring(pair_in[0], (0,))
        ring.step()
        field = backward_first_conv(plain, pair_in, weight)
        parts, sums = backward_first_norm(plain, field, first["fields"], first["stats"], *norm)
        gs = ring.blocks
        sums, gs[1:3] = fence((sums, gs[1:3]))
        side, rows, sent = projection_grad(plain, first["ring"], pair_in, sums)

        def to(k):
            return move(sent, [((d, 0), (d ^ k, 0)) for d in range(MICRO)])

        got = to(1)
        parts = exchange(after(parts, sent))
        late = Ring(sixth["a0"], (0,))
        late.blocks = acts = listed(sixth, "a", 5) + listed(seventh, "a", 2)
        ring.step()
        side, rows, sent = add_sides(side, rows, got)
        got = to(2)
        acts[0] = after(acts[0], side)
        total = kernel_grads(acts[0:3], gs[0:3], first=True)
        gs[3:5], acts[3:], total = fence((gs[3:5], acts[3:], total))
        ring.step()
        late.step(True)
        total = kernel_grads(acts[3:5], gs[3:5], total, first=True)
        gs[5:7], got, total = fence((gs[5:7], got, total))
        ring.step()
        side, rows, sent = add_sides(side, rows, got)
        got = to(4)
        acts[5] = after(acts[5], side)
        total = kernel_grads(acts[5:7], gs[5:7], total, first=True)
        got, total = fence((got, total))
        side, rows, _ = add_sides(side, rows, got)
        total = kernel_grads(acts[7:8], gs[7:8], total, True, True, side)
        parts, total = fence((parts, total))
        return [parts, total, rows]

    def eight_rest():
        gs = Ring(seventh["g"], (1, 2, 3))
        gs.step()
        acts = Ring(wait_5["u0"], (1, 2, 3))
        acts.blocks = listed(wait_5, "u", 5)
        total = work(gs, acts)
        return [*empty([PARTS]), total, add_rows(gs.blocks, 512)]

    parts, grads, sums = lax.cond(section > 0, eight_rest, eight_0)

    mine = parts[:, 0]
    for k in range(1, 4):
        mine = jnp.where(section == k, hop(parts[:, k], 0, k), mine)
    out = exchange(after(wait_5["out"], parts))
    return (out[None], mine.reshape(8, 4, 16, 320), grads[None], sums[1:2], sums[0:1])


def solution(mesh):
    one_each = mesh.shape["dp"] == MICRO and mesh.shape["section"] == 4

    def on_device(images, *rest):
        if one_each and images.shape == (MICRO, 16, 16, 320):
            return by_micro_batch(images, *rest)
        return pipelined(images, *rest)

    return jax.shard_map(
        on_device,
        mesh=mesh,
        in_specs=(
            P("dp", None, None, None),
            P("dp"),
            P("section", None, None),
            P("section", None),
            P("section", None),
            P("dp", None, None, None),
        ),
        out_specs=(
            P("section", "dp", None, None, None),
            P("dp", "section", None, None),
            P("section", None, None),
            P("section", None),
            P("section", None),
        ),
        check_vma=False,
    )
```

```python
import jax
import jax.numpy as jnp
from jax import lax
from jax.experimental import pallas as pl
from jax.experimental.pallas import tpu as pltpu
from jax.sharding import PartitionSpec as P

MICRO = 8


EPSILON = 1e-05


def for_sending(value):

    def short(part):
        return part.astype(jnp.bfloat16) if part.dtype == jnp.float32 else part

    return jax.tree.map(short, value)


def shifted(value, axis, steps):
    count = lax.axis_size(axis)
    initial, last = (max(0, -steps), min(count, count - steps))
    return lax.ppermute(value, axis, [(source, source + steps) for source in range(initial, last)])


def conv_forward(activation, kernel, stride):
    return lax.conv_general_dilated(
        activation,
        kernel,
        (stride, stride),
        ((1, 1), (1, 1)),
        dimension_numbers=("NHWC", "HWIO", "NHWC"),
        preferred_element_type=jnp.float32,
    )


def conv_input_grad(gradient, kernel, stride):
    upper = 1 if stride == 1 else 2
    return lax.conv_general_dilated(
        gradient,
        kernel[::-1, ::-1],
        (1, 1),
        ((1, upper), (1, upper)),
        lhs_dilation=(stride, stride),
        dimension_numbers=("NHWC", "HWOI", "NHWC"),
        preferred_element_type=jnp.float32,
    )


def conv_kernel_grad(activation, gradient, stride):
    upper = 1 if stride == 1 else 0
    return lax.conv_general_dilated(
        activation,
        gradient,
        (1, 1),
        ((1, upper), (1, upper)),
        rhs_dilation=(stride, stride),
        dimension_numbers=("CHWN", "IHWO", "HWNC"),
        preferred_element_type=jnp.float32,
    )


def channel_sum(values, image_mask):
    return jnp.sum(image_mask[:, None, None, None] * values, axis=(0, 1, 2))


def normalize(values, channel_mean, inv_std, norm_gain, norm_bias):
    scaled = (values - channel_mean) * inv_std
    return (scaled, scaled * norm_gain + norm_bias)


def norm_terms(grad_act, values, image_mask, channel_mean, inv_std, norm_gain, norm_bias):
    scaled, pre_act = normalize(values, channel_mean, inv_std, norm_gain, norm_bias)
    sigmoid_val = jax.nn.sigmoid(pre_act)
    grad_pre = (
        grad_act
        * image_mask[:, None, None, None]
        * sigmoid_val
        * (1.0 + pre_act * (1.0 - sigmoid_val))
    )
    return (grad_pre, scaled)


def pipelined(images, image_counts, conv_weight, bn_gain, bn_bias, out_grad):
    section_count = lax.axis_size("section")
    section_index = lax.axis_index("section")
    img_dev = images.shape[0]
    per_micro = img_dev // MICRO
    height = images.shape[1]
    side = height // 2
    c_in = images.shape[3]
    c_out = conv_weight.shape[2]
    kernel_rows = conv_weight.shape[1]
    is_first = section_index == 0
    is_last = section_index == section_count - 1
    adds_residual = section_index % 2 == 1
    merges_back = (section_index % 2 == 0) & (section_index > 0)
    valid_img = (jnp.arange(img_dev, dtype=jnp.int32) < image_counts[0]).astype(jnp.float32)
    valid_img = valid_img.reshape(per_micro, MICRO)
    image_groups = images.reshape(per_micro, MICRO, height, height, c_in)
    grad_groups = out_grad.reshape(per_micro, MICRO, side, side, c_out)
    kernel_all = conv_weight[0]
    kernel_first = kernel_all[: 9 * c_in].reshape(3, 3, c_in, c_out)
    kernel_proj = kernel_all[9 * c_in : 10 * c_in]
    kernel_rest = kernel_all.reshape(3, 3, c_out, c_out)
    norm_gain = bn_gain[0]
    norm_bias = bn_bias[0]
    tick_count = MICRO + section_count - 1
    pad_width = (0, c_out - c_in)

    def forward_first(raw_input, section_input, residual, image_mask, channel_mean, inv_std):
        scaled, pre_act = normalize(
            raw_input, channel_mean[:c_in], inv_std[:c_in], norm_gain[:c_in], norm_bias[:c_in]
        )
        activation = (jax.nn.silu(pre_act) * image_mask[:, None, None, None]).astype(jnp.bfloat16)
        conv_out = conv_forward(activation, kernel_first, 2)
        sub_grid = activation[:, 0::2, 0::2, :].reshape(-1, c_in)
        projected = jnp.dot(sub_grid, kernel_proj, preferred_element_type=jnp.float32)
        projected = projected.reshape(per_micro, side, side, c_out)
        return (conv_out.astype(jnp.bfloat16), projected.astype(jnp.bfloat16))

    def forward_rest(raw_input, section_input, residual, image_mask, channel_mean, inv_std):
        scaled, pre_act = normalize(section_input, channel_mean, inv_std, norm_gain, norm_bias)
        activation = (jax.nn.silu(pre_act) * image_mask[:, None, None, None]).astype(jnp.bfloat16)
        conv_out = conv_forward(activation, kernel_rest, 1)
        summed = conv_out + jnp.where(adds_residual, 1.0, 0.0) * residual.astype(jnp.float32)
        sent_main = summed.astype(jnp.bfloat16)
        return (sent_main, jnp.where(adds_residual, sent_main, residual))

    def forward_tick(step_index, state_carry):
        recv_main, recv_side, out_buf, in_buf, moment_buf, count_buf = state_carry
        micro_index = step_index - section_index
        active = (micro_index >= 0) & (micro_index < MICRO)
        slot_index = jnp.clip(micro_index, 0, MICRO - 1)
        image_mask = lax.dynamic_index_in_dim(valid_img, slot_index, 1, keepdims=False)
        raw_input = lax.dynamic_index_in_dim(image_groups, slot_index, 1, keepdims=False).astype(
            jnp.float32
        )
        section_input = recv_main.astype(jnp.float32)
        positions = jnp.where(is_first, float(height * height), float(side * side))
        local_count = jnp.sum(image_mask) * positions
        local_total = jnp.where(
            is_first,
            jnp.pad(channel_sum(raw_input, image_mask), pad_width),
            channel_sum(section_input, image_mask),
        )
        total_sum, count_sum = lax.psum((local_total, local_count), "dp")
        channel_mean = total_sum / count_sum
        first_dev = raw_input - channel_mean[:c_in]
        rest_dev = section_input - channel_mean
        local_spread = jnp.where(
            is_first,
            jnp.pad(channel_sum(first_dev * first_dev, image_mask), pad_width),
            channel_sum(rest_dev * rest_dev, image_mask),
        )
        spread_sum = lax.psum(local_spread, "dp")
        variance = spread_sum / count_sum
        inv_std = lax.rsqrt(variance + EPSILON)
        sent_main, sent_side = lax.cond(
            is_first,
            forward_first,
            forward_rest,
            raw_input,
            section_input,
            recv_side,
            image_mask,
            channel_mean,
            inv_std,
        )
        old_out = lax.dynamic_index_in_dim(out_buf, slot_index, 0, keepdims=False)
        out_buf = lax.dynamic_update_index_in_dim(
            out_buf, jnp.where(active, sent_main, old_out), slot_index, 0
        )
        old_in = lax.dynamic_index_in_dim(in_buf, slot_index, 0, keepdims=False)
        in_buf = lax.dynamic_update_index_in_dim(
            in_buf, jnp.where(active, recv_main, old_in), slot_index, 0
        )
        moments = jnp.stack([channel_mean, inv_std])
        old_moment = lax.dynamic_index_in_dim(moment_buf, slot_index, 0, keepdims=False)
        moment_buf = lax.dynamic_update_index_in_dim(
            moment_buf, jnp.where(active, moments, old_moment), slot_index, 0
        )
        old_count = lax.dynamic_index_in_dim(count_buf, slot_index, 0, keepdims=False)
        count_buf = lax.dynamic_update_index_in_dim(
            count_buf, jnp.where(active, count_sum, old_count), slot_index, 0
        )
        recv_main, recv_side = (
            shifted(for_sending(sent_main), "section", 1).astype(sent_main.dtype),
            shifted(for_sending(sent_side), "section", 1).astype(sent_side.dtype),
        )
        return (recv_main, recv_side, out_buf, in_buf, moment_buf, count_buf)

    act_zeros = jnp.zeros((per_micro, side, side, c_out), jnp.bfloat16)
    forward_init = (
        act_zeros,
        act_zeros,
        jnp.zeros((MICRO, per_micro, side, side, c_out), jnp.bfloat16),
        jnp.zeros((MICRO, per_micro, side, side, c_out), jnp.bfloat16),
        jnp.zeros((MICRO, 2, c_out), jnp.float32),
        jnp.ones((MICRO,), jnp.float32),
    )
    forward_done = lax.fori_loop(0, tick_count, forward_tick, forward_init)
    out_buf, in_buf, moment_buf, count_buf = (
        forward_done[2],
        forward_done[3],
        forward_done[4],
        forward_done[5],
    )

    def backward_first(
        raw_input, section_input, grad_conv, grad_side, image_mask, channel_mean, inv_std
    ):
        scaled, pre_act = normalize(
            raw_input, channel_mean[:c_in], inv_std[:c_in], norm_gain[:c_in], norm_bias[:c_in]
        )
        activation = (jax.nn.silu(pre_act) * image_mask[:, None, None, None]).astype(jnp.bfloat16)
        kernel_part = conv_kernel_grad(activation, grad_conv, 2).reshape(9 * c_in, c_out)
        sub_grid = activation[:, 0::2, 0::2, :].reshape(-1, c_in)
        side_flat = grad_side.reshape(-1, c_out)
        proj_part = lax.dot_general(
            sub_grid, side_flat, (((0,), (0,)), ((), ())), preferred_element_type=jnp.float32
        )
        weight_part = jnp.concatenate(
            [kernel_part, proj_part, jnp.zeros((kernel_rows - 10 * c_in, c_out), jnp.float32)],
            axis=0,
        )
        sub_grad = lax.dot_general(
            side_flat, kernel_proj, (((1,), (1,)), ((), ())), preferred_element_type=jnp.float32
        )
        sub_grad = sub_grad.reshape(per_micro, side, side, c_in)
        spread_grad = lax.pad(
            sub_grad, jnp.float32(0.0), ((0, 0, 0), (0, 1, 1), (0, 1, 1), (0, 0, 0))
        )
        grad_first = conv_input_grad(grad_conv, kernel_first, 2) + spread_grad
        return (weight_part, grad_first, jnp.zeros((per_micro, side, side, c_out), jnp.float32))

    def backward_rest(
        raw_input, section_input, grad_conv, grad_side, image_mask, channel_mean, inv_std
    ):
        scaled, pre_act = normalize(section_input, channel_mean, inv_std, norm_gain, norm_bias)
        activation = (jax.nn.silu(pre_act) * image_mask[:, None, None, None]).astype(jnp.bfloat16)
        weight_part = conv_kernel_grad(activation, grad_conv, 1).reshape(kernel_rows, c_out)
        grad_rest = conv_input_grad(grad_conv, kernel_rest, 1)
        return (weight_part, jnp.zeros((per_micro, height, height, c_in), jnp.float32), grad_rest)

    def backward_tick(step_index, state_carry):
        recv_main, recv_side, weight_acc, gain_acc, bias_acc, input_buf = state_carry
        micro_index = step_index - (section_count - 1 - section_index)
        active = (micro_index >= 0) & (micro_index < MICRO)
        slot_index = jnp.clip(micro_index, 0, MICRO - 1)
        image_mask = lax.dynamic_index_in_dim(valid_img, slot_index, 1, keepdims=False)
        raw_input = lax.dynamic_index_in_dim(image_groups, slot_index, 1, keepdims=False).astype(
            jnp.float32
        )
        section_input = lax.dynamic_index_in_dim(in_buf, slot_index, 0, keepdims=False).astype(
            jnp.float32
        )
        moments = lax.dynamic_index_in_dim(moment_buf, slot_index, 0, keepdims=False)
        channel_mean, inv_std = (moments[0], moments[1])
        count_sum = lax.dynamic_index_in_dim(count_buf, slot_index, 0, keepdims=False)
        top_grad = jnp.where(
            is_last, lax.dynamic_index_in_dim(grad_groups, slot_index, 1, keepdims=False), recv_main
        )
        joined = (top_grad.astype(jnp.float32) + recv_side.astype(jnp.float32)).astype(jnp.bfloat16)
        grad_conv = jnp.where(adds_residual, joined, top_grad)
        grad_side = jnp.where(adds_residual, joined, recv_side)
        weight_part, grad_first, grad_rest = lax.cond(
            is_first,
            backward_first,
            backward_rest,
            raw_input,
            section_input,
            grad_conv,
            grad_side,
            image_mask,
            channel_mean,
            inv_std,
        )
        pre_first, scaled_first = norm_terms(
            grad_first,
            raw_input,
            image_mask,
            channel_mean[:c_in],
            inv_std[:c_in],
            norm_gain[:c_in],
            norm_bias[:c_in],
        )
        pre_rest, scaled_rest = norm_terms(
            grad_rest, section_input, image_mask, channel_mean, inv_std, norm_gain, norm_bias
        )
        local_pre = jnp.where(
            is_first,
            jnp.pad(jnp.sum(pre_first, axis=(0, 1, 2)), pad_width),
            jnp.sum(pre_rest, axis=(0, 1, 2)),
        )
        local_cross = jnp.where(
            is_first,
            jnp.pad(jnp.sum(pre_first * scaled_first, axis=(0, 1, 2)), pad_width),
            jnp.sum(pre_rest * scaled_rest, axis=(0, 1, 2)),
        )
        sum_pre, sum_cross = lax.psum((local_pre, local_cross), "dp")
        mean_pre = sum_pre / count_sum
        mean_cross = sum_cross / count_sum
        mask_four = image_mask[:, None, None, None]
        grad_in_rest = (
            mask_four * inv_std * norm_gain * (pre_rest - mean_pre - scaled_rest * mean_cross)
        )
        grad_in_first = (
            mask_four
            * inv_std[:c_in]
            * norm_gain[:c_in]
            * (pre_first - mean_pre[:c_in] - scaled_first * mean_cross[:c_in])
        )
        sent_main = jnp.where(
            merges_back, grad_in_rest + grad_side.astype(jnp.float32), grad_in_rest
        ).astype(jnp.bfloat16)
        sent_side = jnp.where(merges_back, jnp.zeros_like(grad_side), grad_side)
        weight_acc = weight_acc + jnp.where(active, weight_part, 0.0)
        gain_acc = gain_acc + jnp.where(active, sum_cross, 0.0)
        bias_acc = bias_acc + jnp.where(active, sum_pre, 0.0)
        old_input = lax.dynamic_index_in_dim(input_buf, slot_index, 0, keepdims=False)
        input_buf = lax.dynamic_update_index_in_dim(
            input_buf, jnp.where(active, grad_in_first, old_input), slot_index, 0
        )
        recv_main, recv_side = shifted((sent_main, sent_side), "section", -1)
        return (recv_main, recv_side, weight_acc, gain_acc, bias_acc, input_buf)

    backward_init = (
        act_zeros,
        act_zeros,
        jnp.zeros((kernel_rows, c_out), jnp.float32),
        jnp.zeros((c_out,), jnp.float32),
        jnp.zeros((c_out,), jnp.float32),
        jnp.zeros((MICRO, per_micro, height, height, c_in), jnp.float32),
    )
    backward_done = lax.fori_loop(0, tick_count, backward_tick, backward_init)
    weight_acc, gain_acc, bias_acc, input_buf = (
        backward_done[2],
        backward_done[3],
        backward_done[4],
        backward_done[5],
    )
    weight_total = lax.psum(weight_acc, "dp")
    input_full = jnp.transpose(input_buf, (1, 0, 2, 3, 4)).reshape(img_dev, height, height, c_in)
    input_full = jnp.where(is_first, input_full, 0.0)
    input_grad = lax.psum_scatter(
        input_full.astype(jnp.bfloat16), "section", scatter_dimension=1, tiled=True
    )
    section_outputs = jnp.transpose(out_buf, (1, 0, 2, 3, 4)).reshape(img_dev, side, side, c_out)[
        None
    ]
    return (section_outputs, input_grad, weight_total[None], gain_acc[None], bias_acc[None])


BF = jnp.bfloat16
F32 = jnp.float32
INF = float("inf")
MIB = 1024 * 1024
ANY = pl.BlockSpec(memory_space=pltpu.HBM)
FREE = pl.BlockSpec(memory_space=pl.ANY)
INSIDE = pl.BlockSpec(memory_space=pltpu.VMEM)
KEPT = pl.BlockSpec(memory_space=pltpu.VMEM)
SCALARS = pl.BlockSpec(memory_space=pltpu.SMEM)
FIELD = jax.ShapeDtypeStruct((512, 640), BF)
TWO = jax.ShapeDtypeStruct((2, 512, 640), BF)
PAIR = jax.ShapeDtypeStruct((2, 640), F32)
SUMS = jax.ShapeDtypeStruct((1920, 1920), F32)


def lane(k, first=0):
    return pl.ds(pl.multiple_of(first + 128 * k, 128), 128)


def from_left(values):
    column = lax.broadcasted_iota(jnp.int32, values.shape, 0) & 7
    return jnp.where(column == 0, 0.0, pltpu.roll(values, 1, 0))


def from_right(values):
    column = lax.broadcasted_iota(jnp.int32, values.shape, 0) & 7
    return jnp.where(column == 7, 0.0, pltpu.roll(values, values.shape[0] - 1, 0))


def total_of(values):
    return jnp.sum(values, axis=0, keepdims=True)


def count_of(valid):
    return total_of(jnp.where(valid, 1.0, 0.0))


def sigmoid(z):
    return 0.5 * jnp.tanh(0.5 * z) + 0.5


def matmul(a, b):
    return jnp.dot(a, b, preferred_element_type=F32)


def matmul_bt(a, b):
    return lax.dot_general(a, b, (((1,), (1,)), ((), ())), preferred_element_type=F32)


def matmul_at(a, b):
    return lax.dot_general(a, b, (((0,), (0,)), ((), ())), preferred_element_type=F32)


def start_all(copies):
    for one in copies:
        one.start()


def wait_all(copies):
    for one in copies:
        one.wait()


PINNED = {id(ANY): pltpu.HBM, id(KEPT): pltpu.VMEM}


def kernel_call(kernel, out_shape, in_specs, out_specs, scratch, aliases=None, flops=0, mib=18):
    outs = out_shape if isinstance(out_shape, tuple) else (out_shape,)
    specs = out_specs if isinstance(out_specs, tuple) else (out_specs,)
    outs = tuple(
        PINNED[id(spec)](one.shape, one.dtype) if id(spec) in PINNED else one for spec, one in zip(specs, outs)
    )
    call = pl.pallas_call(
        kernel,
        out_shape=outs,
        in_specs=in_specs,
        out_specs=specs,
        scratch_shapes=scratch,
        input_output_aliases=aliases or {},
        compiler_params=pltpu.CompilerParams(vmem_limit_bytes=mib * MIB),
        cost_estimate=pl.CostEstimate(flops=int(flops * 1.0), bytes_accessed=0, transcendentals=0),
    )

    def run(*args):
        args = [
            pltpu.with_memory_space_constraint(one, PINNED[id(spec)]) if id(spec) in PINNED else one
            for spec, one in zip(in_specs, args)
        ]
        results = call(*args)
        return results if isinstance(out_shape, tuple) else results[0]

    return run


def half_turn(values):
    return jnp.concatenate([values[:, 320:640], values[:, 0:320]], axis=1)


def twice(values):
    return jnp.concatenate([values[:, 0:320], values[:, 0:320]], axis=1)


def weight_first(w_ref, w_vm, sems):
    copies = []
    for p in range(3):
        copies.append(
            pltpu.make_async_copy(
                w_ref.at[pl.ds(960 * p + 320, 640)], w_vm.at[pl.ds(1024 * p, 640)], sems.at[2 * p]
            )
        )
        copies.append(
            pltpu.make_async_copy(
                w_ref.at[pl.ds(960 * p, 320)], w_vm.at[pl.ds(1024 * p + 704, 320)], sems.at[2 * p + 1]
            )
        )
        w_vm[1024 * p + 640 : 1024 * p + 704, :] = jnp.zeros((64, 640), BF)
    copies.append(pltpu.make_async_copy(w_ref.at[pl.ds(2880, 320)], w_vm.at[pl.ds(3072, 320)], sems.at[6]))
    w_vm[3392:3456, :] = jnp.zeros((64, 640), BF)
    return copies


def forward_first_kernel(
    flags, own, one, two, three, four, others, w_ref, gain, bias, out_ref, ring_ref, field_ref, stats_ref,
    w_vm, x_vm, cat, acc, part, sems, x_sems,
):
    @pl.when(flags[0] == 1)
    def _():
        pieces = [ref.at[0] for ref in (own, one, two, three, four)] + [others.at[k] for k in range(3)]
        in_x = []
        for k, piece in enumerate(pieces):
            slot = flags[1] ^ k
            for a in range(2):
                in_x.append(
                    pltpu.make_async_copy(piece.at[:, a], x_vm.at[a, :, slot], x_sems.at[2 * k + a])
                )
        start_all(in_x)
        in_w = weight_first(w_ref, w_vm, sems)
        start_all(in_w)
        cat[0:64, :] = jnp.zeros((64, 1024), BF)
        part[4:5, :] = twice(gain)
        part[5:6, :] = twice(bias)
        wait_all(in_x)

        @pl.loop(0, 5)
        def _(k):
            here = lane(k)
            x = x_vm[0, :, :, :, here].astype(F32).reshape(512, 128)
            y = x_vm[1, :, :, :, here].astype(F32).reshape(512, 128)
            field_ref[0, :, here] = x.astype(BF)
            field_ref[1, :, here] = y.astype(BF)
            valid = x < INF
            part[0:1, here] = total_of(jnp.where(valid, x + y, 0.0))
            part[2:3, here] = 4.0 * count_of(valid)

        part[0:1, :] = (part[0:1, :] + half_turn(part[0:1, :])) / part[2:3, :]

        @pl.loop(0, 5)
        def _(k):
            here = lane(k)
            x, y = field_ref[0, :, here].astype(F32), field_ref[1, :, here].astype(F32)
            valid = x < INF
            x = x - part[0:1, here]
            y = y - part[0:1, here]
            part[1:2, here] = total_of(jnp.where(valid, x * x + y * y, 0.0))

        part[1:2, :] = lax.rsqrt((part[1:2, :] + half_turn(part[1:2, :])) / part[2:3, :] + EPSILON)
        stats_ref[...] = part[0:2, :]

        @pl.loop(0, 5)
        def _(k):
            here = lane(k)
            for a in range(2):
                x = field_ref[a, :, here].astype(F32)
                z = (x - part[0:1, here]) * part[1:2, here] * part[4:5, here] + part[5:6, here]
                act = jnp.where(x < INF, z * sigmoid(z), 0.0)
                first = 576 if a == 0 else 64
                cat[first : first + 512, here] = act.astype(BF)

                @pl.when(k >= 2)
                def _():
                    cat[first : first + 512, lane(k, 384)] = from_left(act).astype(BF)

        keep = [
            pltpu.make_async_copy(cat.at[pl.ds(576, 512), pl.ds(0, 640)], ring_ref.at[0], x_sems.at[0]),
            pltpu.make_async_copy(cat.at[pl.ds(64, 512), pl.ds(0, 640)], ring_ref.at[1], x_sems.at[1]),
        ]
        start_all(keep)
        acc[...] = jnp.zeros((512, 640), F32)
        wait_all(in_w)

        @pl.loop(0, 3)
        def _(p):
            first = pl.multiple_of(jnp.where(p == 1, 576, 32 * p), 64)
            acc[...] += matmul(cat[pl.ds(first, 512), :], w_vm[pl.ds(pl.multiple_of(1024 * p, 1024), 1024), :])

        @pl.loop(0, 5)
        def _(k):
            row_valid = field_ref[0, :, 0:128].astype(F32) < INF
            out_ref[0, :, lane(k)] = jnp.where(row_valid, acc[:, lane(k)], INF).astype(BF)

        out_ref[1] = matmul(cat[576:1088, 0:384], w_vm[3072:3456, :]).astype(BF)
        wait_all(keep)


def forward_first(flags, pieces, weight, gain, bias):
    return kernel_call(
        forward_first_kernel,
        (TWO, TWO, TWO, PAIR),
        [SCALARS] + [FREE] * 6 + [ANY, INSIDE, INSIDE],
        (INSIDE, ANY, INSIDE, INSIDE),
        [
            pltpu.VMEM((3456, 640), BF),
            pltpu.VMEM((2, 8, 8, 8, 640), BF),
            pltpu.VMEM((1088, 1024), BF),
            pltpu.VMEM((512, 640), F32),
            pltpu.VMEM((8, 640), F32),
            pltpu.SemaphoreType.DMA((7,)),
            pltpu.SemaphoreType.DMA((16,)),
        ],
        flops=4_000_000_000,
    )(flags, *pieces, weight, gain, bias)


def weight_part(w_ref, w_vm, sems, p):
    rows = pl.ds(pl.multiple_of(1920 * p, 1920), 1920)
    return pltpu.make_async_copy(w_ref.at[rows], w_vm.at[rows], sems.at[p])


def clear_edges(x3):
    x3[0:64, :] = jnp.zeros((64, x3.shape[1]), BF)
    x3[576:640, :] = jnp.zeros((64, x3.shape[1]), BF)


def place(x3, k, values, left, right):
    x3[64:576, lane(k, left)] = from_left(values).astype(BF)
    x3[64:576, lane(k, 640)] = values.astype(BF)
    x3[64:576, lane(k, right)] = from_right(values).astype(BF)


def forward_conv(x3, w_ref, w_vm, w_sems, acc):
    @pl.loop(0, 3)
    def _(p):
        weight_part(w_ref, w_vm, w_sems, p).wait()
        acc[...] += matmul(
            x3[pl.ds(pl.multiple_of(64 * p, 64), 512), :], w_vm[pl.ds(pl.multiple_of(1920 * p, 1920), 1920), :]
        )


def statistics(x):
    valid = x < INF
    count = count_of(valid)
    mean = total_of(jnp.where(valid, x, 0.0)) / count
    centred = jnp.where(valid, x - mean, 0.0)
    inv = lax.rsqrt(total_of(centred * centred) / count + EPSILON)
    return valid, count, mean, inv, centred


def forward_rest_kernel(
    handed, flags, h, res, w_ref, gain, bias, out_ref, stats_ref, act_ref, w_vm, x3, acc, w_sems
):
    if not handed:
        h, res = h.at[0], res.at[1]

    @pl.when(flags[0] == 1)
    def _():
        for p in range(3):
            weight_part(w_ref, w_vm, w_sems, p).start()
        clear_edges(x3)

        @pl.loop(0, 5)
        def _(k):
            here = lane(k)
            valid, _, mean, inv, centred = statistics(h[:, here].astype(F32))
            stats_ref[0:1, here] = mean
            stats_ref[1:2, here] = inv
            z = centred * inv * gain[:, here] + bias[:, here]
            act = jnp.where(valid, z * sigmoid(z), 0.0)
            act_ref[:, here] = act.astype(BF)
            place(x3, k, act, 0, 1280)
            acc[:, here] = jnp.zeros((512, 128), F32) if handed else res[:, here].astype(F32)

        forward_conv(x3, w_ref, w_vm, w_sems, acc)

        @pl.loop(0, 5)
        def _(k):
            here = lane(k)
            row_valid = h[:, 0:128].astype(F32) < INF
            out = jnp.where(row_valid, acc[:, here], INF).astype(BF)
            if handed:
                out_ref[0, :, here] = out
                out_ref[1, :, here] = h[:, here]
            else:
                out_ref[:, here] = out


def forward_rest(flags, h, res, weight, gain, bias, handed=False):
    return kernel_call(
        lambda *refs: forward_rest_kernel(handed, *refs),
        (TWO if handed else FIELD, PAIR, FIELD),
        [SCALARS, INSIDE, INSIDE, ANY, INSIDE, INSIDE],
        (INSIDE, INSIDE, INSIDE),
        [
            pltpu.VMEM((5760, 640), BF),
            pltpu.VMEM((640, 1920), BF),
            pltpu.VMEM((512, 640), F32),
            pltpu.SemaphoreType.DMA((3,)),
        ],
        flops=4_000_000_000,
    )(flags, h, res, weight, gain, bias)


def forward_last_kernel(flags, act, pair, w_ref, out_ref, w_vm, x3, acc, w_sems):
    @pl.when(flags[0] == 1)
    def _():
        for p in range(3):
            weight_part(w_ref, w_vm, w_sems, p).start()
        clear_edges(x3)

        @pl.loop(0, 5)
        def _(k):
            place(x3, k, act[:, lane(k)].astype(F32), 0, 1280)
            acc[:, lane(k)] = pair[1, :, lane(k)].astype(F32)

        forward_conv(x3, w_ref, w_vm, w_sems, acc)

        @pl.loop(0, 5)
        def _(k):
            row_valid = pair[0, :, 0:128].astype(F32) < INF
            out_ref[:, lane(k)] = jnp.where(row_valid, acc[:, lane(k)], INF).astype(BF)


def forward_last(flags, act, pair, weight):
    return kernel_call(
        forward_last_kernel,
        FIELD,
        [SCALARS, INSIDE, INSIDE, ANY],
        INSIDE,
        [
            pltpu.VMEM((5760, 640), BF),
            pltpu.VMEM((640, 1920), BF),
            pltpu.VMEM((512, 640), F32),
            pltpu.SemaphoreType.DMA((3,)),
        ],
        flops=4_000_000_000,
    )(flags, act, pair, weight)


def by_row(values):
    return values.transpose(1, 0, 2, 3).reshape(512, values.shape[3])


def backward_conv(g3, w_ref, w_vm, w_sems, acc):
    @pl.loop(0, 3)
    def _(p):
        weight_part(w_ref, w_vm, w_sems, p).wait()

        @pl.loop(0, 3)
        def _(q):
            acc[...] += matmul_bt(
                g3[pl.ds(pl.multiple_of(64 * (2 - p), 64), 512), pl.ds(pl.multiple_of(640 * q, 640), 640)],
                w_vm[pl.ds(pl.multiple_of(640 * (3 * p + q), 640), 640), :],
            )


def backward_conv_turned(g3, w_ref, w_vm, w_sems, acc):
    @pl.loop(0, 3)
    def _(p):
        weight_part(w_ref, w_vm, w_sems, p).wait()
        acc[...] += matmul(
            g3[pl.ds(pl.multiple_of(64 * (2 - p), 64), 512), :],
            w_vm[pl.ds(pl.multiple_of(1920 * p, 1920), 1920), :],
        )


def backward_top_kernel(flags, g_ref, w_ref, total_ref, own_ref, w_vm, g3, w_sems):
    for p in range(3):
        weight_part(w_ref, w_vm, w_sems, p).start()
    clear_edges(g3)

    @pl.loop(0, 5)
    def _(k):
        here = lane(k)
        g = by_row(g_ref[:, :, :, here].astype(F32))
        own_ref[:, here] = g.astype(BF)
        place(g3, k, g, 1280, 0)
        total_ref[:, here] = jnp.zeros((512, 128), F32)

    backward_conv(g3, w_ref, w_vm, w_sems, total_ref)


def backward_top(flags, g, weight):
    return kernel_call(
        backward_top_kernel,
        (jax.ShapeDtypeStruct((512, 640), F32), FIELD),
        [SCALARS, INSIDE, ANY],
        (INSIDE, INSIDE),
        [
            pltpu.VMEM((5760, 640), BF),
            pltpu.VMEM((640, 1920), BF),
            pltpu.SemaphoreType.DMA((3,)),
        ],
        flops=4_000_000_000,
    )(flags, g, weight)


def norm_back(grad, valid, count, centred, inv, scale, offset, sums_ref, here):
    xhat = centred * inv
    z = xhat * scale + offset
    sig = sigmoid(z)
    dz = jnp.where(valid, grad * sig * (1.0 + z * (1.0 - sig)), 0.0)
    s1 = total_of(dz)
    s2 = total_of(dz * xhat)
    sums_ref[0:1, here] = s1
    sums_ref[1:2, here] = s2
    back = scale * inv * (dz - s1 / count - xhat * (s2 / count))
    return jnp.where(valid, back, 0.0), jnp.where(valid, z * sig, 0.0)


def turn_kernel(flags, pair, grad, gain, bias, out_ref, sums_ref, act_ref):
    @pl.when(flags[0] == 1)
    def _():
        @pl.loop(0, 5)
        def _(k):
            here = lane(k)
            valid, count, _, inv, centred = statistics(pair[0, :, here].astype(F32))
            back, act = norm_back(
                grad[:, here], valid, count, centred, inv, gain[:, here], bias[:, here], sums_ref, here
            )
            act_ref[:, here] = act.astype(BF)
            out_ref[:, here] = back.astype(BF)


def turn(flags, h, grad, gain, bias):
    return kernel_call(
        turn_kernel,
        (FIELD, PAIR, FIELD),
        [SCALARS] + [INSIDE] * 4,
        (INSIDE, INSIDE, INSIDE),
        [],
        flops=1_000_000_000,
    )(flags, h, grad, gain, bias)


def backward_rest_kernel(
    handed, flags, g_ref, add, h, stats, w_ref, gain, bias, out_ref, sums_ref, w_vm, g3, acc, w_sems
):
    if handed:
        h = h.at[0]

    @pl.when(flags[0] == 1)
    def _():
        for p in range(3):
            weight_part(w_ref, w_vm, w_sems, p).start()
        clear_edges(g3)

        @pl.loop(0, 5)
        def _(k):
            place(g3, k, g_ref[:, lane(k)].astype(F32), 1280, 0)
            acc[:, lane(k)] = jnp.zeros((512, 128), F32)

        backward_conv_turned(g3, w_ref, w_vm, w_sems, acc)
        @pl.loop(0, 5)
        def _(k):
            here = lane(k)
            x = h[:, here].astype(F32)
            valid = x < INF
            centred = jnp.where(valid, x - stats[0:1, here], 0.0)
            back, _ = norm_back(
                acc[:, here], valid, count_of(valid), centred, stats[1:2, here], gain[:, here], bias[:, here],
                sums_ref, here,
            )
            if handed:
                out_ref[0, :, here] = back.astype(BF)
                out_ref[1, :, here] = g_ref[:, here]
            else:
                out_ref[:, here] = (back + by_row(add[:, :, :, here].astype(F32))).astype(BF)


def backward_rest(flags, g, add, h, stats, weight, gain, bias, handed=False):
    return kernel_call(
        lambda *refs: backward_rest_kernel(handed, *refs),
        (TWO if handed else FIELD, PAIR),
        [SCALARS, INSIDE, INSIDE, INSIDE, INSIDE, ANY, INSIDE, INSIDE],
        (INSIDE, INSIDE),
        [
            pltpu.VMEM((5760, 640), BF),
            pltpu.VMEM((640, 1920), BF),
            pltpu.VMEM((512, 640), F32),
            pltpu.SemaphoreType.DMA((3,)),
        ],
        flops=4_000_000_000,
    )(flags, g, add, h, stats, weight, gain, bias)


def backward_first_conv_kernel(flags, pair, w_ref, acc, w_vm, g2, sems):
    in_w = weight_first(w_ref, w_vm, sems)
    start_all(in_w)
    g2[512:576, :] = jnp.zeros((64, 1280), BF)

    @pl.loop(0, 5)
    def _(k):
        g = pair[0, :, lane(k)].astype(F32)
        g2[0:512, lane(k)] = g.astype(BF)
        g2[0:512, lane(k, 640)] = from_right(g).astype(BF)

    acc[...] = jnp.zeros((2, 512, 640), F32)
    wait_all(in_w)

    @pl.loop(0, 3)
    def _(p):
        rows = pl.ds(pl.multiple_of(jnp.where(p == 0, 64, 0), 64), 512)
        a = jnp.where(p == 1, 0, 1)
        first = pl.multiple_of(1024 * p, 1024)
        acc[a] += matmul_bt(g2[rows, 0:640], w_vm[pl.ds(first, 640), :])
        acc[a, :, 256:640] += matmul_bt(g2[rows, 640:1280], w_vm[pl.ds(first + 640, 384), :])

    acc[0, :, 0:384] += matmul_bt(pair[1], w_vm[3072:3456, :])


def backward_first_conv(flags, pair, weight):
    return kernel_call(
        backward_first_conv_kernel,
        jax.ShapeDtypeStruct((2, 512, 640), F32),
        [SCALARS, INSIDE, ANY],
        INSIDE,
        [
            pltpu.VMEM((3456, 640), BF),
            pltpu.VMEM((576, 1280), BF),
            pltpu.SemaphoreType.DMA((7,)),
        ],
        flops=5_000_000_000,
    )(flags, pair, weight)


def backward_first_norm_kernel(flags, acc, x_ref, stats, gain, bias, out_ref, sums_ref, dz_vm, part):
    part[4:5, :] = twice(gain)
    part[5:6, :] = twice(bias)

    @pl.loop(0, 5)
    def _(k):
        here = lane(k)
        s1 = s2 = 0.0
        for a in range(2):
            x = x_ref[a, :, here].astype(F32)
            valid = x < INF
            xhat = jnp.where(valid, x - stats[0:1, here], 0.0) * stats[1:2, here]
            z = xhat * part[4:5, here] + part[5:6, here]
            sig = sigmoid(z)
            dz = jnp.where(valid, acc[a, :, here] * sig * (1.0 + z * (1.0 - sig)), 0.0)
            dz_vm[a, :, here] = dz
            s1 = s1 + total_of(dz)
            s2 = s2 + total_of(dz * xhat)
        part[0:1, here] = s1
        part[1:2, here] = s2
        part[2:3, here] = 4.0 * count_of(valid)

    part[0:1, :] = part[0:1, :] + half_turn(part[0:1, :])
    part[1:2, :] = part[1:2, :] + half_turn(part[1:2, :])
    sums_ref[...] = jnp.where(lax.broadcasted_iota(jnp.int32, (2, 640), 1) < 320, part[0:2, :], 0.0)

    @pl.loop(0, 5)
    def _(k):
        here = lane(k)
        count = part[2:3, here]
        scale = part[4:5, here] * stats[1:2, here]
        for a in range(2):
            x = x_ref[a, :, here].astype(F32)
            xhat = (x - stats[0:1, here]) * stats[1:2, here]
            back = scale * (dz_vm[a, :, here] - part[0:1, here] / count - xhat * (part[1:2, here] / count))
            back = jnp.where(x < INF, back, 0.0).reshape(4, 2, 8, 8, 128).transpose(2, 0, 1, 3, 4)
            out_ref[:, :, :, a, :, here] = back.astype(BF)


def backward_first_norm(flags, field, x, stats, gain, bias):
    return kernel_call(
        backward_first_norm_kernel,
        (jax.ShapeDtypeStruct((8, 4, 2, 2, 8, 640), BF), PAIR),
        [SCALARS, INSIDE, INSIDE, INSIDE, INSIDE, INSIDE],
        (INSIDE, INSIDE),
        [pltpu.VMEM((2, 512, 640), F32), pltpu.VMEM((8, 640), F32)],
        flops=1_000_000_000,
    )(flags, field, x, stats, gain, bias)


def send_sides(side, rows, sent_ref):
    sent_ref[0:320, :] = side.astype(BF)
    for k in range(3):
        piece = rows.astype(BF)
        sent_ref[320 + 2 * k : 322 + 2 * k, :] = piece
        rows = rows - piece.astype(F32)
    sent_ref[326:336, :] = jnp.zeros((10, 640), BF)


def projection_grad_kernel(flags, ring_ref, pair_ref, rows, out_ref, rows_ref, sent_ref, a_vm, g_vm, sems):
    ins = [
        pltpu.make_async_copy(ring_ref.at[0], a_vm, sems.at[0]),
        pltpu.make_async_copy(pair_ref.at[1], g_vm, sems.at[1]),
    ]
    start_all(ins)
    wait_all(ins)
    side = matmul_at(a_vm[:, 0:384], g_vm[...])[0:320, :]
    out_ref[...] = side
    rows_ref[...] = rows[...]
    send_sides(side, rows[...], sent_ref)


SIDES = (jax.ShapeDtypeStruct((320, 640), F32), PAIR, jax.ShapeDtypeStruct((336, 640), BF))


def projection_grad(flags, ring, pair, rows):
    return kernel_call(
        projection_grad_kernel,
        SIDES,
        [SCALARS, FREE, FREE, INSIDE],
        (INSIDE, INSIDE, INSIDE),
        [pltpu.VMEM((512, 640), BF), pltpu.VMEM((512, 640), BF), pltpu.SemaphoreType.DMA((2,))],
        flops=200_000_000,
        mib=8,
    )(flags, ring, pair, rows)


def add_sides_kernel(side, rows, got, out_ref, rows_ref, sent_ref):
    side = side[...] + got[0:320, :].astype(F32)
    rows = rows[...]
    for k in range(3):
        rows = rows + got[320 + 2 * k : 322 + 2 * k, :].astype(F32)
    out_ref[...] = side
    rows_ref[...] = rows
    send_sides(side, rows, sent_ref)


def add_sides(side, rows, got):
    return kernel_call(
        add_sides_kernel, SIDES, [INSIDE, INSIDE, INSIDE], (INSIDE, INSIDE, INSIDE), [], mib=8
    )(side, rows, got)


def ring_value_kernel(g, sums, out_ref):
    out_ref[0:512, :] = g[...]
    rows = sums[...]
    pieces = []
    for _ in range(3):
        pieces.append(rows.astype(BF).astype(F32))
        rows = rows - pieces[-1]
    out_ref[512:528, :] = jnp.concatenate([*pieces, jnp.zeros((10, 640), F32)], axis=0).astype(BF)


def ring_value(g, sums):
    return kernel_call(
        ring_value_kernel, jax.ShapeDtypeStruct((528, 640), BF), [INSIDE, INSIDE], INSIDE, [], mib=8
    )(g, sums)


def add_rows_kernel(first, *refs):
    blocks, out_ref, rows, sems = refs[:8], refs[8], refs[9], refs[10]
    copies = [
        pltpu.make_async_copy(blocks[b].at[pl.ds(first, 16)], rows.at[b], sems.at[b]) for b in range(8)
    ]
    start_all(copies)
    wait_all(copies)
    total = rows[0].astype(F32)
    for b in range(1, 8):
        total = total + rows[b].astype(F32)
    out_ref[...] = total[0:2, :] + total[2:4, :] + total[4:6, :]


def add_rows(blocks, first):
    return kernel_call(
        lambda *refs: add_rows_kernel(first, *refs),
        PAIR,
        [FREE] * 8,
        INSIDE,
        [pltpu.VMEM((8, 16, 640), BF), pltpu.SemaphoreType.DMA((8,))],
        mib=8,
    )(*blocks)


def kernel_grads_kernel(blocks, fresh, last, *refs):
    acts, gs = refs[:blocks], refs[blocks : 2 * blocks]
    refs = refs[2 * blocks :]
    gs = [one.at[pl.ds(512 if one.shape[0] == 1040 else 0, 512)] for one in gs]
    acts = [one.at[pl.ds(0, 512)] for one in acts]
    if not fresh:
        kept, refs = refs[0], refs[1:]
    sums, a_vm, g_vm, g3, sems = refs[0], *refs[-4:]
    if last:
        out_ref, out_sems = refs[0], refs[1]
        sums = kept
    ins = []
    for b in range(blocks):
        ins.append(pltpu.make_async_copy(gs[b], g_vm.at[b], sems.at[b, 0]))
        ins.append(pltpu.make_async_copy(acts[b], a_vm.at[b], sems.at[b, 1]))
    start_all(ins)

    @pl.loop(0, blocks)
    def _(b):
        clear_edges(g3.at[b])

    @pl.loop(0, blocks)
    def _(b):
        pltpu.make_async_copy(gs[0], g_vm.at[b], sems.at[b, 0]).wait()

        @pl.loop(0, 5)
        def _(k):
            place(g3.at[b], k, g_vm[b, :, lane(k)].astype(F32), 1280, 0)

    wait_all(ins[1::2])

    def outs(p):
        rows = pl.ds(pl.multiple_of(640 * p, 640), 640)
        return [
            pltpu.make_async_copy(
                sums.at[rows, pl.ds(640 * q, 640)],
                out_ref.at[pl.ds(pl.multiple_of(640 * (3 * p + q), 640), 640)],
                out_sems.at[p, q],
            )
            for q in range(3)
        ]

    @pl.loop(0, 3)
    def _(p):
        rows = pl.ds(pl.multiple_of(640 * p, 640), 640)
        here = pl.ds(pl.multiple_of(64 * (2 - p), 64), 512)
        if fresh:
            sums[rows, :] = jnp.zeros((640, 1920), F32)
        elif not last:
            sums[rows, :] = kept[rows, :]

        @pl.loop(0, blocks)
        def _(b):
            sums[rows, :] += matmul_at(a_vm[b], g3[b, here, :])

        if last:
            start_all(outs(p))

    if last:
        for p in range(3):
            wait_all(outs(p))


def kernel_grads_first_kernel(blocks, fresh, last, *refs):
    acts, gs = refs[:blocks], refs[blocks : 2 * blocks]
    refs = refs[2 * blocks :]
    if last:
        side, refs = refs[0], refs[1:]
    if not fresh:
        kept, refs = refs[0], refs[1:]
    sums, a_vm, g_vm, g2, sems = refs[0], *refs[-4:]
    extra = []
    if last:
        out_ref, zeros, out_sems, extra_sems = refs[:4]
        sums = kept
    ins = []
    for b in range(blocks):
        ins.append(pltpu.make_async_copy(gs[b].at[pl.ds(0, 512)], g_vm.at[b], sems.at[b, 0]))
        ins.append(pltpu.make_async_copy(acts[b], a_vm.at[b], sems.at[b, 1]))
    start_all(ins)
    if last:
        zeros[...] = jnp.zeros((320, 640), F32)
        extra.append(pltpu.make_async_copy(side, out_ref.at[pl.ds(2880, 320)], extra_sems.at[0]))
        for k in range(8):
            extra.append(pltpu.make_async_copy(zeros, out_ref.at[pl.ds(3200 + 320 * k, 320)], extra_sems.at[1 + k]))
        start_all(extra)
    @pl.loop(0, blocks)
    def _(b):
        g2[b, 512:576, :] = jnp.zeros((64, 1280), BF)
        pltpu.make_async_copy(gs[0].at[pl.ds(0, 512)], g_vm.at[b], sems.at[b, 0]).wait()

        @pl.loop(0, 5)
        def _(k):
            g = g_vm[b, :, lane(k)].astype(F32)
            g2[b, 0:512, lane(k)] = g.astype(BF)
            g2[b, 0:512, lane(k, 640)] = from_right(g).astype(BF)

    wait_all(ins[1::2])

    def outs(p):
        low = pl.multiple_of(640 * p, 640)
        return [
            pltpu.make_async_copy(
                sums.at[pl.ds(low, 640), pl.ds(0, 640)],
                out_ref.at[pl.ds(pl.multiple_of(960 * p + 320, 320), 640)],
                out_sems.at[p, 0],
            ),
            pltpu.make_async_copy(
                sums.at[pl.ds(low, 320), pl.ds(640, 640)],
                out_ref.at[pl.ds(pl.multiple_of(960 * p, 320), 320)],
                out_sems.at[p, 1],
            ),
        ]

    @pl.loop(0, 3)
    def _(p):
        here = pl.ds(pl.multiple_of(jnp.where(p == 0, 64, 0), 64), 512)
        low = pl.multiple_of(640 * p, 640)
        odd = jnp.where(p == 1, 0, 1)
        if fresh:
            sums[pl.ds(low, 640), :] = jnp.zeros((640, 1280), F32)
        elif not last:
            sums[pl.ds(low, 640), :] = kept[pl.ds(low, 640), :]

        @pl.loop(0, blocks)
        def _(b):
            sums[pl.ds(low, 640), 0:640] += matmul_at(a_vm[b, odd], g2[b, here, 0:640])
            left = matmul_at(a_vm[b, odd, :, 256:640], g2[b, here, 640:1280])
            sums[pl.ds(low, 320), 640:1280] += left[64:384, :]

        if last:
            start_all(outs(p))

    if last:
        for p in range(3):
            wait_all(outs(p))
    wait_all(extra)


def kernel_grads(acts, gs, kept=None, last=False, first=False, side=None):
    blocks = len(acts)
    fresh = kept is None
    scratch = []
    if last and first:
        scratch += [pltpu.VMEM((320, 640), F32)]
    if last:
        scratch += [pltpu.SemaphoreType.DMA((3, 3))]
    if last and first:
        scratch += [pltpu.SemaphoreType.DMA((9,))]
    scratch += [
        pltpu.VMEM((blocks, 2, 512, 640) if first else (blocks, 512, 640), BF),
        pltpu.VMEM((blocks, 512, 640), BF),
        pltpu.VMEM((blocks, 576, 1280) if first else (blocks, 640, 1920), BF),
        pltpu.SemaphoreType.DMA((blocks, 2)),
    ]
    extra = [side] if last and first else []
    count = 2 * blocks + len(extra)
    kernel = kernel_grads_first_kernel if first else kernel_grads_kernel
    sums = jax.ShapeDtypeStruct((1920, 1280 if first else 1920), F32)
    return kernel_call(
        lambda *refs: kernel(blocks, fresh, last, *refs),
        jax.ShapeDtypeStruct((5760, 640), F32) if last else sums,
        [FREE] * count + ([] if fresh else [KEPT]),
        ANY if last else KEPT,
        scratch,
        aliases={} if fresh or last else {count: 0},
        flops=4_000_000_000 * blocks,
        mib=20,
    )(*acts, *gs, *extra, *([] if fresh else [kept]))


def empty(shapes):
    return pl.pallas_call(
        lambda *refs: None,
        out_shape=tuple(shapes),
        out_specs=tuple(ANY for _ in shapes),
    )()


BOTH = ("dp", "section")
RING = (0, 2, 4, 6, 7, 5, 3, 1)


def move(value, triples):
    count = lax.axis_size("section")
    return lax.ppermute(value, BOTH, [(d * count + s, e * count + t) for (d, s), (e, t) in triples])


def hop(value, source, target):
    return move(value, [((d, source), (d, target)) for d in range(MICRO)])


class Ring:
    def __init__(self, value, sections):
        self.up = [((RING[k], s), (RING[(k + 1) % 8], s)) for k in range(8) for s in sections]
        self.down = [(b, a) for a, b in self.up]
        self.blocks = [value]

    def step(self, last_down=False):
        count = len(self.blocks)
        high = self.blocks[max(0, count - 2)]
        low = self.blocks[count - 1]
        if count < 7 or not last_down:
            self.blocks.append(move(high, self.up))
        if count < 7 or last_down:
            self.blocks.append(move(low, self.down))


def dp_total(value, sections):
    for k in (1, 2, 4):
        value = value + move(value, [((d, s), (d ^ k, s)) for d in range(MICRO) for s in sections])
    return value


def after(value, *others):
    return lax.optimization_barrier((value, *others))[0]


def pick(images, image_count, index):
    image = lax.dynamic_index_in_dim(images, index, 0)
    return jnp.where(index < image_count, image, INF).reshape(1, 8, 2, 8, 640)


def exchange_images(images, image_count, row, section, offsets):
    return [
        move(pick(images, image_count, row ^ k), [((d, section), (d ^ k, section)) for d in range(MICRO)])
        for k in offsets
    ]


SLOTS = jax.ShapeDtypeStruct((8, 8, 8, 640), BF)
PARTS = jax.ShapeDtypeStruct((4, 8, 2, 2, 8, 640), BF)


SLOTS = jax.ShapeDtypeStruct((8, 8, 8, 640), BF)
PARTS = jax.ShapeDtypeStruct((8, 4, 2, 2, 8, 640), BF)


def by_micro_batch(images, image_counts, conv_weight, bn_gain, bn_bias, out_grad):
    section = lax.axis_index("section")
    row = lax.axis_index("dp")
    weight = conv_weight[0]
    norm = (bn_gain, bn_bias)
    plain, adds = jnp.array([1, 0], jnp.int32), jnp.array([1, 1], jnp.int32)

    def segment(shapes, *branches):
        def whole(branch):
            def run():
                found = branch()
                missing = [name for name in shapes if name not in found]
                if missing:
                    found.update(zip(missing, empty([shapes[name] for name in missing])))
                return [found[name] for name in shapes]

            return run

        return dict(zip(shapes, lax.switch(section, [whole(branch) for branch in branches])))

    def on_section(first, second, third, fourth):
        return jnp.where(
            section == 0, first, jnp.where(section == 1, second, jnp.where(section == 2, third, fourth))
        )

    def nothing():
        return {}

    def named(prefix, blocks):
        return {f"{prefix}{k}": one for k, one in enumerate(blocks)}

    def listed(found, prefix, count):
        return [found[f"{prefix}{k}"] for k in range(count)]

    def many(prefix, count, shape):
        return {f"{prefix}{k}": shape for k in range(count)}

    def exchange(value):
        return lax.all_to_all(value, "dp", 0, 0, tiled=True)

    def resume(value, blocks, index):
        ring = Ring(value, (index,))
        ring.blocks += blocks
        return ring

    def shown(value):
        return jnp.where(value < INF, value, 0.0).reshape(8, 8, 8, 640).transpose(1, 0, 2, 3)

    count = image_counts[0]
    piece = jax.ShapeDtypeStruct((1, 8, 2, 8, 640), BF)
    grad_shape = jax.ShapeDtypeStruct((512, 640), F32)

    def zero_0():
        got = exchange_images(images, count, row, 0, (4, 3, 2, 1))
        return {"p0": pick(images, count, row), "p1": got[3], "p2": got[2], "p3": got[1], "p4": got[0]}

    def zero_1():
        return {"others": jnp.concatenate(exchange_images(images, count, row, 1, (5, 6, 7)), axis=0)}

    def zero_2():
        return {"top": exchange(out_grad)}

    def zero_3():
        grad, own = backward_top(plain, exchange(out_grad), weight)
        return {"grad": grad, "own": own}

    zeroth = segment(
        {
            **{f"p{k}": piece for k in range(5)}, "others": jax.ShapeDtypeStruct((3, 8, 2, 8, 640), BF),
            "top": SLOTS, "grad": grad_shape, "own": FIELD,
        },
        zero_0, zero_1, zero_2, zero_3,
    )
    others = hop(zeroth["others"], 1, 0)

    def one_0():
        pieces = (*[zeroth[f"p{k}"] for k in range(5)], others)
        pair, ring, fields, stats = forward_first(
            jnp.stack([jnp.int32(1), row.astype(jnp.int32)]), pieces, weight, *norm
        )
        return {"pair": pair, "ring": ring, "fields": fields, "stats": stats}

    def turn_weight(weight):
        return weight.reshape(9, 640, 640).transpose(0, 2, 1).reshape(5760, 640)

    def turned():
        return {"weight": turn_weight(weight)}

    first = segment(
        {"weight": jax.ShapeDtypeStruct((5760, 640), BF), "pair": TWO, "ring": TWO, "fields": TWO, "stats": PAIR},
        one_0, nothing, turned, nothing,
    )
    h1_in = hop(first["pair"], 0, 1)

    def two_1():
        y1, stats, act = forward_rest(adds, h1_in, h1_in, weight, *norm)
        return {"y1": y1, "stats": stats, "act": act}

    second = segment(
        {"y1": FIELD, "act": FIELD, "stats": PAIR}, nothing, two_1, nothing, nothing
    )
    y1_in = hop(second["y1"], 1, 2)

    def turned_1():
        return {"weight": turn_weight(after(weight, second["y1"]))}

    wait_2 = segment({"weight": jax.ShapeDtypeStruct((5760, 640), BF)}, nothing, turned_1, nothing, nothing)
    y1_in = after(y1_in, wait_2["weight"])

    def three_2():
        pair, stats, act = forward_rest(plain, y1_in, y1_in, weight, *norm, handed=True)
        return {"pair": pair, "stats": stats, "act": act}

    third = segment({"pair": TWO, "act": FIELD, "stats": PAIR}, nothing, nothing, three_2, nothing)
    h3_in = hop(third["pair"], 2, 3)

    def four_3():
        g_h3, sums, act = turn(plain, h3_in, zeroth["grad"], *norm)
        return {"g": g_h3, "sums": sums, "act": act}

    fourth = segment({"g": FIELD, "act": FIELD, "sums": PAIR}, nothing, nothing, nothing, four_3)
    g_h3_in = hop(fourth["g"], 3, 2)

    def five_2():
        g_y1, sums = backward_rest(adds, g_h3_in, zeroth["top"], y1_in, third["stats"], first["weight"], *norm)
        return {"g": g_y1, "sums": sums}

    fifth = segment({"g": FIELD, "sums": PAIR}, nothing, nothing, five_2, nothing)
    g_y1_in = hop(fifth["g"], 2, 1)

    def one_step(value, index, beside):
        value = after(value, fifth["g"])
        ring = Ring(value, (index,))
        ring.step()
        ring.step()
        return {"out": beside(value), **named("u", ring.blocks)}

    wait_5 = segment(
        {"out": SLOTS, **many("u", 5, FIELD)},
        lambda: {"out": shown(after(first["pair"], fifth["g"])[0])},
        lambda: one_step(second["act"], 1, lambda _: shown(second["y1"])),
        lambda: one_step(third["act"], 2, lambda _: shown(third["pair"][0])),
        lambda: one_step(fourth["act"], 3, lambda act: shown(forward_last(plain, act, h3_in, weight))),
    )
    g_y1_in = after(g_y1_in, wait_5["u0"])

    def six_0():
        ring = Ring(first["ring"], (0,))
        ring.step()
        ring.step()
        return named("a", ring.blocks)

    def six_1():
        pair, sums = backward_rest(
            plain, g_y1_in, zeroth["top"], h1_in, second["stats"], wait_2["weight"], *norm, handed=True
        )
        return {"pair": pair, "sums": sums}

    sixth = segment(
        {"pair": TWO, "sums": PAIR, **many("a", 5, TWO)}, six_0, six_1, nothing, nothing
    )
    pair_sent = hop(sixth["pair"], 1, 0)

    def seven_0():
        ring = Ring(after(sixth["a0"], sixth["pair"]), (0,))
        ring.blocks = listed(sixth, "a", 5)
        ring.blocks[3] = after(ring.blocks[3], sixth["pair"])
        ring.step()
        return named("a", ring.blocks[5:])

    def seven_1():
        return {"g": ring_value(after(g_y1_in, sixth["pair"]), sixth["sums"])}

    def seven_2():
        return {"g": ring_value(g_h3_in, fifth["sums"])}

    def seven_3():
        return {"g": ring_value(zeroth["own"], fourth["sums"])}

    tall = jax.ShapeDtypeStruct((528, 640), BF)
    seventh = segment({"g": tall, **many("a", 2, TWO)}, seven_0, seven_1, seven_2, seven_3)

    pair_in = after(pair_sent, seventh["g"])

    def work(ring, late):
        gs, acts = ring.blocks, late.blocks
        total = None
        for low, high in ((0, 3), (3, 5), (5, 7)):
            ring.step()
            if low > 0:
                late.step(True)
            total = kernel_grads(acts[low:high], gs[low:high], total)
            if low < 5:
                gs[high : high + 2], acts[high:], total = lax.optimization_barrier(
                    (gs[high : high + 2], acts[high:], total)
                )
        return kernel_grads(acts[7:8], gs[7:8], total, True)

    def eight_0():
        fence = lax.optimization_barrier
        ring = Ring(pair_in[0], (0,))
        ring.step()
        field = backward_first_conv(plain, pair_in, weight)
        parts, sums = backward_first_norm(plain, field, first["fields"], first["stats"], *norm)
        gs = ring.blocks
        sums, gs[1:3] = fence((sums, gs[1:3]))
        side, rows, sent = projection_grad(plain, first["ring"], pair_in, sums)

        def to(k):
            return move(sent, [((d, 0), (d ^ k, 0)) for d in range(MICRO)])

        got = to(1)
        parts = exchange(after(parts, sent))
        late = Ring(sixth["a0"], (0,))
        late.blocks = acts = listed(sixth, "a", 5) + listed(seventh, "a", 2)
        ring.step()
        side, rows, sent = add_sides(side, rows, got)
        got = to(2)
        acts[0] = after(acts[0], side)
        total = kernel_grads(acts[0:3], gs[0:3], first=True)
        gs[3:5], acts[3:], total = fence((gs[3:5], acts[3:], total))
        ring.step()
        late.step(True)
        total = kernel_grads(acts[3:5], gs[3:5], total, first=True)
        gs[5:7], got, total = fence((gs[5:7], got, total))
        ring.step()
        side, rows, sent = add_sides(side, rows, got)
        got = to(4)
        acts[5] = after(acts[5], side)
        total = kernel_grads(acts[5:7], gs[5:7], total, first=True)
        got, total = fence((got, total))
        side, rows, _ = add_sides(side, rows, got)
        total = kernel_grads(acts[7:8], gs[7:8], total, True, True, side)
        parts, total = fence((parts, total))
        return [parts, total, rows]

    def eight_rest():
        gs = Ring(seventh["g"], (1, 2, 3))
        gs.step()
        acts = Ring(wait_5["u0"], (1, 2, 3))
        acts.blocks = listed(wait_5, "u", 5)
        total = work(gs, acts)
        return [*empty([PARTS]), total, add_rows(gs.blocks, 512)]

    parts, grads, sums = lax.cond(section > 0, eight_rest, eight_0)

    mine = parts[:, 0]
    for k in range(1, 4):
        mine = jnp.where(section == k, hop(parts[:, k], 0, k), mine)
    out = exchange(after(wait_5["out"], sums))
    return (out[None], mine.reshape(8, 4, 16, 320), grads[None], sums[1:2], sums[0:1])


def solution(mesh):
    one_each = mesh.shape["dp"] == MICRO and mesh.shape["section"] == 4

    def on_device(images, *rest):
        if one_each and images.shape == (MICRO, 16, 16, 320):
            return by_micro_batch(images, *rest)
        return pipelined(images, *rest)

    return jax.shard_map(
        on_device,
        mesh=mesh,
        in_specs=(
            P("dp", None, None, None),
            P("dp"),
            P("section", None, None),
            P("section", None),
            P("section", None),
            P("dp", None, None, None),
        ),
        out_specs=(
            P("section", "dp", None, None, None),
            P("dp", "section", None, None),
            P("section", None, None),
            P("section", None),
            P("section", None),
        ),
        check_vma=False,
    )
```

```python
import jax
import jax.numpy as jnp
from jax import lax
from jax.experimental import pallas as pl
from jax.experimental.pallas import tpu as pltpu
from jax.sharding import PartitionSpec as P

MICRO = 8


EPSILON = 1e-05


def for_sending(value):

    def short(part):
        return part.astype(jnp.bfloat16) if part.dtype == jnp.float32 else part

    return jax.tree.map(short, value)


def shifted(value, axis, steps):
    count = lax.axis_size(axis)
    initial, last = (max(0, -steps), min(count, count - steps))
    return lax.ppermute(value, axis, [(source, source + steps) for source in range(initial, last)])


def conv_forward(activation, kernel, stride):
    return lax.conv_general_dilated(
        activation,
        kernel,
        (stride, stride),
        ((1, 1), (1, 1)),
        dimension_numbers=("NHWC", "HWIO", "NHWC"),
        preferred_element_type=jnp.float32,
    )


def conv_input_grad(gradient, kernel, stride):
    upper = 1 if stride == 1 else 2
    return lax.conv_general_dilated(
        gradient,
        kernel[::-1, ::-1],
        (1, 1),
        ((1, upper), (1, upper)),
        lhs_dilation=(stride, stride),
        dimension_numbers=("NHWC", "HWOI", "NHWC"),
        preferred_element_type=jnp.float32,
    )


def conv_kernel_grad(activation, gradient, stride):
    upper = 1 if stride == 1 else 0
    return lax.conv_general_dilated(
        activation,
        gradient,
        (1, 1),
        ((1, upper), (1, upper)),
        rhs_dilation=(stride, stride),
        dimension_numbers=("CHWN", "IHWO", "HWNC"),
        preferred_element_type=jnp.float32,
    )


def channel_sum(values, image_mask):
    return jnp.sum(image_mask[:, None, None, None] * values, axis=(0, 1, 2))


def normalize(values, channel_mean, inv_std, norm_gain, norm_bias):
    scaled = (values - channel_mean) * inv_std
    return (scaled, scaled * norm_gain + norm_bias)


def norm_terms(grad_act, values, image_mask, channel_mean, inv_std, norm_gain, norm_bias):
    scaled, pre_act = normalize(values, channel_mean, inv_std, norm_gain, norm_bias)
    sigmoid_val = jax.nn.sigmoid(pre_act)
    grad_pre = (
        grad_act
        * image_mask[:, None, None, None]
        * sigmoid_val
        * (1.0 + pre_act * (1.0 - sigmoid_val))
    )
    return (grad_pre, scaled)


def pipelined(images, image_counts, conv_weight, bn_gain, bn_bias, out_grad):
    section_count = lax.axis_size("section")
    section_index = lax.axis_index("section")
    img_dev = images.shape[0]
    per_micro = img_dev // MICRO
    height = images.shape[1]
    side = height // 2
    c_in = images.shape[3]
    c_out = conv_weight.shape[2]
    kernel_rows = conv_weight.shape[1]
    is_first = section_index == 0
    is_last = section_index == section_count - 1
    adds_residual = section_index % 2 == 1
    merges_back = (section_index % 2 == 0) & (section_index > 0)
    valid_img = (jnp.arange(img_dev, dtype=jnp.int32) < image_counts[0]).astype(jnp.float32)
    valid_img = valid_img.reshape(per_micro, MICRO)
    image_groups = images.reshape(per_micro, MICRO, height, height, c_in)
    grad_groups = out_grad.reshape(per_micro, MICRO, side, side, c_out)
    kernel_all = conv_weight[0]
    kernel_first = kernel_all[: 9 * c_in].reshape(3, 3, c_in, c_out)
    kernel_proj = kernel_all[9 * c_in : 10 * c_in]
    kernel_rest = kernel_all.reshape(3, 3, c_out, c_out)
    norm_gain = bn_gain[0]
    norm_bias = bn_bias[0]
    tick_count = MICRO + section_count - 1
    pad_width = (0, c_out - c_in)

    def forward_first(raw_input, section_input, residual, image_mask, channel_mean, inv_std):
        scaled, pre_act = normalize(
            raw_input, channel_mean[:c_in], inv_std[:c_in], norm_gain[:c_in], norm_bias[:c_in]
        )
        activation = (jax.nn.silu(pre_act) * image_mask[:, None, None, None]).astype(jnp.bfloat16)
        conv_out = conv_forward(activation, kernel_first, 2)
        sub_grid = activation[:, 0::2, 0::2, :].reshape(-1, c_in)
        projected = jnp.dot(sub_grid, kernel_proj, preferred_element_type=jnp.float32)
        projected = projected.reshape(per_micro, side, side, c_out)
        return (conv_out.astype(jnp.bfloat16), projected.astype(jnp.bfloat16))

    def forward_rest(raw_input, section_input, residual, image_mask, channel_mean, inv_std):
        scaled, pre_act = normalize(section_input, channel_mean, inv_std, norm_gain, norm_bias)
        activation = (jax.nn.silu(pre_act) * image_mask[:, None, None, None]).astype(jnp.bfloat16)
        conv_out = conv_forward(activation, kernel_rest, 1)
        summed = conv_out + jnp.where(adds_residual, 1.0, 0.0) * residual.astype(jnp.float32)
        sent_main = summed.astype(jnp.bfloat16)
        return (sent_main, jnp.where(adds_residual, sent_main, residual))

    def forward_tick(step_index, state_carry):
        recv_main, recv_side, out_buf, in_buf, moment_buf, count_buf = state_carry
        micro_index = step_index - section_index
        active = (micro_index >= 0) & (micro_index < MICRO)
        slot_index = jnp.clip(micro_index, 0, MICRO - 1)
        image_mask = lax.dynamic_index_in_dim(valid_img, slot_index, 1, keepdims=False)
        raw_input = lax.dynamic_index_in_dim(image_groups, slot_index, 1, keepdims=False).astype(
            jnp.float32
        )
        section_input = recv_main.astype(jnp.float32)
        positions = jnp.where(is_first, float(height * height), float(side * side))
        local_count = jnp.sum(image_mask) * positions
        local_total = jnp.where(
            is_first,
            jnp.pad(channel_sum(raw_input, image_mask), pad_width),
            channel_sum(section_input, image_mask),
        )
        total_sum, count_sum = lax.psum((local_total, local_count), "dp")
        channel_mean = total_sum / count_sum
        first_dev = raw_input - channel_mean[:c_in]
        rest_dev = section_input - channel_mean
        local_spread = jnp.where(
            is_first,
            jnp.pad(channel_sum(first_dev * first_dev, image_mask), pad_width),
            channel_sum(rest_dev * rest_dev, image_mask),
        )
        spread_sum = lax.psum(local_spread, "dp")
        variance = spread_sum / count_sum
        inv_std = lax.rsqrt(variance + EPSILON)
        sent_main, sent_side = lax.cond(
            is_first,
            forward_first,
            forward_rest,
            raw_input,
            section_input,
            recv_side,
            image_mask,
            channel_mean,
            inv_std,
        )
        old_out = lax.dynamic_index_in_dim(out_buf, slot_index, 0, keepdims=False)
        out_buf = lax.dynamic_update_index_in_dim(
            out_buf, jnp.where(active, sent_main, old_out), slot_index, 0
        )
        old_in = lax.dynamic_index_in_dim(in_buf, slot_index, 0, keepdims=False)
        in_buf = lax.dynamic_update_index_in_dim(
            in_buf, jnp.where(active, recv_main, old_in), slot_index, 0
        )
        moments = jnp.stack([channel_mean, inv_std])
        old_moment = lax.dynamic_index_in_dim(moment_buf, slot_index, 0, keepdims=False)
        moment_buf = lax.dynamic_update_index_in_dim(
            moment_buf, jnp.where(active, moments, old_moment), slot_index, 0
        )
        old_count = lax.dynamic_index_in_dim(count_buf, slot_index, 0, keepdims=False)
        count_buf = lax.dynamic_update_index_in_dim(
            count_buf, jnp.where(active, count_sum, old_count), slot_index, 0
        )
        recv_main, recv_side = (
            shifted(for_sending(sent_main), "section", 1).astype(sent_main.dtype),
            shifted(for_sending(sent_side), "section", 1).astype(sent_side.dtype),
        )
        return (recv_main, recv_side, out_buf, in_buf, moment_buf, count_buf)

    act_zeros = jnp.zeros((per_micro, side, side, c_out), jnp.bfloat16)
    forward_init = (
        act_zeros,
        act_zeros,
        jnp.zeros((MICRO, per_micro, side, side, c_out), jnp.bfloat16),
        jnp.zeros((MICRO, per_micro, side, side, c_out), jnp.bfloat16),
        jnp.zeros((MICRO, 2, c_out), jnp.float32),
        jnp.ones((MICRO,), jnp.float32),
    )
    forward_done = lax.fori_loop(0, tick_count, forward_tick, forward_init)
    out_buf, in_buf, moment_buf, count_buf = (
        forward_done[2],
        forward_done[3],
        forward_done[4],
        forward_done[5],
    )

    def backward_first(
        raw_input, section_input, grad_conv, grad_side, image_mask, channel_mean, inv_std
    ):
        scaled, pre_act = normalize(
            raw_input, channel_mean[:c_in], inv_std[:c_in], norm_gain[:c_in], norm_bias[:c_in]
        )
        activation = (jax.nn.silu(pre_act) * image_mask[:, None, None, None]).astype(jnp.bfloat16)
        kernel_part = conv_kernel_grad(activation, grad_conv, 2).reshape(9 * c_in, c_out)
        sub_grid = activation[:, 0::2, 0::2, :].reshape(-1, c_in)
        side_flat = grad_side.reshape(-1, c_out)
        proj_part = lax.dot_general(
            sub_grid, side_flat, (((0,), (0,)), ((), ())), preferred_element_type=jnp.float32
        )
        weight_part = jnp.concatenate(
            [kernel_part, proj_part, jnp.zeros((kernel_rows - 10 * c_in, c_out), jnp.float32)],
            axis=0,
        )
        sub_grad = lax.dot_general(
            side_flat, kernel_proj, (((1,), (1,)), ((), ())), preferred_element_type=jnp.float32
        )
        sub_grad = sub_grad.reshape(per_micro, side, side, c_in)
        spread_grad = lax.pad(
            sub_grad, jnp.float32(0.0), ((0, 0, 0), (0, 1, 1), (0, 1, 1), (0, 0, 0))
        )
        grad_first = conv_input_grad(grad_conv, kernel_first, 2) + spread_grad
        return (weight_part, grad_first, jnp.zeros((per_micro, side, side, c_out), jnp.float32))

    def backward_rest(
        raw_input, section_input, grad_conv, grad_side, image_mask, channel_mean, inv_std
    ):
        scaled, pre_act = normalize(section_input, channel_mean, inv_std, norm_gain, norm_bias)
        activation = (jax.nn.silu(pre_act) * image_mask[:, None, None, None]).astype(jnp.bfloat16)
        weight_part = conv_kernel_grad(activation, grad_conv, 1).reshape(kernel_rows, c_out)
        grad_rest = conv_input_grad(grad_conv, kernel_rest, 1)
        return (weight_part, jnp.zeros((per_micro, height, height, c_in), jnp.float32), grad_rest)

    def backward_tick(step_index, state_carry):
        recv_main, recv_side, weight_acc, gain_acc, bias_acc, input_buf = state_carry
        micro_index = step_index - (section_count - 1 - section_index)
        active = (micro_index >= 0) & (micro_index < MICRO)
        slot_index = jnp.clip(micro_index, 0, MICRO - 1)
        image_mask = lax.dynamic_index_in_dim(valid_img, slot_index, 1, keepdims=False)
        raw_input = lax.dynamic_index_in_dim(image_groups, slot_index, 1, keepdims=False).astype(
            jnp.float32
        )
        section_input = lax.dynamic_index_in_dim(in_buf, slot_index, 0, keepdims=False).astype(
            jnp.float32
        )
        moments = lax.dynamic_index_in_dim(moment_buf, slot_index, 0, keepdims=False)
        channel_mean, inv_std = (moments[0], moments[1])
        count_sum = lax.dynamic_index_in_dim(count_buf, slot_index, 0, keepdims=False)
        top_grad = jnp.where(
            is_last, lax.dynamic_index_in_dim(grad_groups, slot_index, 1, keepdims=False), recv_main
        )
        joined = (top_grad.astype(jnp.float32) + recv_side.astype(jnp.float32)).astype(jnp.bfloat16)
        grad_conv = jnp.where(adds_residual, joined, top_grad)
        grad_side = jnp.where(adds_residual, joined, recv_side)
        weight_part, grad_first, grad_rest = lax.cond(
            is_first,
            backward_first,
            backward_rest,
            raw_input,
            section_input,
            grad_conv,
            grad_side,
            image_mask,
            channel_mean,
            inv_std,
        )
        pre_first, scaled_first = norm_terms(
            grad_first,
            raw_input,
            image_mask,
            channel_mean[:c_in],
            inv_std[:c_in],
            norm_gain[:c_in],
            norm_bias[:c_in],
        )
        pre_rest, scaled_rest = norm_terms(
            grad_rest, section_input, image_mask, channel_mean, inv_std, norm_gain, norm_bias
        )
        local_pre = jnp.where(
            is_first,
            jnp.pad(jnp.sum(pre_first, axis=(0, 1, 2)), pad_width),
            jnp.sum(pre_rest, axis=(0, 1, 2)),
        )
        local_cross = jnp.where(
            is_first,
            jnp.pad(jnp.sum(pre_first * scaled_first, axis=(0, 1, 2)), pad_width),
            jnp.sum(pre_rest * scaled_rest, axis=(0, 1, 2)),
        )
        sum_pre, sum_cross = lax.psum((local_pre, local_cross), "dp")
        mean_pre = sum_pre / count_sum
        mean_cross = sum_cross / count_sum
        mask_four = image_mask[:, None, None, None]
        grad_in_rest = (
            mask_four * inv_std * norm_gain * (pre_rest - mean_pre - scaled_rest * mean_cross)
        )
        grad_in_first = (
            mask_four
            * inv_std[:c_in]
            * norm_gain[:c_in]
            * (pre_first - mean_pre[:c_in] - scaled_first * mean_cross[:c_in])
        )
        sent_main = jnp.where(
            merges_back, grad_in_rest + grad_side.astype(jnp.float32), grad_in_rest
        ).astype(jnp.bfloat16)
        sent_side = jnp.where(merges_back, jnp.zeros_like(grad_side), grad_side)
        weight_acc = weight_acc + jnp.where(active, weight_part, 0.0)
        gain_acc = gain_acc + jnp.where(active, sum_cross, 0.0)
        bias_acc = bias_acc + jnp.where(active, sum_pre, 0.0)
        old_input = lax.dynamic_index_in_dim(input_buf, slot_index, 0, keepdims=False)
        input_buf = lax.dynamic_update_index_in_dim(
            input_buf, jnp.where(active, grad_in_first, old_input), slot_index, 0
        )
        recv_main, recv_side = shifted((sent_main, sent_side), "section", -1)
        return (recv_main, recv_side, weight_acc, gain_acc, bias_acc, input_buf)

    backward_init = (
        act_zeros,
        act_zeros,
        jnp.zeros((kernel_rows, c_out), jnp.float32),
        jnp.zeros((c_out,), jnp.float32),
        jnp.zeros((c_out,), jnp.float32),
        jnp.zeros((MICRO, per_micro, height, height, c_in), jnp.float32),
    )
    backward_done = lax.fori_loop(0, tick_count, backward_tick, backward_init)
    weight_acc, gain_acc, bias_acc, input_buf = (
        backward_done[2],
        backward_done[3],
        backward_done[4],
        backward_done[5],
    )
    weight_total = lax.psum(weight_acc, "dp")
    input_full = jnp.transpose(input_buf, (1, 0, 2, 3, 4)).reshape(img_dev, height, height, c_in)
    input_full = jnp.where(is_first, input_full, 0.0)
    input_grad = lax.psum_scatter(
        input_full.astype(jnp.bfloat16), "section", scatter_dimension=1, tiled=True
    )
    section_outputs = jnp.transpose(out_buf, (1, 0, 2, 3, 4)).reshape(img_dev, side, side, c_out)[
        None
    ]
    return (section_outputs, input_grad, weight_total[None], gain_acc[None], bias_acc[None])


BF = jnp.bfloat16
F32 = jnp.float32
INF = float("inf")
MIB = 1024 * 1024
ANY = pl.BlockSpec(memory_space=pltpu.HBM)
FREE = pl.BlockSpec(memory_space=pl.ANY)
INSIDE = pl.BlockSpec(memory_space=pltpu.VMEM)
KEPT = pl.BlockSpec(memory_space=pltpu.VMEM)
SCALARS = pl.BlockSpec(memory_space=pltpu.SMEM)
FIELD = jax.ShapeDtypeStruct((512, 640), BF)
TWO = jax.ShapeDtypeStruct((2, 512, 640), BF)
PAIR = jax.ShapeDtypeStruct((2, 640), F32)
SUMS = jax.ShapeDtypeStruct((1920, 1920), F32)


def lane(k, first=0):
    return pl.ds(pl.multiple_of(first + 128 * k, 128), 128)


def from_left(values):
    column = lax.broadcasted_iota(jnp.int32, values.shape, 0) & 7
    return jnp.where(column == 0, 0.0, pltpu.roll(values, 1, 0))


def from_right(values):
    column = lax.broadcasted_iota(jnp.int32, values.shape, 0) & 7
    return jnp.where(column == 7, 0.0, pltpu.roll(values, values.shape[0] - 1, 0))


def total_of(values):
    return jnp.sum(values, axis=0, keepdims=True)


def count_of(valid):
    return total_of(jnp.where(valid, 1.0, 0.0))


def sigmoid(z):
    return 0.5 * jnp.tanh(0.5 * z) + 0.5


def matmul(a, b):
    return jnp.dot(a, b, preferred_element_type=F32)


def matmul_bt(a, b):
    return lax.dot_general(a, b, (((1,), (1,)), ((), ())), preferred_element_type=F32)


def matmul_at(a, b):
    return lax.dot_general(a, b, (((0,), (0,)), ((), ())), preferred_element_type=F32)


def start_all(copies):
    for one in copies:
        one.start()


def wait_all(copies):
    for one in copies:
        one.wait()


PINNED = {id(ANY): pltpu.HBM, id(KEPT): pltpu.VMEM}


def kernel_call(kernel, out_shape, in_specs, out_specs, scratch, aliases=None, flops=0, mib=18):
    outs = out_shape if isinstance(out_shape, tuple) else (out_shape,)
    specs = out_specs if isinstance(out_specs, tuple) else (out_specs,)
    outs = tuple(
        PINNED[id(spec)](one.shape, one.dtype) if id(spec) in PINNED else one for spec, one in zip(specs, outs)
    )
    call = pl.pallas_call(
        kernel,
        out_shape=outs,
        in_specs=in_specs,
        out_specs=specs,
        scratch_shapes=scratch,
        input_output_aliases=aliases or {},
        compiler_params=pltpu.CompilerParams(vmem_limit_bytes=mib * MIB),
        cost_estimate=pl.CostEstimate(flops=int(flops * 1.0), bytes_accessed=0, transcendentals=0),
    )

    def run(*args):
        args = [
            pltpu.with_memory_space_constraint(one, PINNED[id(spec)]) if id(spec) in PINNED else one
            for spec, one in zip(in_specs, args)
        ]
        results = call(*args)
        return results if isinstance(out_shape, tuple) else results[0]

    return run


def half_turn(values):
    return jnp.concatenate([values[:, 320:640], values[:, 0:320]], axis=1)


def twice(values):
    return jnp.concatenate([values[:, 0:320], values[:, 0:320]], axis=1)


def weight_first(w_ref, w_vm, sems):
    copies = []
    for p in range(3):
        copies.append(
            pltpu.make_async_copy(
                w_ref.at[pl.ds(960 * p + 320, 640)], w_vm.at[pl.ds(1024 * p, 640)], sems.at[2 * p]
            )
        )
        copies.append(
            pltpu.make_async_copy(
                w_ref.at[pl.ds(960 * p, 320)], w_vm.at[pl.ds(1024 * p + 704, 320)], sems.at[2 * p + 1]
            )
        )
        w_vm[1024 * p + 640 : 1024 * p + 704, :] = jnp.zeros((64, 640), BF)
    copies.append(pltpu.make_async_copy(w_ref.at[pl.ds(2880, 320)], w_vm.at[pl.ds(3072, 320)], sems.at[6]))
    w_vm[3392:3456, :] = jnp.zeros((64, 640), BF)
    return copies


def forward_first_kernel(
    flags, own, one, two, three, four, others, w_ref, gain, bias, out_ref, ring_ref, field_ref, stats_ref,
    w_vm, x_vm, cat, acc, part, sems, x_sems,
):
    @pl.when(flags[0] == 1)
    def _():
        pieces = [ref.at[0] for ref in (own, one, two, three, four)] + [others.at[k] for k in range(3)]
        in_x = []
        for k, piece in enumerate(pieces):
            slot = flags[1] ^ k
            for a in range(2):
                in_x.append(
                    pltpu.make_async_copy(piece.at[:, a], x_vm.at[a, :, slot], x_sems.at[2 * k + a])
                )
        start_all(in_x)
        in_w = weight_first(w_ref, w_vm, sems)
        start_all(in_w)
        cat[0:64, :] = jnp.zeros((64, 1024), BF)
        part[4:5, :] = twice(gain)
        part[5:6, :] = twice(bias)
        wait_all(in_x)

        @pl.loop(0, 5)
        def _(k):
            here = lane(k)
            x = x_vm[0, :, :, :, here].astype(F32).reshape(512, 128)
            y = x_vm[1, :, :, :, here].astype(F32).reshape(512, 128)
            field_ref[0, :, here] = x.astype(BF)
            field_ref[1, :, here] = y.astype(BF)
            valid = x < INF
            part[0:1, here] = total_of(jnp.where(valid, x + y, 0.0))
            part[2:3, here] = 4.0 * count_of(valid)

        part[0:1, :] = (part[0:1, :] + half_turn(part[0:1, :])) / part[2:3, :]

        @pl.loop(0, 5)
        def _(k):
            here = lane(k)
            x, y = field_ref[0, :, here].astype(F32), field_ref[1, :, here].astype(F32)
            valid = x < INF
            x = x - part[0:1, here]
            y = y - part[0:1, here]
            part[1:2, here] = total_of(jnp.where(valid, x * x + y * y, 0.0))

        part[1:2, :] = lax.rsqrt((part[1:2, :] + half_turn(part[1:2, :])) / part[2:3, :] + EPSILON)
        stats_ref[...] = part[0:2, :]

        @pl.loop(0, 5)
        def _(k):
            here = lane(k)
            for a in range(2):
                x = field_ref[a, :, here].astype(F32)
                z = (x - part[0:1, here]) * part[1:2, here] * part[4:5, here] + part[5:6, here]
                act = jnp.where(x < INF, z * sigmoid(z), 0.0)
                first = 576 if a == 0 else 64
                cat[first : first + 512, here] = act.astype(BF)

                @pl.when(k >= 2)
                def _():
                    cat[first : first + 512, lane(k, 384)] = from_left(act).astype(BF)

        keep = [
            pltpu.make_async_copy(cat.at[pl.ds(576, 512), pl.ds(0, 640)], ring_ref.at[0], x_sems.at[0]),
            pltpu.make_async_copy(cat.at[pl.ds(64, 512), pl.ds(0, 640)], ring_ref.at[1], x_sems.at[1]),
        ]
        start_all(keep)
        acc[...] = jnp.zeros((512, 640), F32)
        wait_all(in_w)

        @pl.loop(0, 3)
        def _(p):
            first = pl.multiple_of(jnp.where(p == 1, 576, 32 * p), 64)
            acc[...] += matmul(cat[pl.ds(first, 512), :], w_vm[pl.ds(pl.multiple_of(1024 * p, 1024), 1024), :])

        @pl.loop(0, 5)
        def _(k):
            row_valid = field_ref[0, :, 0:128].astype(F32) < INF
            out_ref[0, :, lane(k)] = jnp.where(row_valid, acc[:, lane(k)], INF).astype(BF)

        out_ref[1] = matmul(cat[576:1088, 0:384], w_vm[3072:3456, :]).astype(BF)
        wait_all(keep)


def forward_first(flags, pieces, weight, gain, bias):
    return kernel_call(
        forward_first_kernel,
        (TWO, TWO, TWO, PAIR),
        [SCALARS] + [FREE] * 6 + [ANY, INSIDE, INSIDE],
        (INSIDE, ANY, INSIDE, INSIDE),
        [
            pltpu.VMEM((3456, 640), BF),
            pltpu.VMEM((2, 8, 8, 8, 640), BF),
            pltpu.VMEM((1088, 1024), BF),
            pltpu.VMEM((512, 640), F32),
            pltpu.VMEM((8, 640), F32),
            pltpu.SemaphoreType.DMA((7,)),
            pltpu.SemaphoreType.DMA((16,)),
        ],
        flops=4_000_000_000,
    )(flags, *pieces, weight, gain, bias)


def weight_part(w_ref, w_vm, sems, p):
    rows = pl.ds(pl.multiple_of(1920 * p, 1920), 1920)
    return pltpu.make_async_copy(w_ref.at[rows], w_vm.at[rows], sems.at[p])


def clear_edges(x3):
    x3[0:64, :] = jnp.zeros((64, x3.shape[1]), BF)
    x3[576:640, :] = jnp.zeros((64, x3.shape[1]), BF)


def place(x3, k, values, left, right):
    x3[64:576, lane(k, left)] = from_left(values).astype(BF)
    x3[64:576, lane(k, 640)] = values.astype(BF)
    x3[64:576, lane(k, right)] = from_right(values).astype(BF)


def forward_conv(x3, w_ref, w_vm, w_sems, acc):
    @pl.loop(0, 3)
    def _(p):
        weight_part(w_ref, w_vm, w_sems, p).wait()
        acc[...] += matmul(
            x3[pl.ds(pl.multiple_of(64 * p, 64), 512), :], w_vm[pl.ds(pl.multiple_of(1920 * p, 1920), 1920), :]
        )


def statistics(x):
    valid = x < INF
    count = count_of(valid)
    mean = total_of(jnp.where(valid, x, 0.0)) / count
    centred = jnp.where(valid, x - mean, 0.0)
    inv = lax.rsqrt(total_of(centred * centred) / count + EPSILON)
    return valid, count, mean, inv, centred


def forward_rest_kernel(
    handed, flags, h, res, w_ref, gain, bias, out_ref, stats_ref, act_ref, w_vm, x3, acc, w_sems
):
    if not handed:
        h, res = h.at[0], res.at[1]

    @pl.when(flags[0] == 1)
    def _():
        for p in range(3):
            weight_part(w_ref, w_vm, w_sems, p).start()
        clear_edges(x3)

        @pl.loop(0, 5)
        def _(k):
            here = lane(k)
            valid, _, mean, inv, centred = statistics(h[:, here].astype(F32))
            stats_ref[0:1, here] = mean
            stats_ref[1:2, here] = inv
            z = centred * inv * gain[:, here] + bias[:, here]
            act = jnp.where(valid, z * sigmoid(z), 0.0)
            act_ref[:, here] = act.astype(BF)
            place(x3, k, act, 0, 1280)
            acc[:, here] = jnp.zeros((512, 128), F32) if handed else res[:, here].astype(F32)

        forward_conv(x3, w_ref, w_vm, w_sems, acc)

        @pl.loop(0, 5)
        def _(k):
            here = lane(k)
            row_valid = h[:, 0:128].astype(F32) < INF
            out = jnp.where(row_valid, acc[:, here], INF).astype(BF)
            if handed:
                out_ref[0, :, here] = out
                out_ref[1, :, here] = h[:, here]
            else:
                out_ref[:, here] = out


def forward_rest(flags, h, res, weight, gain, bias, handed=False):
    return kernel_call(
        lambda *refs: forward_rest_kernel(handed, *refs),
        (TWO if handed else FIELD, PAIR, FIELD),
        [SCALARS, INSIDE, INSIDE, ANY, INSIDE, INSIDE],
        (INSIDE, INSIDE, INSIDE),
        [
            pltpu.VMEM((5760, 640), BF),
            pltpu.VMEM((640, 1920), BF),
            pltpu.VMEM((512, 640), F32),
            pltpu.SemaphoreType.DMA((3,)),
        ],
        flops=4_000_000_000,
    )(flags, h, res, weight, gain, bias)


def forward_last_kernel(flags, act, pair, w_ref, out_ref, w_vm, x3, acc, w_sems):
    @pl.when(flags[0] == 1)
    def _():
        for p in range(3):
            weight_part(w_ref, w_vm, w_sems, p).start()
        clear_edges(x3)

        @pl.loop(0, 5)
        def _(k):
            place(x3, k, act[:, lane(k)].astype(F32), 0, 1280)
            acc[:, lane(k)] = pair[1, :, lane(k)].astype(F32)

        forward_conv(x3, w_ref, w_vm, w_sems, acc)

        @pl.loop(0, 5)
        def _(k):
            row_valid = pair[0, :, 0:128].astype(F32) < INF
            out_ref[:, lane(k)] = jnp.where(row_valid, acc[:, lane(k)], INF).astype(BF)


def forward_last(flags, act, pair, weight):
    return kernel_call(
        forward_last_kernel,
        FIELD,
        [SCALARS, INSIDE, INSIDE, ANY],
        INSIDE,
        [
            pltpu.VMEM((5760, 640), BF),
            pltpu.VMEM((640, 1920), BF),
            pltpu.VMEM((512, 640), F32),
            pltpu.SemaphoreType.DMA((3,)),
        ],
        flops=4_000_000_000,
    )(flags, act, pair, weight)


def by_row(values):
    return values.transpose(1, 0, 2, 3).reshape(512, values.shape[3])


def backward_conv(g3, w_ref, w_vm, w_sems, acc):
    @pl.loop(0, 3)
    def _(p):
        weight_part(w_ref, w_vm, w_sems, p).wait()

        @pl.loop(0, 3)
        def _(q):
            acc[...] += matmul_bt(
                g3[pl.ds(pl.multiple_of(64 * (2 - p), 64), 512), pl.ds(pl.multiple_of(640 * q, 640), 640)],
                w_vm[pl.ds(pl.multiple_of(640 * (3 * p + q), 640), 640), :],
            )


def backward_conv_turned(g3, w_ref, w_vm, w_sems, acc):
    @pl.loop(0, 3)
    def _(p):
        weight_part(w_ref, w_vm, w_sems, p).wait()
        acc[...] += matmul(
            g3[pl.ds(pl.multiple_of(64 * (2 - p), 64), 512), :],
            w_vm[pl.ds(pl.multiple_of(1920 * p, 1920), 1920), :],
        )


def backward_top_kernel(flags, g_ref, w_ref, total_ref, own_ref, w_vm, g3, w_sems):
    for p in range(3):
        weight_part(w_ref, w_vm, w_sems, p).start()
    clear_edges(g3)

    @pl.loop(0, 5)
    def _(k):
        here = lane(k)
        g = by_row(g_ref[:, :, :, here].astype(F32))
        own_ref[:, here] = g.astype(BF)
        place(g3, k, g, 1280, 0)
        total_ref[:, here] = jnp.zeros((512, 128), F32)

    backward_conv(g3, w_ref, w_vm, w_sems, total_ref)


def backward_top(flags, g, weight):
    return kernel_call(
        backward_top_kernel,
        (jax.ShapeDtypeStruct((512, 640), F32), FIELD),
        [SCALARS, INSIDE, ANY],
        (INSIDE, INSIDE),
        [
            pltpu.VMEM((5760, 640), BF),
            pltpu.VMEM((640, 1920), BF),
            pltpu.SemaphoreType.DMA((3,)),
        ],
        flops=4_000_000_000,
    )(flags, g, weight)


def norm_back(grad, valid, count, centred, inv, scale, offset, sums_ref, here):
    xhat = centred * inv
    z = xhat * scale + offset
    sig = sigmoid(z)
    dz = jnp.where(valid, grad * sig * (1.0 + z * (1.0 - sig)), 0.0)
    s1 = total_of(dz)
    s2 = total_of(dz * xhat)
    sums_ref[0:1, here] = s1
    sums_ref[1:2, here] = s2
    back = scale * inv * (dz - s1 / count - xhat * (s2 / count))
    return jnp.where(valid, back, 0.0), jnp.where(valid, z * sig, 0.0)


def turn_kernel(flags, pair, grad, gain, bias, out_ref, sums_ref, act_ref):
    @pl.when(flags[0] == 1)
    def _():
        @pl.loop(0, 5)
        def _(k):
            here = lane(k)
            valid, count, _, inv, centred = statistics(pair[0, :, here].astype(F32))
            back, act = norm_back(
                grad[:, here], valid, count, centred, inv, gain[:, here], bias[:, here], sums_ref, here
            )
            act_ref[:, here] = act.astype(BF)
            out_ref[:, here] = back.astype(BF)


def turn(flags, h, grad, gain, bias):
    return kernel_call(
        turn_kernel,
        (FIELD, PAIR, FIELD),
        [SCALARS] + [INSIDE] * 4,
        (INSIDE, INSIDE, INSIDE),
        [],
        flops=1_000_000_000,
    )(flags, h, grad, gain, bias)


def backward_rest_kernel(
    handed, flags, g_ref, add, h, stats, w_ref, gain, bias, out_ref, sums_ref, w_vm, g3, acc, w_sems
):
    if handed:
        h = h.at[0]

    @pl.when(flags[0] == 1)
    def _():
        for p in range(3):
            weight_part(w_ref, w_vm, w_sems, p).start()
        clear_edges(g3)

        @pl.loop(0, 5)
        def _(k):
            place(g3, k, g_ref[:, lane(k)].astype(F32), 1280, 0)
            acc[:, lane(k)] = jnp.zeros((512, 128), F32)

        backward_conv_turned(g3, w_ref, w_vm, w_sems, acc)
        @pl.loop(0, 5)
        def _(k):
            here = lane(k)
            x = h[:, here].astype(F32)
            valid = x < INF
            centred = jnp.where(valid, x - stats[0:1, here], 0.0)
            back, _ = norm_back(
                acc[:, here], valid, count_of(valid), centred, stats[1:2, here], gain[:, here], bias[:, here],
                sums_ref, here,
            )
            if handed:
                out_ref[0, :, here] = back.astype(BF)
                out_ref[1, :, here] = g_ref[:, here]
            else:
                out_ref[:, here] = (back + by_row(add[:, :, :, here].astype(F32))).astype(BF)


def backward_rest(flags, g, add, h, stats, weight, gain, bias, handed=False):
    return kernel_call(
        lambda *refs: backward_rest_kernel(handed, *refs),
        (TWO if handed else FIELD, PAIR),
        [SCALARS, INSIDE, INSIDE, INSIDE, INSIDE, ANY, INSIDE, INSIDE],
        (INSIDE, INSIDE),
        [
            pltpu.VMEM((5760, 640), BF),
            pltpu.VMEM((640, 1920), BF),
            pltpu.VMEM((512, 640), F32),
            pltpu.SemaphoreType.DMA((3,)),
        ],
        flops=4_000_000_000,
    )(flags, g, add, h, stats, weight, gain, bias)


def backward_first_conv_kernel(flags, pair, w_ref, acc, w_vm, g2, sems):
    in_w = weight_first(w_ref, w_vm, sems)
    start_all(in_w)
    g2[512:576, :] = jnp.zeros((64, 1280), BF)

    @pl.loop(0, 5)
    def _(k):
        g = pair[0, :, lane(k)].astype(F32)
        g2[0:512, lane(k)] = g.astype(BF)
        g2[0:512, lane(k, 640)] = from_right(g).astype(BF)

    acc[...] = jnp.zeros((2, 512, 640), F32)
    wait_all(in_w)

    @pl.loop(0, 3)
    def _(p):
        rows = pl.ds(pl.multiple_of(jnp.where(p == 0, 64, 0), 64), 512)
        a = jnp.where(p == 1, 0, 1)
        first = pl.multiple_of(1024 * p, 1024)
        acc[a] += matmul_bt(g2[rows, 0:640], w_vm[pl.ds(first, 640), :])
        acc[a, :, 256:640] += matmul_bt(g2[rows, 640:1280], w_vm[pl.ds(first + 640, 384), :])

    acc[0, :, 0:384] += matmul_bt(pair[1], w_vm[3072:3456, :])


def backward_first_conv(flags, pair, weight):
    return kernel_call(
        backward_first_conv_kernel,
        jax.ShapeDtypeStruct((2, 512, 640), F32),
        [SCALARS, INSIDE, ANY],
        INSIDE,
        [
            pltpu.VMEM((3456, 640), BF),
            pltpu.VMEM((576, 1280), BF),
            pltpu.SemaphoreType.DMA((7,)),
        ],
        flops=5_000_000_000,
    )(flags, pair, weight)


def backward_first_norm_kernel(flags, acc, x_ref, stats, gain, bias, out_ref, sums_ref, dz_vm, part):
    part[4:5, :] = twice(gain)
    part[5:6, :] = twice(bias)

    @pl.loop(0, 5)
    def _(k):
        here = lane(k)
        s1 = s2 = 0.0
        for a in range(2):
            x = x_ref[a, :, here].astype(F32)
            valid = x < INF
            xhat = jnp.where(valid, x - stats[0:1, here], 0.0) * stats[1:2, here]
            z = xhat * part[4:5, here] + part[5:6, here]
            sig = sigmoid(z)
            dz = jnp.where(valid, acc[a, :, here] * sig * (1.0 + z * (1.0 - sig)), 0.0)
            dz_vm[a, :, here] = dz
            s1 = s1 + total_of(dz)
            s2 = s2 + total_of(dz * xhat)
        part[0:1, here] = s1
        part[1:2, here] = s2
        part[2:3, here] = 4.0 * count_of(valid)

    part[0:1, :] = part[0:1, :] + half_turn(part[0:1, :])
    part[1:2, :] = part[1:2, :] + half_turn(part[1:2, :])
    sums_ref[...] = jnp.where(lax.broadcasted_iota(jnp.int32, (2, 640), 1) < 320, part[0:2, :], 0.0)

    @pl.loop(0, 5)
    def _(k):
        here = lane(k)
        count = part[2:3, here]
        scale = part[4:5, here] * stats[1:2, here]
        for a in range(2):
            x = x_ref[a, :, here].astype(F32)
            xhat = (x - stats[0:1, here]) * stats[1:2, here]
            back = scale * (dz_vm[a, :, here] - part[0:1, here] / count - xhat * (part[1:2, here] / count))
            back = jnp.where(x < INF, back, 0.0).reshape(4, 2, 8, 8, 128).transpose(2, 0, 1, 3, 4)
            out_ref[:, :, :, a, :, here] = back.astype(BF)


def backward_first_norm(flags, field, x, stats, gain, bias):
    return kernel_call(
        backward_first_norm_kernel,
        (jax.ShapeDtypeStruct((8, 4, 2, 2, 8, 640), BF), PAIR),
        [SCALARS, INSIDE, INSIDE, INSIDE, INSIDE, INSIDE],
        (INSIDE, INSIDE),
        [pltpu.VMEM((2, 512, 640), F32), pltpu.VMEM((8, 640), F32)],
        flops=1_000_000_000,
    )(flags, field, x, stats, gain, bias)


def send_sides(side, rows, sent_ref):
    sent_ref[0:320, :] = side.astype(BF)
    for k in range(3):
        piece = rows.astype(BF)
        sent_ref[320 + 2 * k : 322 + 2 * k, :] = piece
        rows = rows - piece.astype(F32)
    sent_ref[326:336, :] = jnp.zeros((10, 640), BF)


def projection_grad_kernel(flags, ring_ref, pair_ref, rows, out_ref, rows_ref, sent_ref, a_vm, g_vm, sems):
    ins = [
        pltpu.make_async_copy(ring_ref.at[0], a_vm, sems.at[0]),
        pltpu.make_async_copy(pair_ref.at[1], g_vm, sems.at[1]),
    ]
    start_all(ins)
    wait_all(ins)
    side = matmul_at(a_vm[:, 0:384], g_vm[...])[0:320, :]
    out_ref[...] = side
    rows_ref[...] = rows[...]
    send_sides(side, rows[...], sent_ref)


SIDES = (jax.ShapeDtypeStruct((320, 640), F32), PAIR, jax.ShapeDtypeStruct((336, 640), BF))


def projection_grad(flags, ring, pair, rows):
    return kernel_call(
        projection_grad_kernel,
        SIDES,
        [SCALARS, FREE, FREE, INSIDE],
        (INSIDE, INSIDE, INSIDE),
        [pltpu.VMEM((512, 640), BF), pltpu.VMEM((512, 640), BF), pltpu.SemaphoreType.DMA((2,))],
        flops=200_000_000,
        mib=8,
    )(flags, ring, pair, rows)


def add_sides_kernel(side, rows, got, out_ref, rows_ref, sent_ref):
    side = side[...] + got[0:320, :].astype(F32)
    rows = rows[...]
    for k in range(3):
        rows = rows + got[320 + 2 * k : 322 + 2 * k, :].astype(F32)
    out_ref[...] = side
    rows_ref[...] = rows
    send_sides(side, rows, sent_ref)


def add_sides(side, rows, got):
    return kernel_call(
        add_sides_kernel, SIDES, [INSIDE, INSIDE, INSIDE], (INSIDE, INSIDE, INSIDE), [], mib=8
    )(side, rows, got)


def ring_value_kernel(g, sums, out_ref):
    out_ref[0:512, :] = g[...]
    rows = sums[...]
    pieces = []
    for _ in range(3):
        pieces.append(rows.astype(BF).astype(F32))
        rows = rows - pieces[-1]
    out_ref[512:528, :] = jnp.concatenate([*pieces, jnp.zeros((10, 640), F32)], axis=0).astype(BF)


def ring_value(g, sums):
    return kernel_call(
        ring_value_kernel, jax.ShapeDtypeStruct((528, 640), BF), [INSIDE, INSIDE], INSIDE, [], mib=8
    )(g, sums)


def add_rows_kernel(first, *refs):
    blocks, out_ref, rows, sems = refs[:8], refs[8], refs[9], refs[10]
    copies = [
        pltpu.make_async_copy(blocks[b].at[pl.ds(first, 16)], rows.at[b], sems.at[b]) for b in range(8)
    ]
    start_all(copies)
    wait_all(copies)
    total = rows[0].astype(F32)
    for b in range(1, 8):
        total = total + rows[b].astype(F32)
    out_ref[...] = total[0:2, :] + total[2:4, :] + total[4:6, :]


def add_rows(blocks, first):
    return kernel_call(
        lambda *refs: add_rows_kernel(first, *refs),
        PAIR,
        [FREE] * 8,
        INSIDE,
        [pltpu.VMEM((8, 16, 640), BF), pltpu.SemaphoreType.DMA((8,))],
        mib=8,
    )(*blocks)


def kernel_grads_kernel(blocks, fresh, last, *refs):
    acts, gs = refs[:blocks], refs[blocks : 2 * blocks]
    refs = refs[2 * blocks :]
    gs = [one.at[pl.ds(512 if one.shape[0] == 1040 else 0, 512)] for one in gs]
    acts = [one.at[pl.ds(0, 512)] for one in acts]
    if not fresh:
        kept, refs = refs[0], refs[1:]
    sums, a_vm, g_vm, g3, sems = refs[0], *refs[-4:]
    if last:
        out_ref, out_sems = refs[0], refs[1]
        sums = kept
    ins = []
    for b in range(blocks):
        ins.append(pltpu.make_async_copy(gs[b], g_vm.at[b], sems.at[b, 0]))
        ins.append(pltpu.make_async_copy(acts[b], a_vm.at[b], sems.at[b, 1]))
    start_all(ins)

    @pl.loop(0, blocks)
    def _(b):
        clear_edges(g3.at[b])

    @pl.loop(0, blocks)
    def _(b):
        pltpu.make_async_copy(gs[0], g_vm.at[b], sems.at[b, 0]).wait()

        @pl.loop(0, 5)
        def _(k):
            place(g3.at[b], k, g_vm[b, :, lane(k)].astype(F32), 1280, 0)

    wait_all(ins[1::2])

    def outs(p):
        rows = pl.ds(pl.multiple_of(640 * p, 640), 640)
        return [
            pltpu.make_async_copy(
                sums.at[rows, pl.ds(640 * q, 640)],
                out_ref.at[pl.ds(pl.multiple_of(640 * (3 * p + q), 640), 640)],
                out_sems.at[p, q],
            )
            for q in range(3)
        ]

    @pl.loop(0, 3)
    def _(p):
        rows = pl.ds(pl.multiple_of(640 * p, 640), 640)
        here = pl.ds(pl.multiple_of(64 * (2 - p), 64), 512)
        if fresh:
            sums[rows, :] = jnp.zeros((640, 1920), F32)
        elif not last:
            sums[rows, :] = kept[rows, :]

        @pl.loop(0, blocks)
        def _(b):
            sums[rows, :] += matmul_at(a_vm[b], g3[b, here, :])

        if last:
            start_all(outs(p))

    if last:
        for p in range(3):
            wait_all(outs(p))


def kernel_grads_first_kernel(blocks, fresh, last, *refs):
    acts, gs = refs[:blocks], refs[blocks : 2 * blocks]
    refs = refs[2 * blocks :]
    if last:
        side, refs = refs[0], refs[1:]
    if not fresh:
        kept, refs = refs[0], refs[1:]
    sums, a_vm, g_vm, g2, sems = refs[0], *refs[-4:]
    extra = []
    if last:
        out_ref, zeros, out_sems, extra_sems = refs[:4]
        sums = kept
    ins = []
    for b in range(blocks):
        ins.append(pltpu.make_async_copy(gs[b].at[pl.ds(0, 512)], g_vm.at[b], sems.at[b, 0]))
        ins.append(pltpu.make_async_copy(acts[b], a_vm.at[b], sems.at[b, 1]))
    start_all(ins)
    if last:
        zeros[...] = jnp.zeros((320, 640), F32)
        extra.append(pltpu.make_async_copy(side, out_ref.at[pl.ds(2880, 320)], extra_sems.at[0]))
        for k in range(8):
            extra.append(pltpu.make_async_copy(zeros, out_ref.at[pl.ds(3200 + 320 * k, 320)], extra_sems.at[1 + k]))
        start_all(extra)
    @pl.loop(0, blocks)
    def _(b):
        g2[b, 512:576, :] = jnp.zeros((64, 1280), BF)
        pltpu.make_async_copy(gs[0].at[pl.ds(0, 512)], g_vm.at[b], sems.at[b, 0]).wait()

        @pl.loop(0, 5)
        def _(k):
            g = g_vm[b, :, lane(k)].astype(F32)
            g2[b, 0:512, lane(k)] = g.astype(BF)
            g2[b, 0:512, lane(k, 640)] = from_right(g).astype(BF)

    wait_all(ins[1::2])

    def outs(p):
        low = pl.multiple_of(640 * p, 640)
        return [
            pltpu.make_async_copy(
                sums.at[pl.ds(low, 640), pl.ds(0, 640)],
                out_ref.at[pl.ds(pl.multiple_of(960 * p + 320, 320), 640)],
                out_sems.at[p, 0],
            ),
            pltpu.make_async_copy(
                sums.at[pl.ds(low, 320), pl.ds(640, 640)],
                out_ref.at[pl.ds(pl.multiple_of(960 * p, 320), 320)],
                out_sems.at[p, 1],
            ),
        ]

    @pl.loop(0, 3)
    def _(p):
        here = pl.ds(pl.multiple_of(jnp.where(p == 0, 64, 0), 64), 512)
        low = pl.multiple_of(640 * p, 640)
        odd = jnp.where(p == 1, 0, 1)
        if fresh:
            sums[pl.ds(low, 640), :] = jnp.zeros((640, 1280), F32)
        elif not last:
            sums[pl.ds(low, 640), :] = kept[pl.ds(low, 640), :]

        @pl.loop(0, blocks)
        def _(b):
            sums[pl.ds(low, 640), 0:640] += matmul_at(a_vm[b, odd], g2[b, here, 0:640])
            left = matmul_at(a_vm[b, odd, :, 256:640], g2[b, here, 640:1280])
            sums[pl.ds(low, 320), 640:1280] += left[64:384, :]

        if last:
            start_all(outs(p))

    if last:
        for p in range(3):
            wait_all(outs(p))
    wait_all(extra)


def kernel_grads(acts, gs, kept=None, last=False, first=False, side=None):
    blocks = len(acts)
    fresh = kept is None
    scratch = []
    if last and first:
        scratch += [pltpu.VMEM((320, 640), F32)]
    if last:
        scratch += [pltpu.SemaphoreType.DMA((3, 3))]
    if last and first:
        scratch += [pltpu.SemaphoreType.DMA((9,))]
    scratch += [
        pltpu.VMEM((blocks, 2, 512, 640) if first else (blocks, 512, 640), BF),
        pltpu.VMEM((blocks, 512, 640), BF),
        pltpu.VMEM((blocks, 576, 1280) if first else (blocks, 640, 1920), BF),
        pltpu.SemaphoreType.DMA((blocks, 2)),
    ]
    extra = [side] if last and first else []
    count = 2 * blocks + len(extra)
    kernel = kernel_grads_first_kernel if first else kernel_grads_kernel
    sums = jax.ShapeDtypeStruct((1920, 1280 if first else 1920), F32)
    return kernel_call(
        lambda *refs: kernel(blocks, fresh, last, *refs),
        jax.ShapeDtypeStruct((5760, 640), F32) if last else sums,
        [FREE] * count + ([] if fresh else [KEPT]),
        ANY if last else KEPT,
        scratch,
        aliases={} if fresh or last else {count: 0},
        flops=4_000_000_000 * blocks,
        mib=20,
    )(*acts, *gs, *extra, *([] if fresh else [kept]))


def empty(shapes):
    return pl.pallas_call(
        lambda *refs: None,
        out_shape=tuple(shapes),
        out_specs=tuple(ANY for _ in shapes),
    )()


BOTH = ("dp", "section")
RING = (0, 2, 4, 6, 7, 5, 3, 1)


def move(value, triples):
    count = lax.axis_size("section")
    return lax.ppermute(value, BOTH, [(d * count + s, e * count + t) for (d, s), (e, t) in triples])


def hop(value, source, target):
    return move(value, [((d, source), (d, target)) for d in range(MICRO)])


class Ring:
    def __init__(self, value, sections):
        self.up = [((RING[k], s), (RING[(k + 1) % 8], s)) for k in range(8) for s in sections]
        self.down = [(b, a) for a, b in self.up]
        self.blocks = [value]

    def step(self, last_down=False):
        count = len(self.blocks)
        high = self.blocks[max(0, count - 2)]
        low = self.blocks[count - 1]
        if count < 7 or not last_down:
            self.blocks.append(move(high, self.up))
        if count < 7 or last_down:
            self.blocks.append(move(low, self.down))


def dp_total(value, sections):
    for k in (1, 2, 4):
        value = value + move(value, [((d, s), (d ^ k, s)) for d in range(MICRO) for s in sections])
    return value


def after(value, *others):
    return lax.optimization_barrier((value, *others))[0]


def pick(images, image_count, index):
    image = lax.dynamic_index_in_dim(images, index, 0)
    return jnp.where(index < image_count, image, INF).reshape(1, 8, 2, 8, 640)


def exchange_images(images, image_count, row, section, offsets):
    return [
        move(pick(images, image_count, row ^ k), [((d, section), (d ^ k, section)) for d in range(MICRO)])
        for k in offsets
    ]


SLOTS = jax.ShapeDtypeStruct((8, 8, 8, 640), BF)
PARTS = jax.ShapeDtypeStruct((4, 8, 2, 2, 8, 640), BF)


SLOTS = jax.ShapeDtypeStruct((8, 8, 8, 640), BF)
PARTS = jax.ShapeDtypeStruct((8, 4, 2, 2, 8, 640), BF)


def by_micro_batch(images, image_counts, conv_weight, bn_gain, bn_bias, out_grad):
    section = lax.axis_index("section")
    row = lax.axis_index("dp")
    weight = conv_weight[0]
    norm = (bn_gain, bn_bias)
    plain, adds = jnp.array([1, 0], jnp.int32), jnp.array([1, 1], jnp.int32)

    def segment(shapes, *branches):
        def whole(branch):
            def run():
                found = branch()
                missing = [name for name in shapes if name not in found]
                if missing:
                    found.update(zip(missing, empty([shapes[name] for name in missing])))
                return [found[name] for name in shapes]

            return run

        return dict(zip(shapes, lax.switch(section, [whole(branch) for branch in branches])))

    def on_section(first, second, third, fourth):
        return jnp.where(
            section == 0, first, jnp.where(section == 1, second, jnp.where(section == 2, third, fourth))
        )

    def nothing():
        return {}

    def named(prefix, blocks):
        return {f"{prefix}{k}": one for k, one in enumerate(blocks)}

    def listed(found, prefix, count):
        return [found[f"{prefix}{k}"] for k in range(count)]

    def many(prefix, count, shape):
        return {f"{prefix}{k}": shape for k in range(count)}

    def exchange(value):
        return lax.all_to_all(value, "dp", 0, 0, tiled=True)

    def resume(value, blocks, index):
        ring = Ring(value, (index,))
        ring.blocks += blocks
        return ring

    def shown(value):
        return jnp.where(value < INF, value, 0.0).reshape(8, 8, 8, 640).transpose(1, 0, 2, 3)

    count = image_counts[0]
    piece = jax.ShapeDtypeStruct((1, 8, 2, 8, 640), BF)
    grad_shape = jax.ShapeDtypeStruct((512, 640), F32)

    def zero_0():
        got = exchange_images(images, count, row, 0, (4, 3, 2, 1))
        return {"p0": pick(images, count, row), "p1": got[3], "p2": got[2], "p3": got[1], "p4": got[0]}

    def zero_1():
        return {"others": jnp.concatenate(exchange_images(images, count, row, 1, (5, 6, 7)), axis=0)}

    def zero_2():
        return {"top": exchange(out_grad)}

    def zero_3():
        grad, own = backward_top(plain, exchange(out_grad), weight)
        return {"grad": grad, "own": own}

    zeroth = segment(
        {
            **{f"p{k}": piece for k in range(5)}, "others": jax.ShapeDtypeStruct((3, 8, 2, 8, 640), BF),
            "top": SLOTS, "grad": grad_shape, "own": FIELD,
        },
        zero_0, zero_1, zero_2, zero_3,
    )
    others = hop(zeroth["others"], 1, 0)

    def one_0():
        pieces = (*[zeroth[f"p{k}"] for k in range(5)], others)
        pair, ring, fields, stats = forward_first(
            jnp.stack([jnp.int32(1), row.astype(jnp.int32)]), pieces, weight, *norm
        )
        return {"pair": pair, "ring": ring, "fields": fields, "stats": stats}

    def turn_weight(weight):
        return weight.reshape(9, 640, 640).transpose(0, 2, 1).reshape(5760, 640)

    def turned():
        return {"weight": turn_weight(weight)}

    first = segment(
        {"weight": jax.ShapeDtypeStruct((5760, 640), BF), "pair": TWO, "ring": TWO, "fields": TWO, "stats": PAIR},
        one_0, nothing, turned, nothing,
    )
    h1_in = hop(first["pair"], 0, 1)

    def two_1():
        y1, stats, act = forward_rest(adds, h1_in, h1_in, weight, *norm)
        return {"y1": y1, "stats": stats, "act": act}

    second = segment(
        {"y1": FIELD, "act": FIELD, "stats": PAIR}, nothing, two_1, nothing, nothing
    )
    y1_in = hop(second["y1"], 1, 2)

    def turned_1():
        return {"weight": turn_weight(after(weight, second["y1"]))}

    wait_2 = segment({"weight": jax.ShapeDtypeStruct((5760, 640), BF)}, nothing, turned_1, nothing, nothing)
    y1_in = after(y1_in, wait_2["weight"])

    def three_2():
        pair, stats, act = forward_rest(plain, y1_in, y1_in, weight, *norm, handed=True)
        return {"pair": pair, "stats": stats, "act": act}

    third = segment({"pair": TWO, "act": FIELD, "stats": PAIR}, nothing, nothing, three_2, nothing)
    h3_in = hop(third["pair"], 2, 3)

    def four_3():
        g_h3, sums, act = turn(plain, h3_in, zeroth["grad"], *norm)
        return {"g": g_h3, "sums": sums, "act": act}

    fourth = segment({"g": FIELD, "act": FIELD, "sums": PAIR}, nothing, nothing, nothing, four_3)
    g_h3_in = hop(fourth["g"], 3, 2)

    def five_2():
        g_y1, sums = backward_rest(adds, g_h3_in, zeroth["top"], y1_in, third["stats"], first["weight"], *norm)
        return {"g": g_y1, "sums": sums}

    fifth = segment({"g": FIELD, "sums": PAIR}, nothing, nothing, five_2, nothing)
    g_y1_in = hop(fifth["g"], 2, 1)

    def one_step(value, index, beside):
        value = after(value, fifth["g"])
        ring = Ring(value, (index,))
        ring.step()
        ring.step()
        return {"out": beside(value), **named("u", ring.blocks)}

    wait_5 = segment(
        {"out": SLOTS, **many("u", 5, FIELD)},
        lambda: {"out": shown(after(first["pair"], fifth["g"])[0])},
        lambda: one_step(second["act"], 1, lambda _: shown(second["y1"])),
        lambda: one_step(third["act"], 2, lambda _: shown(third["pair"][0])),
        lambda: one_step(fourth["act"], 3, lambda act: shown(forward_last(plain, act, h3_in, weight))),
    )
    g_y1_in = after(g_y1_in, wait_5["u0"])

    def six_0():
        ring = Ring(first["ring"], (0,))
        ring.step()
        ring.step()
        return named("a", ring.blocks)

    def six_1():
        pair, sums = backward_rest(
            plain, g_y1_in, zeroth["top"], h1_in, second["stats"], wait_2["weight"], *norm, handed=True
        )
        return {"pair": pair, "sums": sums}

    sixth = segment(
        {"pair": TWO, "sums": PAIR, **many("a", 5, TWO)}, six_0, six_1, nothing, nothing
    )
    pair_sent = hop(sixth["pair"], 1, 0)

    def seven_0():
        ring = Ring(after(sixth["a0"], sixth["pair"]), (0,))
        ring.blocks = listed(sixth, "a", 5)
        ring.blocks[3] = after(ring.blocks[3], sixth["pair"])
        ring.step()
        return named("a", ring.blocks[5:])

    def seven_1():
        return {"g": ring_value(after(g_y1_in, sixth["pair"]), sixth["sums"])}

    def seven_2():
        return {"g": ring_value(g_h3_in, fifth["sums"])}

    def seven_3():
        return {"g": ring_value(zeroth["own"], fourth["sums"])}

    tall = jax.ShapeDtypeStruct((528, 640), BF)
    seventh = segment({"g": tall, **many("a", 2, TWO)}, seven_0, seven_1, seven_2, seven_3)

    pair_in = after(pair_sent, seventh["g"])

    def work(ring, late):
        gs, acts = ring.blocks, late.blocks
        total = None
        for low, high in ((0, 3), (3, 5), (5, 7)):
            ring.step()
            if low > 0:
                late.step(True)
            total = kernel_grads(acts[low:high], gs[low:high], total)
            if low < 5:
                gs[high : high + 2], acts[high:], total = lax.optimization_barrier(
                    (gs[high : high + 2], acts[high:], total)
                )
        return kernel_grads(acts[7:8], gs[7:8], total, True)

    def eight_0():
        fence = lax.optimization_barrier
        ring = Ring(pair_in[0], (0,))
        ring.step()
        field = backward_first_conv(plain, pair_in, weight)
        parts, sums = backward_first_norm(plain, field, first["fields"], first["stats"], *norm)
        gs = ring.blocks
        sums, gs[1:3] = fence((sums, gs[1:3]))
        side, rows, sent = projection_grad(plain, first["ring"], pair_in, sums)

        def to(k):
            return move(sent, [((d, 0), (d ^ k, 0)) for d in range(MICRO)])

        got = to(1)
        parts = exchange(parts)
        late = Ring(sixth["a0"], (0,))
        late.blocks = acts = listed(sixth, "a", 5) + listed(seventh, "a", 2)
        ring.step()
        side, rows, sent = add_sides(side, rows, got)
        got = to(2)
        acts[0] = after(acts[0], side)
        total = kernel_grads(acts[0:3], gs[0:3], first=True)
        gs[3:5], acts[3:], total = fence((gs[3:5], acts[3:], total))
        ring.step()
        late.step(True)
        total = kernel_grads(acts[3:5], gs[3:5], total, first=True)
        gs[5:7], got, total = fence((gs[5:7], got, total))
        ring.step()
        side, rows, sent = add_sides(side, rows, got)
        got = to(4)
        acts[5] = after(acts[5], side)
        total = kernel_grads(acts[5:7], gs[5:7], total, first=True)
        got, total = fence((got, total))
        side, rows, _ = add_sides(side, rows, got)
        total = kernel_grads(acts[7:8], gs[7:8], total, True, True, side)
        parts, total = fence((parts, total))
        return [parts, total, rows]

    def eight_rest():
        gs = Ring(seventh["g"], (1, 2, 3))
        gs.step()
        acts = Ring(wait_5["u0"], (1, 2, 3))
        acts.blocks = listed(wait_5, "u", 5)
        total = work(gs, acts)
        return [*empty([PARTS]), total, add_rows(gs.blocks, 512)]

    parts, grads, sums = lax.cond(section > 0, eight_rest, eight_0)

    mine = parts[:, 0]
    for k in range(1, 4):
        mine = jnp.where(section == k, hop(parts[:, k], 0, k), mine)
    out = exchange(after(wait_5["out"], sums))
    return (out[None], mine.reshape(8, 4, 16, 320), grads[None], sums[1:2], sums[0:1])


def solution(mesh):
    one_each = mesh.shape["dp"] == MICRO and mesh.shape["section"] == 4

    def on_device(images, *rest):
        if one_each and images.shape == (MICRO, 16, 16, 320):
            return by_micro_batch(images, *rest)
        return pipelined(images, *rest)

    return jax.shard_map(
        on_device,
        mesh=mesh,
        in_specs=(
            P("dp", None, None, None),
            P("dp"),
            P("section", None, None),
            P("section", None),
            P("section", None),
            P("dp", None, None, None),
        ),
        out_specs=(
            P("section", "dp", None, None, None),
            P("dp", "section", None, None),
            P("section", None, None),
            P("section", None),
            P("section", None),
        ),
        check_vma=False,
    )
```
